128 devices in a mesh: dp: 2 (over core), vocab: 16 (over y, z), mp: 4 (over x).
Axes of the slice: x: 4, y: 4, z: 4, core: 2. Of those that a mesh axis runs over, the one named last changes fastest.
Arguments:
- grad_parts: bfloat16 [2, 16384, 16384], P('dp', 'vocab', 'mp'), may hold values from -150 to 150
- old_basis: float32 [64, 16384], P(None, 'mp'), may hold values from -0.046875 to 0.046875
- first_moment: float32 [64, 16384], P(None, 'mp'), may hold values from -3 to 3
- second_moment: float32 [64, 16384], P(None, 'mp'), may hold values from 0.5 to 4
Outputs:
- update: bfloat16 [16384, 16384], P('vocab', 'mp')
- new_basis: float32 [64, 16384], P(None, 'mp')
- new_first: float32 [64, 16384], P(None, 'mp')
- new_second: float32 [64, 16384], P(None, 'mp')
The draws below stay inside these ranges and needn't reach their ends.
All inputs are finite; a program needn't handle non-finite values.
Results may differ from the reference program's by a relative error of at most 0.035.
Values may be sent and summed in bfloat16 or wider, within the bound.
No kernel may reach another device: no remote copies, remote signals or barrier semaphores. Data moves between devices by JAX's collectives and lax.ppermute only.
A program may use at most 128 MiB of HBM per device.

```python
import math
import jax
import jax.numpy as jnp
from jax import lax

D = 16384
RANK = 64
ITERS = 2
VOCAB = 16384
REPLICAS = 2


def draw_grad_parts(key, part):
    key = jax.random.fold_in(key, 1)
    key_rows, key_cols, key_noise = jax.random.split(key, 3)
    row_scale = jnp.exp(jax.random.uniform(key_rows, (1, VOCAB, 1), jnp.float32) * math.log(10.0))
    col_scale = jnp.exp(jax.random.uniform(key_cols, (1, 1, D), jnp.float32) * math.log(10.0))
    values = jnp.clip(jax.random.normal(key_noise, (REPLICAS, VOCAB, D), jnp.float32), -6.0, 6.0)
    return (values * row_scale * col_scale * 0.25).astype(jnp.bfloat16)


def levels(rng, dims, pieces, low, high):
    def one(axis_at, blocks):
        draws = jax.random.uniform(jax.random.fold_in(jax.random.fold_in(rng, 6), axis_at), (blocks,), jnp.float32, low / len(pieces), high / len(pieces))
        return jnp.repeat(jnp.exp(draws), dims[axis_at] // blocks).reshape((-1,) + (1,) * (len(dims) - axis_at - 1))

    loudness = one(*pieces[0])
    for cut in pieces[1:]:
        loudness = loudness * one(*cut)
    return loudness


def scatter_about(rng, dims, scale, limit, cuts=(), dtype=jnp.bfloat16):
    array = scale * jax.random.normal(rng, dims, jnp.float32)
    if cuts:
        array = array * levels(rng, dims, cuts, -0.22, 0.18)
    return jnp.clip(array, -limit, limit).astype(dtype)


def setup_inputs(seed: int = 0) -> dict:
    streams_of = jax.random.split(jax.random.key(seed), 5)
    return {
        "grad_parts": draw_grad_parts(jax.random.fold_in(streams_of[4], 71), 0),
        "old_basis": scatter_about(streams_of[1], (RANK, D), D ** -0.5, 0.046875, ((1, 4),), jnp.float32),
        "first_moment": scatter_about(streams_of[2], (RANK, D), 0.5, 3.0, ((1, 4),), jnp.float32),
        "second_moment": jnp.clip(jnp.exp(math.log(4.0) - 2.0794415 * jax.random.uniform(streams_of[3], (RANK, D), jnp.float32) ** levels(streams_of[3], (RANK, D), ((1, 4),), -0.2, 0.2)), 0.5, 4.0),
    }


def orthonormal(block):
    gram = jnp.dot(block, block.T, precision=lax.Precision.HIGHEST)
    factor = jnp.linalg.cholesky(gram)
    return jax.scipy.linalg.solve_triangular(factor, block, lower=True)

def reference(grad_parts, old_basis, first_moment, second_moment):
    grad = grad_parts[0].astype(jnp.float32)
    for replica in range(1, REPLICAS):
        grad = grad + grad_parts[replica].astype(jnp.float32)
    basis = old_basis
    for step in range(ITERS):
        basis_half = basis.astype(jnp.bfloat16)
        rows = jnp.dot(basis_half.astype(jnp.float32), grad.T, precision=lax.Precision.HIGHEST)
        left_half = orthonormal(rows).astype(jnp.bfloat16)
        columns = jnp.dot(left_half.astype(jnp.float32), grad, precision=lax.Precision.HIGHEST)
        basis = orthonormal(columns)
    new_first = 0.9 * first_moment + 0.1 * columns
    new_second = 0.999 * second_moment + 0.001 * columns * columns
    corr_one = 1.0 - 0.9 ** 10
    corr_two = 1.0 - 0.999 ** 10
    direction = new_first / corr_one / (jnp.sqrt(new_second / corr_two) + 1e-08)
    direction_half = direction.astype(jnp.bfloat16)
    update = jnp.dot(left_half.T.astype(jnp.float32), direction_half.astype(jnp.float32), preferred_element_type=jnp.float32)
    update = (update * jnp.sqrt(jnp.float32(VOCAB))).astype(jnp.bfloat16)
    return (update, basis, new_first, new_second)
```

```python
import functools
import math

import jax
import jax.numpy as jnp
from jax import lax
from jax.experimental import pallas as pl
from jax.experimental.pallas import tpu as pltpu
from jax.sharding import PartitionSpec as P

F32 = jnp.float32
BF16 = jnp.bfloat16
LANE = 128
EXTRA = 16
TILE = 512
WIDE = 256
VMEM_LIMIT = 28 * 1024 * 1024

VMEM = pl.BlockSpec(memory_space=pltpu.VMEM)
SMEM = pl.BlockSpec(memory_space=pltpu.SMEM)


def thirds(value):
    high = value.astype(BF16).astype(F32)
    rest = value - high
    mid = rest.astype(BF16).astype(F32)
    return high, mid, rest - mid


def stacked(value):
    return jnp.concatenate(thirds(value), axis=0).astype(BF16)


def dot(a, b, ca, cb):
    return lax.dot_general(a, b, (((ca,), (cb,)), ((), ())), preferred_element_type=F32)


def inverse_factor(gram):
    rank = gram.shape[0]
    lanes = lax.broadcasted_iota(jnp.int32, (8, rank), 1)
    subs = lax.broadcasted_iota(jnp.int32, (8, LANE), 0)
    blocks = rank // 8
    both = []
    for b in range(blocks):
        eye = jnp.where(lanes == subs[:, :rank] + 8 * b, 1.0, 0.0).astype(F32)
        both.append(jnp.concatenate([gram[8 * b : 8 * b + 8, :], eye], axis=1))
    scale = []
    for b in range(blocks):
        diag = jnp.ones((8, LANE), F32)
        cols = {
            (j, i): jnp.broadcast_to(both[i][:, 8 * b + j : 8 * b + j + 1], (8, LANE))
            for j in range(8)
            for i in range(b, blocks)
        }
        for j in range(8):
            pivot = cols[j, b][j : j + 1, :]
            inverse = 1.0 / pivot
            diag = jnp.where(subs == j, pivot, diag)
            row = both[b][j : j + 1, :] * inverse
            heads = {m: cols[m, b][j : j + 1, :] * inverse for m in range(j + 1, 8)}
            for i in range(b, blocks):
                f = cols[j, i]
                if i == b:
                    f = jnp.where(subs > j, f, 0.0)
                both[i] = both[i] - f * row
                for m in range(j + 1, 8):
                    cols[m, i] = cols[m, i] - f * heads[m]
        scale.append(lax.rsqrt(diag))
    return jnp.concatenate(
        [both[b][:, rank:] * scale[b][:, :rank] for b in range(blocks)], axis=0
    )


def applied(factor3, block):
    rank = factor3.shape[0] // 3
    r = dot(factor3, block, 1, 0)
    return r[:rank] + r[rank : 2 * rank] + r[2 * rank :]


def gathered_gram(chunks_ref, rank):
    n = chunks_ref.shape[0]
    each = rank // n
    parts = []
    for c in range(n):
        e = chunks_ref[c, rank : rank + EXTRA, :].astype(F32)
        parts.append(e[:each] + e[each : 2 * each] + e[2 * each : 3 * each])
    return jnp.concatenate(parts, axis=0)[:, :rank]


def extra_rows(piece):
    pad = jnp.zeros((EXTRA - 3 * piece.shape[0], piece.shape[1]), F32)
    return jnp.concatenate([*thirds(piece), pad], axis=0).astype(BF16)


def split_products(me, left, slab_ref, theirs_ref, mine_ref):
    half = slab_ref.shape[0] // 2
    for base, out in (((1 - me) * half, theirs_ref), (me * half, mine_ref)):
        for t in range(0, half, WIDE):
            rows = pl.ds(pl.multiple_of(base + t, WIDE), WIDE)
            out[:, t : t + WIDE] = dot(left, slab_ref[rows, :], 1, 1).astype(out.dtype)


def first_rows_kernel(me_ref, basis_ref, slab_ref, theirs_ref, mine_ref):
    split_products(me_ref[0], basis_ref[...].astype(BF16), slab_ref, theirs_ref, mine_ref)


def next_rows_kernel(me_ref, chunks_ref, slab_ref, theirs_ref, mine_ref, pack_ref, half_ref):
    me = me_ref[0]
    rank = half_ref.shape[0]
    factor3 = stacked(inverse_factor(gathered_gram(chunks_ref, rank)))
    per = TILE // LANE
    total = jnp.zeros((3 * rank, 3 * rank), F32)
    for j in range(chunks_ref.shape[0] // per):
        block = jnp.concatenate([chunks_ref[j * per + q, :rank, :] for q in range(per)], axis=1)
        columns = applied(factor3, block)
        half_ref[:, j * TILE : (j + 1) * TILE] = columns.astype(BF16)
        three = stacked(columns)
        total = total + dot(three, three, 1, 1)
    gram = folded(total, rank)
    own = jnp.where(me == 0, gram[: rank // 2], gram[rank // 2 :])
    quarter = rank // 4
    own = jnp.concatenate([own[:quarter], own[quarter:]], axis=1)
    pad = jnp.zeros((EXTRA, pack_ref.shape[1] - 3 * LANE), F32)
    pack_ref[...] = jnp.concatenate([*thirds(own), pad], axis=1).astype(BF16)
    split_products(me, half_ref[...], slab_ref, theirs_ref, mine_ref)


def folded(total, rank):
    wide = total[:rank] + total[rank : 2 * rank] + total[2 * rank :]
    return wide[:, :rank] + wide[:, rank : 2 * rank] + wide[:, 2 * rank :]


def packed_half(ref, rank):
    e = ref[rank:, :].astype(F32)
    g = e[:, :LANE] + e[:, LANE : 2 * LANE] + e[:, 2 * LANE : 3 * LANE]
    return jnp.concatenate([g[:, :rank], g[:, rank:]], axis=0)


def columns_kernel(orthogonal, me_ref, mine_ref, other_ref, slab_ref, chunks_ref, rows_ref, gram_ref):
    me = me_ref[0]
    rank = rows_ref.shape[0]
    half = mine_ref.shape[1]
    mine, other = mine_ref[:rank, :], other_ref[:rank, :]
    if orthogonal:
        a, b = packed_half(mine_ref, rank), packed_half(other_ref, rank)
        first = me == 0
        gram = jnp.concatenate([jnp.where(first, a, b), jnp.where(first, b, a)], axis=0)
        factor3 = stacked(inverse_factor(gram))
        mine = applied(factor3, mine).astype(BF16)
        other = applied(factor3, other).astype(BF16)
    rows_ref[:, pl.ds(pl.multiple_of(me * half, half), half)] = mine
    rows_ref[:, pl.ds(pl.multiple_of((1 - me) * half, half), half)] = other
    gram_ref[...] = jnp.zeros_like(gram_ref)
    gram_ref[:, :rank] = dot(mine, mine, 1, 1)
    n = chunks_ref.shape[0]
    each = rank // n
    rows = rows_ref[...]
    per = TILE // LANE
    for j in range(n // per):
        product = dot(rows, slab_ref[:, j * TILE : (j + 1) * TILE], 1, 0).astype(BF16)
        for q in range(per):
            c = j * per + q
            chunks_ref[c, :rank, :] = product[:, q * LANE : (q + 1) * LANE]
            chunks_ref[c, rank:, :] = extra_rows(gram_ref[c * each : (c + 1) * each, :])


def sum_chunks_kernel(parts_ref, out_ref):
    n = parts_ref.shape[0]
    rank = parts_ref.shape[1] - EXTRA
    each = rank // n
    total = parts_ref[0].astype(F32)
    for c in range(1, n):
        total = total + parts_ref[c].astype(F32)
    e = total[rank:]
    gram = e[:each] + e[each : 2 * each] + e[2 * each : 3 * each]
    piece = jnp.concatenate([total[:rank].astype(BF16), extra_rows(gram)], axis=0)
    for c in range(n):
        out_ref[c] = piece


def sum_packed_kernel(a_ref, b_ref, c_ref, d_ref, out_ref):
    total = (a_ref[...].astype(F32) + b_ref[...].astype(F32)) + (
        c_ref[...].astype(F32) + d_ref[...].astype(F32)
    )
    rank = out_ref.shape[0] - EXTRA
    out_ref[:rank, :] = total[:rank].astype(BF16)
    e = total[rank:]
    g = e[:, :LANE] + e[:, LANE : 2 * LANE] + e[:, 2 * LANE : 3 * LANE]
    pad = jnp.zeros((EXTRA, out_ref.shape[1] - 3 * LANE), F32)
    out_ref[rank:, :] = jnp.concatenate([*thirds(g), pad], axis=1).astype(BF16)


def moments_kernel(
    chunks_ref, rows_ref, first_ref, second_ref,
    columns_ref, gram_ref, new_first_ref, new_second_ref, direction_ref, left_ref,
):
    rank = rows_ref.shape[0]
    factor3 = stacked(inverse_factor(gathered_gram(chunks_ref, rank)))
    left_ref[...] = applied(factor3, rows_ref[...]).astype(BF16)
    corr_one = 1.0 - 0.9**10
    corr_two = 1.0 - 0.999**10
    per = TILE // LANE
    total = jnp.zeros((3 * rank, 3 * rank), F32)
    for j in range(chunks_ref.shape[0] // per):
        at = slice(j * TILE, (j + 1) * TILE)
        block = jnp.concatenate([chunks_ref[j * per + q, :rank, :] for q in range(per)], axis=1)
        columns = applied(factor3, block)
        columns_ref[:, at] = columns
        three = stacked(columns)
        total = total + dot(three, three, 1, 1)
        new_first = 0.9 * first_ref[:, at] + 0.1 * columns
        new_second = 0.999 * second_ref[:, at] + 0.001 * columns * columns
        new_first_ref[:, at] = new_first
        new_second_ref[:, at] = new_second
        direction = new_first / corr_one / (jnp.sqrt(new_second / corr_two) + 1e-08)
        direction_ref[:, at] = direction.astype(BF16)
    gram_ref[...] = folded(total, rank)


def update_kernel(scale, left_ref, direction_ref, update_ref):
    left = left_ref[...]
    for t in range(0, direction_ref.shape[1], TILE):
        product = dot(left, direction_ref[:, t : t + TILE], 0, 0)
        update_ref[:, t : t + TILE] = (product * scale).astype(BF16)


def basis_kernel(a_ref, b_ref, c_ref, d_ref, columns_ref, basis_ref):
    factor = inverse_factor((a_ref[...] + b_ref[...]) + (c_ref[...] + d_ref[...]))
    factor3 = stacked(factor)
    for t in range(0, columns_ref.shape[1], TILE):
        high, mid, low = thirds(columns_ref[:, t : t + TILE])
        basis_ref[:, t : t + TILE] = (
            applied(factor3, high.astype(BF16))
            + applied(factor3, mid.astype(BF16))
            + applied(factor3, low.astype(BF16))
        )


def call(kernel, outs, operands, scratch=(), flops=0, moved=0):
    return pl.pallas_call(
        kernel,
        out_shape=[jax.ShapeDtypeStruct(s, t) for s, t in outs],
        in_specs=[SMEM if x.dtype == jnp.int32 else VMEM for x in operands],
        out_specs=[VMEM] * len(outs),
        scratch_shapes=[pltpu.VMEM(s, t) for s, t in scratch],
        compiler_params=pltpu.CompilerParams(vmem_limit_bytes=VMEM_LIMIT),
        cost_estimate=pl.CostEstimate(flops=flops, bytes_accessed=moved, transcendentals=0),
    )(*operands)


def swapped(x):
    return lax.ppermute(x, "dp", [(0, 1), (1, 0)])


def others(x):
    n = lax.axis_size("mp")
    return [lax.ppermute(x, "mp", [(i, (i + k) % n) for i in range(n)]) for k in (1, 3, 2)]


def sum_over_owners(chunks):
    axes = ("dp", "vocab")
    parts = lax.all_to_all(chunks, axes, 0, 0)
    copies = call(sum_chunks_kernel, [(parts.shape, BF16)], [parts])[0]
    return lax.all_to_all(copies, axes, 0, 0)


def local(grad_parts, old_basis, first_moment, second_moment):
    slab = grad_parts[0]
    vocab, width = slab.shape
    rank = old_basis.shape[0]
    half = vocab // 2
    owners = lax.axis_size("dp") * lax.axis_size("vocab")
    me = lax.axis_index("dp").astype(jnp.int32).reshape(1)
    halves = [((rank, half), BF16), ((rank, half), F32)]
    chunks_out = [((owners, rank + EXTRA, LANE), BF16), ((rank, vocab), BF16)]
    gram_scratch = [((rank, LANE), F32)]

    theirs, mine = call(first_rows_kernel, halves, [me, old_basis, slab])
    mine = (mine + swapped(theirs).astype(F32)).astype(BF16)
    total = mine.astype(F32)
    for x in others(mine):
        total = total + x.astype(F32)
    mine = total.astype(BF16)
    chunks, _ = call(
        functools.partial(columns_kernel, False),
        chunks_out,
        [me, mine, swapped(mine), slab],
        gram_scratch,
    )
    chunks = sum_over_owners(chunks)

    theirs, mine, pack = call(
        next_rows_kernel,
        halves + [((EXTRA, half), BF16)],
        [me, chunks, slab],
        [((rank, width), BF16)],
    )
    mine = (mine + swapped(theirs).astype(F32)).astype(BF16)
    mine = jnp.concatenate([mine, pack], axis=0)
    mine = call(sum_packed_kernel, [(mine.shape, BF16)], [mine, *others(mine)])[0]
    chunks, rows = call(
        functools.partial(columns_kernel, True),
        chunks_out,
        [me, mine, swapped(mine), slab],
        gram_scratch,
    )
    chunks = sum_over_owners(chunks)

    wide = ((rank, width), F32)
    columns, gram, new_first, new_second, direction, left = call(
        moments_kernel,
        [wide, ((rank, rank), F32), wide, wide, ((rank, width), BF16), ((rank, vocab), BF16)],
        [chunks, rows, first_moment, second_moment],
    )
    gram_others = others(gram)
    scale = math.sqrt(vocab * lax.axis_size("vocab"))
    update = pl.pallas_call(
        functools.partial(update_kernel, scale),
        out_shape=jax.ShapeDtypeStruct((vocab, width), BF16),
        grid=(vocab // WIDE,),
        in_specs=[
            pl.BlockSpec((rank, WIDE), lambda i: (0, i)),
            pl.BlockSpec((rank, width), lambda i: (0, 0)),
        ],
        out_specs=pl.BlockSpec((WIDE, width), lambda i: (i, 0)),
        compiler_params=pltpu.CompilerParams(vmem_limit_bytes=VMEM_LIMIT),
        cost_estimate=pl.CostEstimate(
            flops=2 * rank * vocab * width, bytes_accessed=2 * vocab * width, transcendentals=0
        ),
    )(left, direction)
    basis = call(basis_kernel, [wide], [gram, *gram_others, columns])[0]
    return (update, basis, new_first, new_second)


def solution(mesh):
    placed = (P("dp", "vocab", "mp"), P(None, "mp"), P(None, "mp"), P(None, "mp"))
    return jax.shard_map(
        local,
        mesh=mesh,
        in_specs=placed,
        out_specs=(P("vocab", "mp"), P(None, "mp"), P(None, "mp"), P(None, "mp")),
        check_vma=False,
    )
```

```python
import functools
import math

import jax
import jax.numpy as jnp
from jax import lax
from jax.experimental import pallas as pl
from jax.experimental.pallas import tpu as pltpu
from jax.sharding import PartitionSpec as P

F32 = jnp.float32
BF16 = jnp.bfloat16
LANE = 128
EXTRA = 16
TILE = 512
WIDE = 256
VMEM_LIMIT = 28 * 1024 * 1024

VMEM = pl.BlockSpec(memory_space=pltpu.VMEM)
SMEM = pl.BlockSpec(memory_space=pltpu.SMEM)


def thirds(value):
    high = value.astype(BF16).astype(F32)
    rest = value - high
    mid = rest.astype(BF16).astype(F32)
    return high, mid, rest - mid


def stacked(value, axis=0):
    return jnp.concatenate(thirds(value), axis=axis).astype(BF16)


def dot(a, b, ca, cb):
    return lax.dot_general(a, b, (((ca,), (cb,)), ((), ())), preferred_element_type=F32)


def inverse_factor(gram):
    rank = gram.shape[0]
    lanes = lax.broadcasted_iota(jnp.int32, (8, rank), 1)
    subs = lax.broadcasted_iota(jnp.int32, (8, LANE), 0)
    blocks = rank // 8
    both = []
    for b in range(blocks):
        eye = jnp.where(lanes == subs[:, :rank] + 8 * b, 1.0, 0.0).astype(F32)
        both.append(jnp.concatenate([gram[8 * b : 8 * b + 8, :], eye], axis=1))
    scale = []
    for b in range(blocks):
        diag = jnp.ones((8, LANE), F32)
        cols = {
            (j, i): jnp.broadcast_to(both[i][:, 8 * b + j : 8 * b + j + 1], (8, LANE))
            for j in range(8)
            for i in range(b, blocks)
        }
        for j in range(8):
            pivot = cols[j, b][j : j + 1, :]
            inverse = 1.0 / pivot
            diag = jnp.where(subs == j, pivot, diag)
            row = both[b][j : j + 1, :] * inverse
            heads = {m: cols[m, b][j : j + 1, :] * inverse for m in range(j + 1, 8)}
            for i in range(b, blocks):
                f = cols[j, i]
                if i == b:
                    f = jnp.where(subs > j, f, 0.0)
                both[i] = both[i] - f * row
                for m in range(j + 1, 8):
                    cols[m, i] = cols[m, i] - f * heads[m]
        scale.append(lax.rsqrt(diag))
    return jnp.concatenate(
        [both[b][:, rank:] * scale[b][:, :rank] for b in range(blocks)], axis=0
    )


def applied(factor3, block):
    return dot(factor3, jnp.concatenate([block] * 3, axis=0), 1, 0)


def folded(total, rank):
    wide = total[:rank] + total[rank : 2 * rank] + total[2 * rank :]
    return wide[:, :rank] + wide[:, rank : 2 * rank] + wide[:, 2 * rank :]


def in_order(me, own, other):
    first = me == 0
    return jnp.concatenate([jnp.where(first, own, other), jnp.where(first, other, own)], axis=0)


def span(base, size):
    return pl.ds(pl.multiple_of(base, size), size)


def extra_rows(piece):
    pad = jnp.zeros((EXTRA - 3 * piece.shape[0], piece.shape[1]), F32)
    return jnp.concatenate([*thirds(piece), pad], axis=0).astype(BF16)


def from_extra(e, each):
    return e[:each] + e[each : 2 * each] + e[2 * each : 3 * each]


def gathered_gram(me, own_ref, other_ref, rank):
    n = own_ref.shape[0]
    each = rank // (2 * n)
    halves = [
        jnp.concatenate(
            [from_extra(ref[c, rank : rank + EXTRA, :].astype(F32), each) for c in range(n)], axis=0
        )
        for ref in (own_ref, other_ref)
    ]
    return in_order(me, *halves)[:, :rank]


def gathered_blocks(me, own_ref, other_ref, rank):
    n = own_ref.shape[0]
    per = TILE // LANE
    for core, ref in ((me, own_ref), (1 - me, other_ref)):
        for j in range(n // per):
            block = jnp.concatenate([ref[j * per + q, :rank, :] for q in range(per)], axis=1)
            yield span(core * (n * LANE) + j * TILE, TILE), block


def packed_gram(own):
    quarter = own.shape[0] // 2
    return stacked(jnp.concatenate([own[:quarter], own[quarter:]], axis=1), 1)


def from_packed(e):
    return e[:, :LANE] + e[:, LANE : 2 * LANE] + e[:, 2 * LANE : 3 * LANE]


def packed_half(ref, rank):
    g = from_packed(ref[rank:, :].astype(F32))
    return jnp.concatenate([g[:, :rank], g[:, rank:]], axis=0)


def split_rows(me, half):
    for t in range(0, 2 * half, WIDE):
        core = 1 - me if t < half else me
        yield t < half, t % half, span(core * half + t % half, WIDE)


def first_rows_kernel(
    me_ref, basis_hbm, slab_hbm, theirs_ref, mine_ref, slab_ref, basis_ref, sems
):
    half = slab_ref.shape[0] // 2
    order = list(split_rows(me_ref[0], half))
    basis_copy = pltpu.make_async_copy(basis_hbm, basis_ref, sems.at[len(order)])
    basis_copy.start()
    copies = [
        pltpu.make_async_copy(slab_hbm.at[rows, :], slab_ref.at[rows, :], sems.at[i])
        for i, (_, _, rows) in enumerate(order)
    ]
    for copy in copies:
        copy.start()
    basis_copy.wait()
    left = basis_ref[...].astype(BF16)
    for copy, (foreign, t, rows) in zip(copies, order):
        copy.wait()
        out = theirs_ref if foreign else mine_ref
        out[:, t : t + WIDE] = dot(left, slab_ref[rows, :], 1, 1).astype(out.dtype)


def next_rows_kernel(
    me_ref, own_ref, other_ref, slab_ref, theirs_ref, mine_ref, pack_ref, half_ref
):
    me = me_ref[0]
    rank = half_ref.shape[0]
    factor3 = stacked(inverse_factor(gathered_gram(me, own_ref, other_ref, rank)), 1)
    total = jnp.zeros((3 * rank, 3 * rank), F32)
    for at, block in gathered_blocks(me, own_ref, other_ref, rank):
        columns = applied(factor3, block)
        half_ref[:, at] = columns.astype(BF16)
        three = stacked(columns)
        total = total + dot(three, three, 1, 1)
    gram = folded(total, rank)
    own = jnp.where(me == 0, gram[: rank // 2], gram[rank // 2 :])
    pack_ref[...] = jnp.zeros_like(pack_ref)
    pack_ref[:, : 3 * LANE] = packed_gram(own)
    left = half_ref[...]
    for foreign, t, rows in split_rows(me, slab_ref.shape[0] // 2):
        out = theirs_ref if foreign else mine_ref
        out[:, t : t + WIDE] = dot(left, slab_ref[rows, :], 1, 1).astype(out.dtype)


def columns_kernel(
    orthogonal, me_ref, mine_ref, other_ref, slab_ref,
    theirs_ref, owned_ref, extra_ref, rows_ref, gram_ref,
):
    me = me_ref[0]
    rank = rows_ref.shape[0]
    half = mine_ref.shape[1]
    mine, other = mine_ref[:rank, :], other_ref[:rank, :]
    if orthogonal:
        gram = in_order(me, packed_half(mine_ref, rank), packed_half(other_ref, rank))
        factor3 = stacked(inverse_factor(gram), 1)
        mine = applied(factor3, mine).astype(BF16)
        other = applied(factor3, other).astype(BF16)
    rows_ref[:, span(me * half, half)] = mine
    rows_ref[:, span((1 - me) * half, half)] = other
    rows = rows_ref[...]
    gram = dot(rows, rows, 1, 1)
    gram_ref[...] = jnp.zeros_like(gram_ref)
    gram_ref[:, :rank] = jnp.where(me == 0, gram[: rank // 2], gram[rank // 2 :])
    n = owned_ref.shape[0]
    each = rank // (2 * n)
    for c in range(n):
        extra_ref[c] = extra_rows(gram_ref[c * each : (c + 1) * each, :])
    per = TILE // LANE
    for core, out in ((1 - me, theirs_ref), (me, owned_ref)):
        for j in range(n // per):
            at = span(core * (n * LANE) + j * TILE, TILE)
            product = dot(rows, slab_ref[:, at], 1, 0).astype(out.dtype)
            for q in range(per):
                out[j * per + q] = product[:, q * LANE : (q + 1) * LANE]


def join_chunks_kernel(owned_ref, got_ref, extra_ref, out_ref):
    rank = owned_ref.shape[1]
    for c in range(out_ref.shape[0]):
        out_ref[c, :rank, :] = (owned_ref[c] + got_ref[c].astype(F32)).astype(BF16)
        out_ref[c, rank:, :] = extra_ref[c]


def sum_chunks_kernel(parts_ref, out_ref):
    n = parts_ref.shape[0]
    rank = parts_ref.shape[1] - EXTRA
    each = rank // (2 * n)
    total = parts_ref[0].astype(F32)
    for c in range(1, n):
        total = total + parts_ref[c].astype(F32)
    extra = extra_rows(from_extra(total[rank:], each))
    piece = jnp.concatenate([total[:rank].astype(BF16), extra], axis=0)
    for c in range(n):
        out_ref[c] = piece


def join_rows_kernel(mine_ref, got_ref, pack_ref, out_ref):
    rank = mine_ref.shape[0]
    out_ref[:rank, :] = (mine_ref[...] + got_ref[...].astype(F32)).astype(BF16)
    out_ref[rank:, :] = pack_ref[...]


def sum_packed_kernel(a_ref, b_ref, c_ref, d_ref, out_ref):
    total = (a_ref[...].astype(F32) + b_ref[...].astype(F32)) + (
        c_ref[...].astype(F32) + d_ref[...].astype(F32)
    )
    rank = out_ref.shape[0] - EXTRA
    out_ref[:rank, :] = total[:rank].astype(BF16)
    out_ref[rank:, :] = jnp.zeros((EXTRA, out_ref.shape[1]), BF16)
    out_ref[rank:, : 3 * LANE] = stacked(from_packed(total[rank:]), 1)


def moments_kernel(
    scale, me_ref, own_ref, other_ref, rows_ref, first_ref, second_ref,
    columns_ref, gram_ref, new_first_ref, new_second_ref, direction_ref, left_ref,
):
    me = me_ref[0]
    rank = rows_ref.shape[0]
    factor3 = stacked(inverse_factor(gathered_gram(me, own_ref, other_ref, rank)), 1)
    left = applied(factor3, rows_ref[...]).astype(BF16)
    left_ref[...] = (left.astype(F32) * scale).astype(BF16)
    corr_one = 1.0 - 0.9**10
    corr_two = 1.0 - 0.999**10
    total = jnp.zeros((3 * rank, 3 * rank), F32)
    for at, block in gathered_blocks(me, own_ref, other_ref, rank):
        columns = applied(factor3, block)
        columns_ref[:, at] = columns
        three = stacked(columns)
        total = total + dot(three, three, 1, 1)
        new_first = 0.9 * first_ref[:, at] + 0.1 * columns
        new_second = 0.999 * second_ref[:, at] + 0.001 * columns * columns
        new_first_ref[:, at] = new_first
        new_second_ref[:, at] = new_second
        direction = new_first / corr_one / (jnp.sqrt(new_second / corr_two) + 1e-08)
        direction_ref[:, at] = direction.astype(BF16)
    gram_ref[...] = folded(total, rank)


def update_kernel(left_ref, direction_ref, update_ref):
    left = left_ref[...]
    for t in range(0, direction_ref.shape[1], TILE):
        product = dot(left, direction_ref[:, t : t + TILE], 0, 0)
        update_ref[:, t : t + TILE] = product.astype(BF16)


def basis_kernel(a_ref, b_ref, c_ref, d_ref, columns_ref, basis_ref):
    factor = inverse_factor((a_ref[...] + b_ref[...]) + (c_ref[...] + d_ref[...]))
    high, mid, low = thirds(factor)
    wide = jnp.concatenate([low, mid, high, mid, high, high], axis=1).astype(BF16)
    for t in range(0, columns_ref.shape[1], TILE):
        high, mid, low = (x.astype(BF16) for x in thirds(columns_ref[:, t : t + TILE]))
        tall = jnp.concatenate([high, mid, low, high, mid, high], axis=0)
        basis_ref[:, t : t + TILE] = dot(wide, tall, 1, 0)


def call(kernel, outs, operands, scratch=(), hbm=()):
    def spec(i, x):
        if x.dtype == jnp.int32:
            return SMEM
        return pl.BlockSpec(memory_space=pltpu.HBM) if i in hbm else VMEM

    return pl.pallas_call(
        kernel,
        out_shape=[jax.ShapeDtypeStruct(s, t) for s, t in outs],
        in_specs=[spec(i, x) for i, x in enumerate(operands)],
        out_specs=[VMEM] * len(outs),
        scratch_shapes=[pltpu.VMEM(*s) if isinstance(s, tuple) else s for s in scratch],
        compiler_params=pltpu.CompilerParams(vmem_limit_bytes=VMEM_LIMIT),
    )(*operands)


def swapped(x):
    return lax.ppermute(x, "dp", [(0, 1), (1, 0)])


def others(x):
    n = lax.axis_size("mp")
    return [lax.ppermute(x, "mp", [(i, (i + k) % n) for i in range(n)]) for k in (1, 3, 2)]


def sum_over_owners(theirs, owned, extra):
    n, rank, lane = owned.shape
    whole = [((n, rank + EXTRA, lane), BF16)]
    chunks = call(join_chunks_kernel, whole, [owned, swapped(theirs), extra])[0]
    parts = lax.all_to_all(chunks, "vocab", 0, 0)
    copies = call(sum_chunks_kernel, whole, [parts])[0]
    own = lax.all_to_all(copies, "vocab", 0, 0)
    return own, swapped(own)


def local(grad_parts, old_basis, first_moment, second_moment):
    slab = grad_parts[0]
    vocab, width = slab.shape
    rank = old_basis.shape[0]
    half = vocab // 2
    owners = lax.axis_size("vocab")
    me = lax.axis_index("dp").astype(jnp.int32).reshape(1)
    halves = [((rank, half), BF16), ((rank, half), F32)]
    chunk = (owners, rank, LANE)
    chunks_out = [(chunk, BF16), (chunk, F32), ((owners, EXTRA, LANE), BF16), ((rank, vocab), BF16)]
    gram_scratch = [((rank // 2, LANE), F32)]

    theirs, mine, slab = call(
        first_rows_kernel,
        halves + [(slab.shape, BF16)],
        [me, *(pltpu.with_memory_space_constraint(x, pltpu.HBM) for x in (old_basis, slab))],
        [((rank, width), F32), pltpu.SemaphoreType.DMA((vocab // WIDE + 1,))],
        hbm=(1, 2),
    )
    mine = (mine + swapped(theirs).astype(F32)).astype(BF16)
    total = mine.astype(F32)
    for x in others(mine):
        total = total + x.astype(F32)
    mine = total.astype(BF16)
    theirs, owned, extra, _ = call(
        functools.partial(columns_kernel, False),
        chunks_out,
        [me, mine, swapped(mine), slab],
        gram_scratch,
    )
    own, other = sum_over_owners(theirs, owned, extra)

    theirs, mine, pack = call(
        next_rows_kernel,
        halves + [((EXTRA, half), BF16)],
        [me, own, other, slab],
        [((rank, width), BF16)],
    )
    packed = [((rank + EXTRA, half), BF16)]
    mine = call(join_rows_kernel, packed, [mine, swapped(theirs), pack])[0]
    mine = call(sum_packed_kernel, packed, [mine, *others(mine)])[0]
    theirs, owned, extra, rows = call(
        functools.partial(columns_kernel, True),
        chunks_out,
        [me, mine, swapped(mine), slab],
        gram_scratch,
    )
    own, other = sum_over_owners(theirs, owned, extra)

    wide = ((rank, width), F32)
    scale = math.sqrt(vocab * owners)
    assert scale == 2.0 ** round(math.log2(scale))
    columns, gram, new_first, new_second, direction, left = call(
        functools.partial(moments_kernel, scale),
        [wide, ((rank, rank), F32), wide, wide, ((rank, width), BF16), ((rank, vocab), BF16)],
        [me, own, other, rows, first_moment, second_moment],
    )
    gram_others = others(gram)
    update = pl.pallas_call(
        update_kernel,
        out_shape=jax.ShapeDtypeStruct((vocab, width), BF16),
        grid=(vocab // WIDE,),
        in_specs=[
            pl.BlockSpec((rank, WIDE), lambda i: (0, i)),
            pl.BlockSpec((rank, width), lambda i: (0, 0)),
        ],
        out_specs=pl.BlockSpec((WIDE, width), lambda i: (i, 0)),
        compiler_params=pltpu.CompilerParams(vmem_limit_bytes=VMEM_LIMIT),
        cost_estimate=pl.CostEstimate(
            flops=2 * rank * vocab * width, bytes_accessed=2 * vocab * width, transcendentals=0
        ),
    )(left, direction)
    basis = call(basis_kernel, [wide], [gram, *gram_others, columns])[0]
    return (update, basis, new_first, new_second)


def solution(mesh):
    placed = (P("dp", "vocab", "mp"), P(None, "mp"), P(None, "mp"), P(None, "mp"))
    return jax.shard_map(
        local,
        mesh=mesh,
        in_specs=placed,
        out_specs=(P("vocab", "mp"), P(None, "mp"), P(None, "mp"), P(None, "mp")),
        check_vma=False,
    )
```

```python
import functools
import math

import jax
import jax.numpy as jnp
from jax import lax
from jax.experimental import pallas as pl
from jax.experimental.pallas import tpu as pltpu
from jax.sharding import PartitionSpec as P

F32 = jnp.float32
BF16 = jnp.bfloat16
LANE = 128
EXTRA = 16
TILE = 512
WIDE = 256
VMEM_LIMIT = 28 * 1024 * 1024

VMEM = pl.BlockSpec(memory_space=pltpu.VMEM)
SMEM = pl.BlockSpec(memory_space=pltpu.SMEM)


def thirds(value):
    high = value.astype(BF16).astype(F32)
    rest = value - high
    mid = rest.astype(BF16).astype(F32)
    return high, mid, rest - mid


def stacked(value, axis=0):
    return jnp.concatenate(thirds(value), axis=axis).astype(BF16)


def dot(a, b, ca, cb):
    return lax.dot_general(a, b, (((ca,), (cb,)), ((), ())), preferred_element_type=F32)


def inverse_factor(gram):
    rank = gram.shape[0]
    lanes = lax.broadcasted_iota(jnp.int32, (8, rank), 1)
    subs = lax.broadcasted_iota(jnp.int32, (8, LANE), 0)
    blocks = rank // 8
    both = []
    for b in range(blocks):
        eye = jnp.where(lanes == subs[:, :rank] + 8 * b, 1.0, 0.0).astype(F32)
        both.append(jnp.concatenate([gram[8 * b : 8 * b + 8, :], eye], axis=1))
    scale = []
    for b in range(blocks):
        diag = jnp.ones((8, LANE), F32)
        cols = {
            (j, i): jnp.broadcast_to(both[i][:, 8 * b + j : 8 * b + j + 1], (8, LANE))
            for j in range(8)
            for i in range(b, blocks)
        }
        for j in range(8):
            pivot = cols[j, b][j : j + 1, :]
            inverse = 1.0 / pivot
            diag = jnp.where(subs == j, pivot, diag)
            row = both[b][j : j + 1, :] * inverse
            heads = {m: cols[m, b][j : j + 1, :] * inverse for m in range(j + 1, 8)}
            for i in range(b, blocks):
                f = cols[j, i]
                if i == b:
                    f = jnp.where(subs > j, f, 0.0)
                both[i] = both[i] - f * row
                for m in range(j + 1, 8):
                    cols[m, i] = cols[m, i] - f * heads[m]
        scale.append(lax.rsqrt(diag))
    return jnp.concatenate(
        [both[b][:, rank:] * scale[b][:, :rank] for b in range(blocks)], axis=0
    )


def applied(factor3, block):
    return dot(factor3, jnp.concatenate([block] * 3, axis=0), 1, 0)


def folded(total, rank):
    wide = total[:rank] + total[rank : 2 * rank] + total[2 * rank :]
    return wide[:, :rank] + wide[:, rank : 2 * rank] + wide[:, 2 * rank :]


def span(base, size):
    return pl.ds(pl.multiple_of(base, size), size)


def extra_rows(piece):
    pad = jnp.zeros((EXTRA - 3 * piece.shape[0], piece.shape[1]), F32)
    return jnp.concatenate([*thirds(piece), pad], axis=0).astype(BF16)


def from_extra(e, each):
    return e[:each] + e[each : 2 * each] + e[2 * each : 3 * each]


def gathered_gram(chunks_ref, rank):
    n = chunks_ref.shape[0]
    pieces = [
        from_extra(chunks_ref[c, rank : rank + EXTRA, :].astype(F32), rank // n) for c in range(n)
    ]
    return jnp.concatenate(pieces, axis=0)[:, :rank]


def blocks_of(chunks_ref, rank):
    per = TILE // LANE
    for j in range(chunks_ref.shape[0] // per):
        block = jnp.concatenate([chunks_ref[j * per + q, :rank, :] for q in range(per)], axis=1)
        yield slice(j * TILE, (j + 1) * TILE), block


def gram_of(columns_ref, at):
    three = stacked(columns_ref[:, at])
    return dot(three, three, 1, 1)


def first_rows(half, left, slab_hbm, out_ref, slab_ref, sems):
    rows = slab_ref.shape[0]
    copies = [
        pltpu.make_async_copy(
            slab_hbm.at[span(half * rows + t, LANE), :], slab_ref.at[t : t + LANE, :], sems.at[t // LANE]
        )
        for t in range(0, rows, LANE)
    ]
    copies[0].start()
    copies[1].start()
    left = left()
    for i, copy in enumerate(copies):
        copy.wait()
        if i + 2 < len(copies):
            copies[i + 2].start()
        at = slice(i * LANE, (i + 1) * LANE)
        out_ref[:, at] = dot(left, slab_ref[at, :], 1, 1).astype(out_ref.dtype)


def first_theirs_kernel(
    me_ref, basis_hbm, slab_hbm, theirs_ref, slab_ref, left_ref, basis_ref, sems, basis_sem
):
    copy = pltpu.make_async_copy(basis_hbm, basis_ref, basis_sem.at[0])
    copy.start()

    def left():
        copy.wait()
        left_ref[...] = basis_ref[...].astype(BF16)
        return left_ref[...]

    first_rows(1 - me_ref[0], left, slab_hbm, theirs_ref, slab_ref, sems)


def first_mine_kernel(me_ref, left_ref, slab_hbm, mine_ref, slab_ref, sems):
    first_rows(me_ref[0], lambda: left_ref[...], slab_hbm, mine_ref, slab_ref, sems)


def columns_mine_kernel(orthogonal, *refs):
    if orthogonal:
        mine_ref, gram_in_ref, slab_ref, acc_ref, gram_ref, factor_ref, rows_ref = refs
        factor3 = stacked(inverse_factor(gram_in_ref[...]), 1)
        factor_ref[...] = factor3
        mine = applied(factor3, mine_ref[...]).astype(BF16)
        rows_ref[...] = mine
    else:
        mine_ref, slab_ref, acc_ref, gram_ref = refs
        mine = mine_ref[...]
    gram_ref[...] = dot(mine, mine, 1, 1)
    for t in range(0, acc_ref.shape[1], TILE):
        acc_ref[:, t : t + TILE] = dot(mine, slab_ref[:, t : t + TILE], 1, 0)


def add_half(core, rows, acc_ref, slab_ref, out_ref):
    n = out_ref.shape[0]
    per = TILE // LANE
    for j in range(n // per):
        at = span(core * (n * LANE) + j * TILE, TILE)
        product = (acc_ref[:, at] + dot(rows, slab_ref[:, at], 1, 0)).astype(out_ref.dtype)
        for q in range(per):
            out_ref[j * per + q] = product[:, q * LANE : (q + 1) * LANE]


def columns_theirs_kernel(orthogonal, *refs):
    if orthogonal:
        me_ref, other_ref, acc_ref, slab_ref, factor_ref, theirs_ref, rows_ref = refs
        other = applied(factor_ref[...], other_ref[...]).astype(BF16)
        rows_ref[...] = other
    else:
        me_ref, other_ref, acc_ref, slab_ref, theirs_ref = refs
        other = other_ref[...]
    add_half(1 - me_ref[0], other, acc_ref, slab_ref, theirs_ref)


def columns_owned_kernel(
    me_ref, other_ref, acc_ref, slab_ref, gram_mine_ref, owned_ref, extra_ref, gram_ref
):
    other = other_ref[...]
    rank = other.shape[0]
    gram_ref[...] = jnp.zeros_like(gram_ref)
    gram_ref[:, :rank] = gram_mine_ref[...] + dot(other, other, 1, 1)
    each = rank // extra_ref.shape[0]
    for c in range(extra_ref.shape[0]):
        extra_ref[c] = extra_rows(gram_ref[c * each : (c + 1) * each, :])
    add_half(me_ref[0], other, acc_ref, slab_ref, owned_ref)


def join_chunks_kernel(owned_ref, got_ref, extra_ref, out_ref):
    rank = owned_ref.shape[1]
    for c in range(out_ref.shape[0]):
        out_ref[c, :rank, :] = (owned_ref[c] + got_ref[c].astype(F32)).astype(BF16)
        out_ref[c, rank:, :] = extra_ref[c]


def sum_chunks_kernel(parts_ref, out_ref):
    n = parts_ref.shape[0]
    rank = parts_ref.shape[1] - EXTRA
    total = parts_ref[0].astype(F32)
    for c in range(1, n):
        total = total + parts_ref[c].astype(F32)
    extra = extra_rows(from_extra(total[rank:], rank // n))
    piece = jnp.concatenate([total[:rank].astype(BF16), extra], axis=0)
    for c in range(n):
        out_ref[c] = piece


def add_rows(columns, core, acc_ref, slab_ref, out_ref):
    at = span(core * columns.shape[1], columns.shape[1])
    for t in range(0, out_ref.shape[1], WIDE):
        product = dot(columns, slab_ref[t : t + WIDE, at], 1, 1)
        if acc_ref is not None:
            product = acc_ref[:, t : t + WIDE] + product
        out_ref[:, t : t + WIDE] = product.astype(out_ref.dtype)


def rows_own_kernel(
    me_ref, own_ref, theirs_slab_ref, mine_slab_ref,
    factor_ref, theirs_ref, mine_ref, gram_ref, columns_ref, half_ref,
):
    rank = gram_ref.shape[0]
    factor3 = stacked(inverse_factor(gathered_gram(own_ref, rank)), 1)
    factor_ref[...] = factor3
    total = jnp.zeros((3 * rank, 3 * rank), F32)
    for at, block in blocks_of(own_ref, rank):
        columns = applied(factor3, block)
        columns_ref[:, at] = columns
        half_ref[:, at] = columns.astype(BF16)
        total = total + gram_of(columns_ref, at)
    gram_ref[...] = folded(total, rank)
    half = half_ref[...]
    add_rows(half, me_ref[0], None, theirs_slab_ref, theirs_ref)
    add_rows(half, me_ref[0], None, mine_slab_ref, mine_ref)


def rows_theirs_kernel(
    me_ref, other_ref, factor_ref, acc_ref, slab_ref, theirs_ref, columns_ref, half_ref
):
    factor3 = factor_ref[...]
    for at, block in blocks_of(other_ref, factor3.shape[0]):
        columns = applied(factor3, block)
        columns_ref[:, at] = columns
        half_ref[:, at] = columns.astype(BF16)
    add_rows(half_ref[...], 1 - me_ref[0], acc_ref, slab_ref, theirs_ref)


def rows_mine_kernel(
    me_ref, half_ref, columns_ref, gram_own_ref, acc_ref, slab_ref, mine_ref, pack_ref
):
    rank, width = columns_ref.shape
    total = jnp.zeros((3 * rank, 3 * rank), F32)
    for t in range(0, width, TILE):
        total = total + gram_of(columns_ref, slice(t, t + TILE))
    gram = gram_own_ref[...] + folded(total, rank)
    gram = jnp.concatenate([gram[: rank // 2], gram[rank // 2 :]], axis=1)
    pack_ref[...] = jnp.zeros_like(pack_ref)
    pack_ref[:, : 3 * LANE] = stacked(gram, 1)
    add_rows(half_ref[...], 1 - me_ref[0], acc_ref, slab_ref, mine_ref)


def join_rows_kernel(mine_ref, got_ref, pack_ref, out_ref):
    rank = mine_ref.shape[0]
    out_ref[:rank, :] = (mine_ref[...] + got_ref[...].astype(F32)).astype(BF16)
    out_ref[rank:, :] = pack_ref[...]


def sum_packed_kernel(a_ref, b_ref, c_ref, d_ref, rows_ref, gram_ref):
    total = (a_ref[...].astype(F32) + b_ref[...].astype(F32)) + (
        c_ref[...].astype(F32) + d_ref[...].astype(F32)
    )
    rank = rows_ref.shape[0]
    rows_ref[...] = total[:rank].astype(BF16)
    e = total[rank:]
    g = e[:, :LANE] + e[:, LANE : 2 * LANE] + e[:, 2 * LANE : 3 * LANE]
    gram_ref[...] = jnp.concatenate([g[:, :rank], g[:, rank:]], axis=0)


def final_own_kernel(
    scale, me_ref, own_ref, rows_mine_ref, rows_other_ref,
    factor_ref, columns_ref, gram_ref, left_ref,
):
    me = me_ref[0]
    rank, half = rows_mine_ref.shape
    factor3 = stacked(inverse_factor(gathered_gram(own_ref, rank)), 1)
    factor_ref[...] = factor3
    for core, ref in ((me, rows_mine_ref), (1 - me, rows_other_ref)):
        left = applied(factor3, ref[...]).astype(BF16)
        left_ref[:, span(core * half, half)] = (left.astype(F32) * scale).astype(BF16)
    total = jnp.zeros((3 * rank, 3 * rank), F32)
    for at, block in blocks_of(own_ref, rank):
        columns_ref[:, at] = applied(factor3, block)
        total = total + gram_of(columns_ref, at)
    gram_ref[...] = folded(total, rank)


def moments_kernel(
    me_ref, other_ref, factor_ref, own_columns_ref, gram_own_ref, first_ref, second_ref,
    columns_ref, gram_ref, new_first_ref, new_second_ref, direction_ref,
):
    me = me_ref[0]
    factor3 = factor_ref[...]
    rank, width = own_columns_ref.shape
    corr_one = 1.0 - 0.9**10
    corr_two = 1.0 - 0.999**10

    def moments(at, columns):
        columns_ref[:, at] = columns
        new_first = 0.9 * first_ref[:, at] + 0.1 * columns
        new_second = 0.999 * second_ref[:, at] + 0.001 * columns * columns
        new_first_ref[:, at] = new_first
        new_second_ref[:, at] = new_second
        direction = new_first / corr_one / (jnp.sqrt(new_second / corr_two) + 1e-08)
        direction_ref[:, at] = direction.astype(BF16)

    total = jnp.zeros((3 * rank, 3 * rank), F32)
    for part, block in blocks_of(other_ref, rank):
        at = span((1 - me) * width + part.start, TILE)
        moments(at, applied(factor3, block))
        total = total + gram_of(columns_ref, at)
        at = span(me * width + part.start, TILE)
        moments(at, own_columns_ref[:, part])
    gram_ref[...] = gram_own_ref[...] + folded(total, rank)


def update_kernel(left_ref, direction_ref, update_ref):
    left = left_ref[...]
    for t in range(0, direction_ref.shape[1], TILE):
        product = dot(left, direction_ref[:, t : t + TILE], 0, 0)
        update_ref[:, t : t + TILE] = product.astype(BF16)


def basis_kernel(a_ref, b_ref, c_ref, d_ref, columns_ref, basis_ref):
    factor = inverse_factor((a_ref[...] + b_ref[...]) + (c_ref[...] + d_ref[...]))
    high, mid, low = thirds(factor)
    wide = jnp.concatenate([low, mid, high, mid, high, high], axis=1).astype(BF16)
    for t in range(0, columns_ref.shape[1], TILE):
        high, mid, low = (x.astype(BF16) for x in thirds(columns_ref[:, t : t + TILE]))
        tall = jnp.concatenate([high, mid, low, high, mid, high], axis=0)
        basis_ref[:, t : t + TILE] = dot(wide, tall, 1, 0)


def call(kernel, outs, operands, scratch=(), hbm=()):
    def spec(i, x):
        if x.dtype == jnp.int32:
            return SMEM
        return pl.BlockSpec(memory_space=pl.ANY) if i in hbm else VMEM

    moved = sum(x.size * x.dtype.itemsize for x in operands)
    return pl.pallas_call(
        kernel,
        out_shape=[jax.ShapeDtypeStruct(s, t) for s, t in outs],
        in_specs=[spec(i, x) for i, x in enumerate(operands)],
        out_specs=[VMEM] * len(outs),
        scratch_shapes=[pltpu.VMEM(*s) if isinstance(s, tuple) else s for s in scratch],
        compiler_params=pltpu.CompilerParams(vmem_limit_bytes=VMEM_LIMIT),
        cost_estimate=pl.CostEstimate(flops=64 * moved, bytes_accessed=moved, transcendentals=0),
    )(*operands)


def swapped(x):
    return lax.ppermute(x, "dp", [(0, 1), (1, 0)])


def others(x):
    n = lax.axis_size("mp")
    return [lax.ppermute(x, "mp", [(i, (i + k) % n) for i in range(n)]) for k in (1, 3, 2)]


def columns_of(me, mine, slabs, owners, gram=None):
    theirs_slab, mine_slab = slabs
    rank, half = mine.shape
    width = mine_slab.shape[1]
    orthogonal = gram is not None
    square = ((rank, rank), F32)
    acc = ((rank, width), F32)
    halves = ((rank, half), BF16)
    chunk = (owners, rank, LANE)
    whole = [((owners, rank + EXTRA, LANE), BF16)]

    other = swapped(mine)
    if orthogonal:
        outs = [acc, square, ((rank, 3 * rank), BF16), halves]
        operands = [mine, gram, mine_slab]
    else:
        outs = [acc, square]
        operands = [mine, mine_slab]
    acc, gram_mine, *rest = call(functools.partial(columns_mine_kernel, orthogonal), outs, operands)
    if orthogonal:
        factor, mine = rest
        theirs, other = call(
            functools.partial(columns_theirs_kernel, True),
            [(chunk, BF16), halves],
            [me, other, acc, theirs_slab, factor],
        )
    else:
        theirs = call(
            functools.partial(columns_theirs_kernel, False),
            [(chunk, BF16)],
            [me, other, acc, theirs_slab],
        )[0]
    got = swapped(theirs)
    owned, extra = call(
        columns_owned_kernel,
        [(chunk, F32), ((owners, EXTRA, LANE), BF16)],
        [me, other, acc, theirs_slab, gram_mine],
        [((rank, LANE), F32)],
    )
    chunks = call(join_chunks_kernel, whole, [owned, got, extra])[0]
    parts = lax.all_to_all(chunks, "vocab", 0, 0)
    copies = call(sum_chunks_kernel, whole, [parts])[0]
    own = lax.all_to_all(copies, "vocab", 0, 0)
    return own, swapped(own), mine, other


def local(grad_parts, old_basis, first_moment, second_moment):
    slab = grad_parts[0]
    vocab, width = slab.shape
    rank = old_basis.shape[0]
    half = vocab // 2
    owners = lax.axis_size("vocab")
    me = lax.axis_index("dp").astype(jnp.int32).reshape(1)
    theirs_out, mine_out = ((rank, half), BF16), ((rank, half), F32)
    wide = ((rank, width), F32)
    narrow = ((rank, width // 2), F32)
    square = ((rank, rank), F32)
    factor_out = ((rank, 3 * rank), BF16)
    half_slab = ((half, width), BF16)
    sems = pltpu.SemaphoreType.DMA((half // LANE,))

    slab, basis = (pltpu.with_memory_space_constraint(x, pltpu.HBM) for x in (slab, old_basis))
    theirs, theirs_slab, left = call(
        first_theirs_kernel,
        [theirs_out, half_slab, ((rank, width), BF16)],
        [me, basis, slab],
        [((rank, width), F32), sems, pltpu.SemaphoreType.DMA((1,))],
        hbm=(1, 2),
    )
    got = swapped(theirs)
    mine, mine_slab = call(
        first_mine_kernel, [mine_out, half_slab], [me, left, slab], [sems], hbm=(2,)
    )
    slabs = (theirs_slab, mine_slab)
    mine = (mine + got.astype(F32)).astype(BF16)
    total = mine.astype(F32)
    for x in others(mine):
        total = total + x.astype(F32)
    own, other, _, _ = columns_of(me, total.astype(BF16), slabs, owners)

    factor, theirs_acc, mine_acc, gram = call(
        rows_own_kernel,
        [factor_out, mine_out, mine_out, square],
        [me, own, theirs_slab, mine_slab],
        [narrow, ((rank, width // 2), BF16)],
    )
    theirs, columns, columns_half = call(
        rows_theirs_kernel,
        [theirs_out, narrow, ((rank, width // 2), BF16)],
        [me, other, factor, theirs_acc, theirs_slab],
    )
    got = swapped(theirs)
    mine, pack = call(
        rows_mine_kernel,
        [mine_out, ((rank // 2, half), BF16)],
        [me, columns_half, columns, gram, mine_acc, mine_slab],
    )
    mine = call(join_rows_kernel, [((rank + rank // 2, half), BF16)], [mine, got, pack])[0]
    mine, gram = call(sum_packed_kernel, [theirs_out, square], [mine, *others(mine)])
    own, other, rows_mine, rows_other = columns_of(me, mine, slabs, owners, gram)

    scale = math.sqrt(vocab * owners)
    assert scale == 2.0 ** round(math.log2(scale))
    factor, columns, gram, left = call(
        functools.partial(final_own_kernel, scale),
        [factor_out, narrow, square, ((rank, vocab), BF16)],
        [me, own, rows_mine, rows_other],
    )
    columns, gram, new_first, new_second, direction = call(
        moments_kernel,
        [wide, square, wide, wide, ((rank, width), BF16)],
        [me, other, factor, columns, gram, first_moment, second_moment],
    )
    gram_others = others(gram)
    update = pl.pallas_call(
        update_kernel,
        out_shape=jax.ShapeDtypeStruct((vocab, width), BF16),
        grid=(vocab // WIDE,),
        in_specs=[
            pl.BlockSpec((rank, WIDE), lambda i: (0, i)),
            pl.BlockSpec((rank, width), lambda i: (0, 0)),
        ],
        out_specs=pl.BlockSpec((WIDE, width), lambda i: (i, 0)),
        compiler_params=pltpu.CompilerParams(vmem_limit_bytes=VMEM_LIMIT),
        cost_estimate=pl.CostEstimate(
            flops=2 * rank * vocab * width, bytes_accessed=2 * vocab * width, transcendentals=0
        ),
    )(left, direction)
    basis = call(basis_kernel, [wide], [gram, *gram_others, columns])[0]
    return (update, basis, new_first, new_second)


def solution(mesh):
    placed = (P("dp", "vocab", "mp"), P(None, "mp"), P(None, "mp"), P(None, "mp"))
    return jax.shard_map(
        local,
        mesh=mesh,
        in_specs=placed,
        out_specs=(P("vocab", "mp"), P(None, "mp"), P(None, "mp"), P(None, "mp")),
        check_vma=False,
    )
```

```python
import functools
import math

import jax
import jax.numpy as jnp
from jax import lax
from jax.experimental import pallas as pl
from jax.experimental.pallas import tpu as pltpu
from jax.sharding import PartitionSpec as P

F32 = jnp.float32
BF16 = jnp.bfloat16
LANE = 128
EXTRA = 16
TILE = 512
WIDE = 256
VMEM_LIMIT = 28 * 1024 * 1024

VMEM = pl.BlockSpec(memory_space=pltpu.VMEM)
SMEM = pl.BlockSpec(memory_space=pltpu.SMEM)


def thirds(value):
    high = value.astype(BF16).astype(F32)
    rest = value - high
    mid = rest.astype(BF16).astype(F32)
    return high, mid, rest - mid


def stacked(value, axis=0):
    return jnp.concatenate(thirds(value), axis=axis).astype(BF16)


def dot(a, b, ca, cb):
    return lax.dot_general(a, b, (((ca,), (cb,)), ((), ())), preferred_element_type=F32)


def inverse_factor(gram):
    rank = gram.shape[0]
    lanes = lax.broadcasted_iota(jnp.int32, (8, rank), 1)
    subs = lax.broadcasted_iota(jnp.int32, (8, LANE), 0)
    blocks = rank // 8
    both = []
    for b in range(blocks):
        eye = jnp.where(lanes == subs[:, :rank] + 8 * b, 1.0, 0.0).astype(F32)
        both.append(jnp.concatenate([gram[8 * b : 8 * b + 8, :], eye], axis=1))
    scale = []
    for b in range(blocks):
        diag = jnp.ones((8, LANE), F32)
        cols = {
            (j, i): jnp.broadcast_to(both[i][:, 8 * b + j : 8 * b + j + 1], (8, LANE))
            for j in range(8)
            for i in range(b, blocks)
        }
        for j in range(8):
            pivot = cols[j, b][j : j + 1, :]
            inverse = 1.0 / pivot
            diag = jnp.where(subs == j, pivot, diag)
            row = both[b][j : j + 1, :] * inverse
            heads = {m: cols[m, b][j : j + 1, :] * inverse for m in range(j + 1, 8)}
            for i in range(b, blocks):
                f = cols[j, i]
                if i == b:
                    f = jnp.where(subs > j, f, 0.0)
                both[i] = both[i] - f * row
                for m in range(j + 1, 8):
                    cols[m, i] = cols[m, i] - f * heads[m]
        scale.append(lax.rsqrt(diag))
    return jnp.concatenate(
        [both[b][:, rank:] * scale[b][:, :rank] for b in range(blocks)], axis=0
    )


def applied(factor3, block):
    return dot(factor3, jnp.concatenate([block] * 3, axis=0), 1, 0)


def folded(total, rank):
    wide = total[:rank] + total[rank : 2 * rank] + total[2 * rank :]
    return wide[:, :rank] + wide[:, rank : 2 * rank] + wide[:, 2 * rank :]


def span(base, size):
    return pl.ds(pl.multiple_of(base, size), size)


def extra_rows(piece):
    pad = jnp.zeros((EXTRA - 3 * piece.shape[0], piece.shape[1]), F32)
    return jnp.concatenate([*thirds(piece), pad], axis=0).astype(BF16)


def from_extra(e, each):
    return e[:each] + e[each : 2 * each] + e[2 * each : 3 * each]


def gathered_gram(chunks_ref, rank):
    n = chunks_ref.shape[0]
    pieces = [
        from_extra(chunks_ref[c, rank : rank + EXTRA, :].astype(F32), rank // n) for c in range(n)
    ]
    return jnp.concatenate(pieces, axis=0)[:, :rank]


def blocks_of(chunks_ref, rank):
    per = TILE // LANE
    for j in range(chunks_ref.shape[0] // per):
        block = jnp.concatenate([chunks_ref[j * per + q, :rank, :] for q in range(per)], axis=1)
        yield slice(j * TILE, (j + 1) * TILE), block


def gram_of(columns_ref, at):
    three = stacked(columns_ref[:, at])
    return dot(three, three, 1, 1)


def first_theirs_kernel(
    me_ref, basis_hbm, slab_hbm, theirs_ref, left_ref, theirs_slab_ref, mine_slab_ref, basis_ref, sems
):
    me = me_ref[0]
    half = theirs_slab_ref.shape[0]
    basis_copy = pltpu.make_async_copy(basis_hbm, basis_ref, sems.at[0])
    theirs_copies, mine_copies = (
        [
            pltpu.make_async_copy(
                slab_hbm.at[span(core * half + t, WIDE), :],
                ref.at[t : t + WIDE, :],
                sems.at[first + t // WIDE],
            )
            for t in range(0, half, WIDE)
        ]
        for core, ref, first in (
            (1 - me, theirs_slab_ref, 1),
            (me, mine_slab_ref, 1 + half // WIDE),
        )
    )
    for copy in (basis_copy, *theirs_copies):
        copy.start()
    basis_copy.wait()
    for copy in mine_copies:
        copy.start()
    left = basis_ref[...].astype(BF16)
    left_ref[...] = left
    for copy in theirs_copies:
        copy.wait()
    for t in range(0, half, WIDE):
        at = slice(t, t + WIDE)
        theirs_ref[:, at] = dot(left, theirs_slab_ref[at, :], 1, 1).astype(BF16)
    for copy in mine_copies:
        copy.wait()


def first_mine_kernel(left_ref, slab_ref, mine_ref):
    left = left_ref[...]
    for t in range(0, mine_ref.shape[1], WIDE):
        mine_ref[:, t : t + WIDE] = dot(left, slab_ref[t : t + WIDE, :], 1, 1)


def columns_mine_kernel(orthogonal, *refs):
    if orthogonal:
        mine_ref, gram_in_ref, slab_ref, acc_ref, gram_ref, factor_ref, rows_ref = refs
        factor3 = stacked(inverse_factor(gram_in_ref[...]), 1)
        factor_ref[...] = factor3
        mine = applied(factor3, mine_ref[...]).astype(BF16)
        rows_ref[...] = mine
    else:
        mine_ref, slab_ref, acc_ref, gram_ref = refs
        mine = mine_ref[...]
    gram_ref[...] = dot(mine, mine, 1, 1)
    for t in range(0, acc_ref.shape[1], TILE):
        acc_ref[:, t : t + TILE] = dot(mine, slab_ref[:, t : t + TILE], 1, 0)


def add_half(core, rows, acc_ref, slab_ref, out_ref):
    n = out_ref.shape[0]
    per = TILE // LANE
    for j in range(n // per):
        at = span(core * (n * LANE) + j * TILE, TILE)
        product = (acc_ref[:, at] + dot(rows, slab_ref[:, at], 1, 0)).astype(out_ref.dtype)
        for q in range(per):
            out_ref[j * per + q] = product[:, q * LANE : (q + 1) * LANE]


def columns_theirs_kernel(orthogonal, *refs):
    if orthogonal:
        me_ref, other_ref, acc_ref, slab_ref, factor_ref, theirs_ref, rows_ref = refs
        other = applied(factor_ref[...], other_ref[...]).astype(BF16)
        rows_ref[...] = other
    else:
        me_ref, other_ref, acc_ref, slab_ref, theirs_ref = refs
        other = other_ref[...]
    add_half(1 - me_ref[0], other, acc_ref, slab_ref, theirs_ref)


def columns_owned_kernel(
    me_ref, other_ref, acc_ref, slab_ref, gram_mine_ref, owned_ref, extra_ref, gram_ref
):
    other = other_ref[...]
    rank = other.shape[0]
    gram_ref[...] = jnp.zeros_like(gram_ref)
    gram_ref[:, :rank] = gram_mine_ref[...] + dot(other, other, 1, 1)
    each = rank // extra_ref.shape[0]
    for c in range(extra_ref.shape[0]):
        extra_ref[c] = extra_rows(gram_ref[c * each : (c + 1) * each, :])
    add_half(me_ref[0], other, acc_ref, slab_ref, owned_ref)


def join_chunks_kernel(owned_ref, got_ref, extra_ref, out_ref):
    rank = owned_ref.shape[1]
    for c in range(out_ref.shape[0]):
        out_ref[c, :rank, :] = (owned_ref[c] + got_ref[c].astype(F32)).astype(BF16)
        out_ref[c, rank:, :] = extra_ref[c]


def sum_chunks_kernel(parts_ref, out_ref):
    n = parts_ref.shape[0]
    rank = parts_ref.shape[1] - EXTRA
    total = parts_ref[0].astype(F32)
    for c in range(1, n):
        total = total + parts_ref[c].astype(F32)
    extra = extra_rows(from_extra(total[rank:], rank // n))
    piece = jnp.concatenate([total[:rank].astype(BF16), extra], axis=0)
    for c in range(n):
        out_ref[c] = piece


def add_rows(columns, core, acc_ref, slab_ref, out_ref):
    at = span(core * columns.shape[1], columns.shape[1])
    for t in range(0, out_ref.shape[1], WIDE):
        product = dot(columns, slab_ref[t : t + WIDE, at], 1, 1)
        if acc_ref is not None:
            product = acc_ref[:, t : t + WIDE] + product
        out_ref[:, t : t + WIDE] = product.astype(out_ref.dtype)


def rows_own_kernel(
    me_ref, own_ref, theirs_slab_ref, mine_slab_ref,
    factor_ref, theirs_ref, mine_ref, gram_ref, columns_ref, half_ref,
):
    rank = gram_ref.shape[0]
    factor3 = stacked(inverse_factor(gathered_gram(own_ref, rank)), 1)
    factor_ref[...] = factor3
    total = jnp.zeros((3 * rank, 3 * rank), F32)
    for at, block in blocks_of(own_ref, rank):
        columns = applied(factor3, block)
        columns_ref[:, at] = columns
        half_ref[:, at] = columns.astype(BF16)
        total = total + gram_of(columns_ref, at)
    gram_ref[...] = folded(total, rank)
    half = half_ref[...]
    add_rows(half, me_ref[0], None, theirs_slab_ref, theirs_ref)
    add_rows(half, me_ref[0], None, mine_slab_ref, mine_ref)


def rows_theirs_kernel(
    me_ref, other_ref, factor_ref, acc_ref, slab_ref, theirs_ref, columns_ref, half_ref
):
    factor3 = factor_ref[...]
    for at, block in blocks_of(other_ref, factor3.shape[0]):
        columns = applied(factor3, block)
        columns_ref[:, at] = columns
        half_ref[:, at] = columns.astype(BF16)
    add_rows(half_ref[...], 1 - me_ref[0], acc_ref, slab_ref, theirs_ref)


def rows_mine_kernel(
    me_ref, half_ref, columns_ref, gram_own_ref, acc_ref, slab_ref, mine_ref, pack_ref
):
    rank, width = columns_ref.shape
    total = jnp.zeros((3 * rank, 3 * rank), F32)
    for t in range(0, width, TILE):
        total = total + gram_of(columns_ref, slice(t, t + TILE))
    gram = gram_own_ref[...] + folded(total, rank)
    gram = jnp.concatenate([gram[: rank // 2], gram[rank // 2 :]], axis=1)
    pack_ref[...] = jnp.zeros_like(pack_ref)
    pack_ref[:, : 3 * LANE] = stacked(gram, 1)
    add_rows(half_ref[...], 1 - me_ref[0], acc_ref, slab_ref, mine_ref)


def join_rows_kernel(mine_ref, got_ref, pack_ref, out_ref):
    rank = mine_ref.shape[0]
    out_ref[:rank, :] = (mine_ref[...] + got_ref[...].astype(F32)).astype(BF16)
    out_ref[rank:, :] = pack_ref[...]


def sum_packed_kernel(a_ref, b_ref, c_ref, d_ref, rows_ref, gram_ref):
    total = (a_ref[...].astype(F32) + b_ref[...].astype(F32)) + (
        c_ref[...].astype(F32) + d_ref[...].astype(F32)
    )
    rank = rows_ref.shape[0]
    rows_ref[...] = total[:rank].astype(BF16)
    e = total[rank:]
    g = e[:, :LANE] + e[:, LANE : 2 * LANE] + e[:, 2 * LANE : 3 * LANE]
    gram_ref[...] = jnp.concatenate([g[:, :rank], g[:, rank:]], axis=0)


def final_own_kernel(
    scale, me_ref, own_ref, rows_mine_ref, rows_other_ref,
    factor_ref, columns_ref, gram_ref, left_ref,
):
    me = me_ref[0]
    rank, half = rows_mine_ref.shape
    factor3 = stacked(inverse_factor(gathered_gram(own_ref, rank)), 1)
    factor_ref[...] = factor3
    for core, ref in ((me, rows_mine_ref), (1 - me, rows_other_ref)):
        left = applied(factor3, ref[...]).astype(BF16)
        left_ref[:, span(core * half, half)] = (left.astype(F32) * scale).astype(BF16)
    total = jnp.zeros((3 * rank, 3 * rank), F32)
    for at, block in blocks_of(own_ref, rank):
        columns_ref[:, at] = applied(factor3, block)
        total = total + gram_of(columns_ref, at)
    gram_ref[...] = folded(total, rank)


def moments_kernel(
    me_ref, other_ref, factor_ref, own_columns_ref, gram_own_ref, first_ref, second_ref,
    columns_ref, gram_ref, new_first_ref, new_second_ref, direction_ref,
):
    me = me_ref[0]
    factor3 = factor_ref[...]
    rank, width = own_columns_ref.shape
    corr_one = 1.0 - 0.9**10
    corr_two = 1.0 - 0.999**10

    def moments(at, columns):
        columns_ref[:, at] = columns
        new_first = 0.9 * first_ref[:, at] + 0.1 * columns
        new_second = 0.999 * second_ref[:, at] + 0.001 * columns * columns
        new_first_ref[:, at] = new_first
        new_second_ref[:, at] = new_second
        direction = new_first / corr_one / (jnp.sqrt(new_second / corr_two) + 1e-08)
        direction_ref[:, at] = direction.astype(BF16)

    total = jnp.zeros((3 * rank, 3 * rank), F32)
    for part, block in blocks_of(other_ref, rank):
        at = span((1 - me) * width + part.start, TILE)
        moments(at, applied(factor3, block))
        total = total + gram_of(columns_ref, at)
        at = span(me * width + part.start, TILE)
        moments(at, own_columns_ref[:, part])
    gram_ref[...] = gram_own_ref[...] + folded(total, rank)


def update_kernel(
    left_ref, direction_ref, first_ref, second_ref, update_hbm, first_hbm, second_hbm, buffer_ref, sems
):
    copies = [
        pltpu.make_async_copy(first_ref, first_hbm, sems.at[0]),
        pltpu.make_async_copy(second_ref, second_hbm, sems.at[1]),
    ]
    for copy in copies:
        copy.start()
    left = left_ref[...].T
    for i in range(left.shape[0] // TILE):
        rows = slice(i * TILE, (i + 1) * TILE)
        for t in range(0, direction_ref.shape[1], TILE):
            product = dot(left[rows, :], direction_ref[:, t : t + TILE], 1, 0)
            buffer_ref[rows, t : t + TILE] = product.astype(BF16)
        copy = pltpu.make_async_copy(buffer_ref.at[rows, :], update_hbm.at[rows, :], sems.at[2 + i])
        copy.start()
        copies.append(copy)
    for copy in copies:
        copy.wait()


def basis_kernel(a_ref, b_ref, c_ref, d_ref, columns_ref, basis_hbm, basis_ref, sems):
    factor = inverse_factor((a_ref[...] + b_ref[...]) + (c_ref[...] + d_ref[...]))
    high, mid, low = thirds(factor)
    wide = jnp.concatenate([low, mid, high, mid, high, high], axis=1).astype(BF16)
    copies = []
    width = columns_ref.shape[1]
    for part in range(2):
        for t in range(part * width // 2, (part + 1) * width // 2, TILE):
            high, mid, low = (x.astype(BF16) for x in thirds(columns_ref[:, t : t + TILE]))
            tall = jnp.concatenate([high, mid, low, high, mid, high], axis=0)
            basis_ref[:, t : t + TILE] = dot(wide, tall, 1, 0)
        at = slice(part * width // 2, (part + 1) * width // 2)
        copy = pltpu.make_async_copy(basis_ref.at[:, at], basis_hbm.at[:, at], sems.at[part])
        copy.start()
        copies.append(copy)
    for copy in copies:
        copy.wait()


def call(kernel, outs, operands, scratch=(), hbm=(), hbm_out=False):
    def spec(i, x):
        if x.dtype == jnp.int32:
            return SMEM
        return pl.BlockSpec(memory_space=pl.ANY) if i in hbm else VMEM

    moved = sum(x.size * x.dtype.itemsize for x in operands)
    return pl.pallas_call(
        kernel,
        out_shape=[jax.ShapeDtypeStruct(s, t) for s, t in outs],
        in_specs=[spec(i, x) for i, x in enumerate(operands)],
        out_specs=[pl.BlockSpec(memory_space=pl.ANY) if hbm_out else VMEM] * len(outs),
        scratch_shapes=[pltpu.VMEM(*s) if isinstance(s, tuple) else s for s in scratch],
        compiler_params=pltpu.CompilerParams(vmem_limit_bytes=VMEM_LIMIT),
        cost_estimate=pl.CostEstimate(flops=64 * moved, bytes_accessed=moved, transcendentals=0),
    )(*operands)


def swapped(x):
    return lax.ppermute(x, "dp", [(0, 1), (1, 0)])


def others(x):
    n = lax.axis_size("mp")
    return [lax.ppermute(x, "mp", [(i, (i + k) % n) for i in range(n)]) for k in (1, 3, 2)]


def columns_of(me, mine, slabs, owners, gram=None):
    theirs_slab, mine_slab = slabs
    rank, half = mine.shape
    width = mine_slab.shape[1]
    orthogonal = gram is not None
    square = ((rank, rank), F32)
    acc = ((rank, width), F32)
    halves = ((rank, half), BF16)
    chunk = (owners, rank, LANE)
    whole = [((owners, rank + EXTRA, LANE), BF16)]

    other = swapped(mine)
    if orthogonal:
        outs = [acc, square, ((rank, 3 * rank), BF16), halves]
        operands = [mine, gram, mine_slab]
    else:
        outs = [acc, square]
        operands = [mine, mine_slab]
    acc, gram_mine, *rest = call(functools.partial(columns_mine_kernel, orthogonal), outs, operands)
    if orthogonal:
        factor, mine = rest
        theirs, other = call(
            functools.partial(columns_theirs_kernel, True),
            [(chunk, BF16), halves],
            [me, other, acc, theirs_slab, factor],
        )
    else:
        theirs = call(
            functools.partial(columns_theirs_kernel, False),
            [(chunk, BF16)],
            [me, other, acc, theirs_slab],
        )[0]
    got = swapped(theirs)
    owned, extra = call(
        columns_owned_kernel,
        [(chunk, F32), ((owners, EXTRA, LANE), BF16)],
        [me, other, acc, theirs_slab, gram_mine],
        [((rank, LANE), F32)],
    )
    chunks = call(join_chunks_kernel, whole, [owned, got, extra])[0]
    parts = lax.all_to_all(chunks, "vocab", 0, 0)
    copies = call(sum_chunks_kernel, whole, [parts])[0]
    own = lax.all_to_all(copies, "vocab", 0, 0)
    return own, swapped(own), mine, other


def local(grad_parts, old_basis, first_moment, second_moment):
    slab = grad_parts[0]
    vocab, width = slab.shape
    rank = old_basis.shape[0]
    half = vocab // 2
    owners = lax.axis_size("vocab")
    me = lax.axis_index("dp").astype(jnp.int32).reshape(1)
    theirs_out, mine_out = ((rank, half), BF16), ((rank, half), F32)
    wide = ((rank, width), F32)
    narrow = ((rank, width // 2), F32)
    square = ((rank, rank), F32)
    factor_out = ((rank, 3 * rank), BF16)
    half_slab = ((half, width), BF16)

    slab, basis = (pltpu.with_memory_space_constraint(x, pltpu.HBM) for x in (slab, old_basis))
    theirs, left, theirs_slab, mine_slab = call(
        first_theirs_kernel,
        [theirs_out, ((rank, width), BF16), half_slab, half_slab],
        [me, basis, slab],
        [((rank, width), F32), pltpu.SemaphoreType.DMA((1 + vocab // WIDE,))],
        hbm=(1, 2),
    )
    got = swapped(theirs)
    mine = call(first_mine_kernel, [mine_out], [left, mine_slab])[0]
    slabs = (theirs_slab, mine_slab)
    mine = (mine + got.astype(F32)).astype(BF16)
    total = mine.astype(F32)
    for x in others(mine):
        total = total + x.astype(F32)
    own, other, _, _ = columns_of(me, total.astype(BF16), slabs, owners)

    factor, theirs_acc, mine_acc, gram = call(
        rows_own_kernel,
        [factor_out, mine_out, mine_out, square],
        [me, own, theirs_slab, mine_slab],
        [narrow, ((rank, width // 2), BF16)],
    )
    theirs, columns, columns_half = call(
        rows_theirs_kernel,
        [theirs_out, narrow, ((rank, width // 2), BF16)],
        [me, other, factor, theirs_acc, theirs_slab],
    )
    got = swapped(theirs)
    mine, pack = call(
        rows_mine_kernel,
        [mine_out, ((rank // 2, half), BF16)],
        [me, columns_half, columns, gram, mine_acc, mine_slab],
    )
    mine = call(join_rows_kernel, [((rank + rank // 2, half), BF16)], [mine, got, pack])[0]
    mine, gram = call(sum_packed_kernel, [theirs_out, square], [mine, *others(mine)])
    own, other, rows_mine, rows_other = columns_of(me, mine, slabs, owners, gram)

    scale = math.sqrt(vocab * owners)
    assert scale == 2.0 ** round(math.log2(scale))
    factor, columns, gram, left = call(
        functools.partial(final_own_kernel, scale),
        [factor_out, narrow, square, ((rank, vocab), BF16)],
        [me, own, rows_mine, rows_other],
    )
    columns, gram, new_first, new_second, direction = call(
        moments_kernel,
        [wide, square, wide, wide, ((rank, width), BF16)],
        [me, other, factor, columns, gram, first_moment, second_moment],
    )
    gram_others = others(gram)
    update, new_first, new_second = call(
        update_kernel,
        [((vocab, width), BF16), wide, wide],
        [left, direction, new_first, new_second],
        [((vocab, width), BF16), pltpu.SemaphoreType.DMA((2 + vocab // TILE,))],
        hbm_out=True,
    )
    basis = call(
        basis_kernel,
        [wide],
        [gram, *gram_others, columns],
        [((rank, width), F32), pltpu.SemaphoreType.DMA((2,))],
        hbm_out=True,
    )[0]
    return (update, basis, new_first, new_second)


def solution(mesh):
    placed = (P("dp", "vocab", "mp"), P(None, "mp"), P(None, "mp"), P(None, "mp"))
    return jax.shard_map(
        local,
        mesh=mesh,
        in_specs=placed,
        out_specs=(P("vocab", "mp"), P(None, "mp"), P(None, "mp"), P(None, "mp")),
        check_vma=False,
    )
```

```python
import functools
import math

import jax
import jax.numpy as jnp
from jax import lax
from jax.experimental import pallas as pl
from jax.experimental.pallas import tpu as pltpu
from jax.sharding import PartitionSpec as P

F32 = jnp.float32
BF16 = jnp.bfloat16
LANE = 128
EXTRA = 16
TILE = 512
WIDE = 256
VMEM_LIMIT = 28 * 1024 * 1024

VMEM = pl.BlockSpec(memory_space=pltpu.VMEM)
SMEM = pl.BlockSpec(memory_space=pltpu.SMEM)


def thirds(value):
    high = value.astype(BF16).astype(F32)
    rest = value - high
    mid = rest.astype(BF16).astype(F32)
    return high, mid, rest - mid


def stacked(value, axis=0):
    return jnp.concatenate(thirds(value), axis=axis).astype(BF16)


def dot(a, b, ca, cb):
    return lax.dot_general(a, b, (((ca,), (cb,)), ((), ())), preferred_element_type=F32)


def inverse_factor(gram):
    rank = gram.shape[0]
    lanes = lax.broadcasted_iota(jnp.int32, (8, rank), 1)
    subs = lax.broadcasted_iota(jnp.int32, (8, LANE), 0)
    blocks = rank // 8
    both = []
    for b in range(blocks):
        eye = jnp.where(lanes == subs[:, :rank] + 8 * b, 1.0, 0.0).astype(F32)
        both.append(jnp.concatenate([gram[8 * b : 8 * b + 8, :], eye], axis=1))
    scale = []
    for b in range(blocks):
        diag = jnp.ones((8, LANE), F32)
        cols = {
            (j, i): jnp.broadcast_to(both[i][:, 8 * b + j : 8 * b + j + 1], (8, LANE))
            for j in range(8)
            for i in range(b, blocks)
        }
        for j in range(8):
            pivot = cols[j, b][j : j + 1, :]
            inverse = 1.0 / pivot
            diag = jnp.where(subs == j, pivot, diag)
            row = both[b][j : j + 1, :] * inverse
            heads = {m: cols[m, b][j : j + 1, :] * inverse for m in range(j + 1, 8)}
            for i in range(b, blocks):
                f = cols[j, i]
                if i == b:
                    f = jnp.where(subs > j, f, 0.0)
                both[i] = both[i] - f * row
                for m in range(j + 1, 8):
                    cols[m, i] = cols[m, i] - f * heads[m]
        scale.append(lax.rsqrt(diag))
    return jnp.concatenate(
        [both[b][:, rank:] * scale[b][:, :rank] for b in range(blocks)], axis=0
    )


def applied(factor3, block):
    return dot(factor3, jnp.concatenate([block] * 3, axis=0), 1, 0)


def applied_wide(factor3, three):
    rank = factor3.shape[0]
    high, mid, low = (factor3[:, i * rank : (i + 1) * rank] for i in range(3))
    first, second, third = (three[i * rank : (i + 1) * rank] for i in range(3))
    wide = jnp.concatenate([low, mid, high, mid, high, high], axis=1)
    tall = jnp.concatenate([first, second, third, first, second, first], axis=0)
    return dot(wide, tall, 1, 0)


def folded(total, rank):
    wide = total[:rank] + total[rank : 2 * rank] + total[2 * rank :]
    return wide[:, :rank] + wide[:, rank : 2 * rank] + wide[:, 2 * rank :]


def span(base, size):
    return pl.ds(pl.multiple_of(base, size), size)


def extra_rows(piece):
    pad = jnp.zeros((EXTRA - 3 * piece.shape[0], piece.shape[1]), F32)
    return jnp.concatenate([*thirds(piece), pad], axis=0).astype(BF16)


def from_extra(e, each):
    return e[:each] + e[each : 2 * each] + e[2 * each : 3 * each]


def gathered_gram(chunks_ref, rank):
    n = chunks_ref.shape[0]
    pieces = [
        from_extra(chunks_ref[c, rank : rank + EXTRA, :].astype(F32), rank // n) for c in range(n)
    ]
    return jnp.concatenate(pieces, axis=0)[:, :rank]


def blocks_of(chunks_ref, rank):
    per = TILE // LANE
    for j in range(chunks_ref.shape[0] // per):
        block = jnp.concatenate([chunks_ref[j * per + q, :rank, :] for q in range(per)], axis=1)
        yield slice(j * TILE, (j + 1) * TILE), block


def first_theirs_kernel(
    me_ref, basis_hbm, slab_hbm, theirs_ref, left_ref, theirs_slab_ref, mine_slab_ref, basis_ref, sems
):
    me = me_ref[0]
    half = theirs_slab_ref.shape[0]
    basis_copy = pltpu.make_async_copy(basis_hbm, basis_ref, sems.at[0])
    theirs_copies, mine_copies = (
        [
            pltpu.make_async_copy(
                slab_hbm.at[span(core * half + t, WIDE), :],
                ref.at[t : t + WIDE, :],
                sems.at[first + t // WIDE],
            )
            for t in range(0, half, WIDE)
        ]
        for core, ref, first in (
            (1 - me, theirs_slab_ref, 1),
            (me, mine_slab_ref, 1 + half // WIDE),
        )
    )
    for copy in (basis_copy, *theirs_copies):
        copy.start()
    basis_copy.wait()
    for copy in mine_copies:
        copy.start()
    left = basis_ref[...].astype(BF16)
    left_ref[...] = left
    for copy in theirs_copies:
        copy.wait()
    for t in range(0, half, WIDE):
        at = slice(t, t + WIDE)
        theirs_ref[:, at] = dot(left, theirs_slab_ref[at, :], 1, 1).astype(BF16)
    for copy in mine_copies:
        copy.wait()


def first_mine_kernel(left_ref, slab_ref, mine_ref):
    left = left_ref[...]
    for t in range(0, mine_ref.shape[1], WIDE):
        mine_ref[:, t : t + WIDE] = dot(left, slab_ref[t : t + WIDE, :], 1, 1)


def columns_mine_kernel(orthogonal, *refs):
    if orthogonal:
        mine_ref, gram_in_ref, slab_ref, acc_ref, gram_ref, factor_ref, rows_ref = refs
        factor3 = stacked(inverse_factor(gram_in_ref[...]), 1)
        factor_ref[...] = factor3
        mine = applied(factor3, mine_ref[...]).astype(BF16)
        rows_ref[...] = mine
    else:
        mine_ref, slab_ref, acc_ref, gram_ref = refs
        mine = mine_ref[...]
    gram_ref[...] = dot(mine, mine, 1, 1)
    for t in range(0, acc_ref.shape[1], TILE):
        acc_ref[:, t : t + TILE] = dot(mine, slab_ref[:, t : t + TILE], 1, 0)


def add_half(core, rows, acc_ref, slab_ref, out_ref):
    n = out_ref.shape[0]
    per = TILE // LANE
    for j in range(n // per):
        at = span(core * (n * LANE) + j * TILE, TILE)
        product = (acc_ref[:, at] + dot(rows, slab_ref[:, at], 1, 0)).astype(out_ref.dtype)
        for q in range(per):
            out_ref[j * per + q] = product[:, q * LANE : (q + 1) * LANE]


def columns_theirs_kernel(orthogonal, *refs):
    if orthogonal:
        me_ref, other_ref, acc_ref, slab_ref, factor_ref, theirs_ref, rows_ref = refs
        other = applied(factor_ref[...], other_ref[...]).astype(BF16)
        rows_ref[...] = other
    else:
        me_ref, other_ref, acc_ref, slab_ref, theirs_ref = refs
        other = other_ref[...]
    add_half(1 - me_ref[0], other, acc_ref, slab_ref, theirs_ref)


def columns_owned_kernel(
    me_ref, other_ref, acc_ref, slab_ref, gram_mine_ref, owned_ref, extra_ref, gram_ref
):
    other = other_ref[...]
    rank = other.shape[0]
    gram_ref[...] = jnp.zeros_like(gram_ref)
    gram_ref[:, :rank] = gram_mine_ref[...] + dot(other, other, 1, 1)
    each = rank // extra_ref.shape[0]
    for c in range(extra_ref.shape[0]):
        extra_ref[c] = extra_rows(gram_ref[c * each : (c + 1) * each, :])
    add_half(me_ref[0], other, acc_ref, slab_ref, owned_ref)


def join_chunks_kernel(owned_ref, got_ref, extra_ref, out_ref):
    rank = owned_ref.shape[1]
    for c in range(out_ref.shape[0]):
        out_ref[c, :rank, :] = (owned_ref[c] + got_ref[c].astype(F32)).astype(BF16)
        out_ref[c, rank:, :] = extra_ref[c]


def sum_chunks_kernel(parts_ref, out_ref):
    n = parts_ref.shape[0]
    rank = parts_ref.shape[1] - EXTRA
    total = parts_ref[0].astype(F32)
    for c in range(1, n):
        total = total + parts_ref[c].astype(F32)
    extra = extra_rows(from_extra(total[rank:], rank // n))
    piece = jnp.concatenate([total[:rank].astype(BF16), extra], axis=0)
    for c in range(n):
        out_ref[c] = piece


def rows_of(half, core, slab_ref, t):
    return dot(half, slab_ref[t : t + WIDE, span(core * half.shape[1], half.shape[1])], 1, 1)


def whole_half(chunks_ref, rank):
    return jnp.concatenate([chunks_ref[c, :rank, :] for c in range(chunks_ref.shape[0])], axis=1)


def rows_own_kernel(
    me_ref, own_ref, theirs_slab_ref, mine_slab_ref, factor_ref, theirs_ref, mine_ref, gram_ref
):
    me = me_ref[0]
    rank = gram_ref.shape[0]
    half = whole_half(own_ref, rank)
    factor3 = stacked(inverse_factor(gathered_gram(own_ref, rank)), 1)
    for slab_ref, out_ref in ((theirs_slab_ref, theirs_ref), (mine_slab_ref, mine_ref)):
        for t in range(0, out_ref.shape[1], WIDE):
            out_ref[:, t : t + WIDE] = rows_of(half, me, slab_ref, t)
    factor_ref[...] = factor3
    gram_ref[...] = columns_gram(factor3, own_ref)


def columns_gram(factor3, chunks_ref):
    rank = factor3.shape[0]
    total = jnp.zeros((3 * rank, 3 * rank), F32)
    for _, block in blocks_of(chunks_ref, rank):
        three = stacked(applied(factor3, block))
        total = total + dot(three, three, 1, 1)
    return folded(total, rank)


def add_rows(me_ref, other_ref, factor3, acc_ref, slab_ref, out_ref):
    half = whole_half(other_ref, factor3.shape[0])
    for t in range(0, out_ref.shape[1], WIDE):
        at = slice(t, t + WIDE)
        product = acc_ref[:, at] + rows_of(half, 1 - me_ref[0], slab_ref, t)
        out_ref[:, at] = applied_wide(factor3, stacked(product)).astype(out_ref.dtype)


def rows_theirs_kernel(me_ref, other_ref, factor_ref, acc_ref, slab_ref, theirs_ref):
    add_rows(me_ref, other_ref, factor_ref[...], acc_ref, slab_ref, theirs_ref)


def rows_mine_kernel(
    me_ref, other_ref, factor_ref, acc_ref, slab_ref, gram_own_ref, mine_ref, pack_ref
):
    factor3 = factor_ref[...]
    rank = factor3.shape[0]
    add_rows(me_ref, other_ref, factor3, acc_ref, slab_ref, mine_ref)
    gram = gram_own_ref[...] + columns_gram(factor3, other_ref)
    gram = jnp.concatenate([gram[: rank // 2], gram[rank // 2 :]], axis=1)
    pack_ref[...] = jnp.zeros_like(pack_ref)
    pack_ref[:, : 3 * LANE] = stacked(gram, 1)


def join_rows_kernel(mine_ref, got_ref, pack_ref, out_ref):
    rank = mine_ref.shape[0]
    out_ref[:rank, :] = (mine_ref[...] + got_ref[...].astype(F32)).astype(BF16)
    out_ref[rank:, :] = pack_ref[...]


def sum_packed_kernel(a_ref, b_ref, c_ref, d_ref, rows_ref, gram_ref):
    total = (a_ref[...].astype(F32) + b_ref[...].astype(F32)) + (
        c_ref[...].astype(F32) + d_ref[...].astype(F32)
    )
    rank = rows_ref.shape[0]
    rows_ref[...] = total[:rank].astype(BF16)
    e = total[rank:]
    g = e[:, :LANE] + e[:, LANE : 2 * LANE] + e[:, 2 * LANE : 3 * LANE]
    gram_ref[...] = jnp.concatenate([g[:, :rank], g[:, rank:]], axis=0)


def final_own_kernel(
    scale, me_ref, own_ref, rows_mine_ref, rows_other_ref,
    factor_ref, columns_ref, gram_ref, left_ref,
):
    me = me_ref[0]
    rank, half = rows_mine_ref.shape
    factor3 = stacked(inverse_factor(gathered_gram(own_ref, rank)), 1)
    factor_ref[...] = factor3
    for core, ref in ((me, rows_mine_ref), (1 - me, rows_other_ref)):
        left = applied(factor3, ref[...]).astype(BF16)
        left_ref[:, span(core * half, half)] = (left.astype(F32) * scale).astype(BF16)
    gram_ref[...] = keep_columns(factor3, own_ref, columns_ref)


def keep_columns(factor3, chunks_ref, columns_ref):
    rank = factor3.shape[0]
    total = jnp.zeros((3 * rank, 3 * rank), F32)
    for at, block in blocks_of(chunks_ref, rank):
        columns = applied(factor3, block)
        columns_ref[:, at] = columns
        three = stacked(columns)
        total = total + dot(three, three, 1, 1)
    return folded(total, rank)


def final_other_kernel(other_ref, factor_ref, gram_own_ref, columns_ref, gram_ref):
    gram_ref[...] = gram_own_ref[...] + keep_columns(factor_ref[...], other_ref, columns_ref)


def update_kernel(
    me_ref, own_ref, other_ref, left_ref, first_ref, second_ref,
    update_hbm, first_hbm, second_hbm, three_ref,
    update_ref, new_first_ref, new_second_ref, sems,
):
    me = me_ref[0]
    corr_one = 1.0 - 0.9**10
    corr_two = 1.0 - 0.999**10
    width = own_ref.shape[1]
    left = left_ref[...].T
    copies = []
    for i, (core, columns_ref) in enumerate(((me, own_ref), (1 - me, other_ref))):
        for t in range(0, width, TILE):
            at = span(core * width + t, TILE)
            columns = columns_ref[:, t : t + TILE]
            three_ref[:, at] = stacked(columns)
            new_first = 0.9 * first_ref[:, at] + 0.1 * columns
            new_second = 0.999 * second_ref[:, at] + 0.001 * columns * columns
            new_first_ref[:, at] = new_first
            new_second_ref[:, at] = new_second
            direction = new_first / corr_one / (jnp.sqrt(new_second / corr_two) + 1e-08)
            update_ref[:, at] = dot(left, direction.astype(BF16), 1, 0).astype(BF16)
        at = span(core * width, width)
        for j, (ref, hbm) in enumerate(
            ((update_ref, update_hbm), (new_first_ref, first_hbm), (new_second_ref, second_hbm))
        ):
            copy = pltpu.make_async_copy(ref.at[:, at], hbm.at[:, at], sems.at[3 * i + j])
            copy.start()
            copies.append(copy)
    for copy in copies:
        copy.wait()


def basis_kernel(a_ref, b_ref, c_ref, d_ref, three_ref, basis_hbm, basis_ref, sems):
    factor3 = stacked(inverse_factor((a_ref[...] + b_ref[...]) + (c_ref[...] + d_ref[...])), 1)
    copies = []
    half = three_ref.shape[1] // 2
    for part in range(2):
        for t in range(part * half, (part + 1) * half, TILE):
            basis_ref[:, t : t + TILE] = applied_wide(factor3, three_ref[:, t : t + TILE])
        at = slice(part * half, (part + 1) * half)
        copy = pltpu.make_async_copy(basis_ref.at[:, at], basis_hbm.at[:, at], sems.at[part])
        copy.start()
        copies.append(copy)
    for copy in copies:
        copy.wait()


def call(kernel, outs, operands, scratch=(), hbm=(), hbm_out=()):
    def spec(i, x):
        if x.dtype == jnp.int32:
            return SMEM
        return pl.BlockSpec(memory_space=pl.ANY) if i in hbm else VMEM

    moved = sum(x.size * x.dtype.itemsize for x in operands)
    return pl.pallas_call(
        kernel,
        out_shape=[jax.ShapeDtypeStruct(s, t) for s, t in outs],
        in_specs=[spec(i, x) for i, x in enumerate(operands)],
        out_specs=[
            pl.BlockSpec(memory_space=pl.ANY) if i in hbm_out else VMEM for i in range(len(outs))
        ],
        scratch_shapes=[pltpu.VMEM(*s) if isinstance(s, tuple) else s for s in scratch],
        compiler_params=pltpu.CompilerParams(vmem_limit_bytes=VMEM_LIMIT),
        cost_estimate=pl.CostEstimate(flops=64 * moved, bytes_accessed=moved, transcendentals=0),
    )(*operands)


def swapped(x):
    return lax.ppermute(x, "dp", [(0, 1), (1, 0)])


def others(x):
    n = lax.axis_size("mp")
    return [lax.ppermute(x, "mp", [(i, (i + k) % n) for i in range(n)]) for k in (1, 3, 2)]


def columns_of(me, mine, slabs, owners, gram=None):
    theirs_slab, mine_slab = slabs
    rank, half = mine.shape
    width = mine_slab.shape[1]
    orthogonal = gram is not None
    square = ((rank, rank), F32)
    acc = ((rank, width), F32)
    halves = ((rank, half), BF16)
    chunk = (owners, rank, LANE)
    whole = [((owners, rank + EXTRA, LANE), BF16)]

    other = swapped(mine)
    if orthogonal:
        outs = [acc, square, ((rank, 3 * rank), BF16), halves]
        operands = [mine, gram, mine_slab]
    else:
        outs = [acc, square]
        operands = [mine, mine_slab]
    acc, gram_mine, *rest = call(functools.partial(columns_mine_kernel, orthogonal), outs, operands)
    if orthogonal:
        factor, mine = rest
        theirs, other = call(
            functools.partial(columns_theirs_kernel, True),
            [(chunk, BF16), halves],
            [me, other, acc, theirs_slab, factor],
        )
    else:
        theirs = call(
            functools.partial(columns_theirs_kernel, False),
            [(chunk, BF16)],
            [me, other, acc, theirs_slab],
        )[0]
    got = swapped(theirs)
    owned, extra = call(
        columns_owned_kernel,
        [(chunk, F32), ((owners, EXTRA, LANE), BF16)],
        [me, other, acc, theirs_slab, gram_mine],
        [((rank, LANE), F32)],
    )
    chunks = call(join_chunks_kernel, whole, [owned, got, extra])[0]
    parts = lax.all_to_all(chunks, "vocab", 0, 0)
    copies = call(sum_chunks_kernel, whole, [parts])[0]
    own = lax.all_to_all(copies, "vocab", 0, 0)
    return own, swapped(own), mine, other


def local(grad_parts, old_basis, first_moment, second_moment):
    slab = grad_parts[0]
    vocab, width = slab.shape
    rank = old_basis.shape[0]
    half = vocab // 2
    owners = lax.axis_size("vocab")
    me = lax.axis_index("dp").astype(jnp.int32).reshape(1)
    theirs_out, mine_out = ((rank, half), BF16), ((rank, half), F32)
    wide = ((rank, width), F32)
    narrow = ((rank, width // 2), F32)
    square = ((rank, rank), F32)
    factor_out = ((rank, 3 * rank), BF16)
    half_slab = ((half, width), BF16)

    slab, basis = (pltpu.with_memory_space_constraint(x, pltpu.HBM) for x in (slab, old_basis))
    theirs, left, theirs_slab, mine_slab = call(
        first_theirs_kernel,
        [theirs_out, ((rank, width), BF16), half_slab, half_slab],
        [me, basis, slab],
        [((rank, width), F32), pltpu.SemaphoreType.DMA((1 + vocab // WIDE,))],
        hbm=(1, 2),
    )
    got = swapped(theirs)
    mine = call(first_mine_kernel, [mine_out], [left, mine_slab])[0]
    slabs = (theirs_slab, mine_slab)
    mine = (mine + got.astype(F32)).astype(BF16)
    total = mine.astype(F32)
    for x in others(mine):
        total = total + x.astype(F32)
    own, other, _, _ = columns_of(me, total.astype(BF16), slabs, owners)

    factor, theirs_acc, mine_acc, gram = call(
        rows_own_kernel,
        [factor_out, mine_out, mine_out, square],
        [me, own, theirs_slab, mine_slab],
    )
    theirs = call(rows_theirs_kernel, [theirs_out], [me, other, factor, theirs_acc, theirs_slab])[0]
    got = swapped(theirs)
    mine, pack = call(
        rows_mine_kernel,
        [mine_out, ((rank // 2, half), BF16)],
        [me, other, factor, mine_acc, mine_slab, gram],
    )
    mine = call(join_rows_kernel, [((rank + rank // 2, half), BF16)], [mine, got, pack])[0]
    mine, gram = call(sum_packed_kernel, [theirs_out, square], [mine, *others(mine)])
    own, other, rows_mine, rows_other = columns_of(me, mine, slabs, owners, gram)

    scale = math.sqrt(vocab * owners)
    assert scale == 2.0 ** round(math.log2(scale))
    factor, columns_own, gram, left = call(
        functools.partial(final_own_kernel, scale),
        [factor_out, narrow, square, ((rank, vocab), BF16)],
        [me, own, rows_mine, rows_other],
    )
    columns_other, gram = call(final_other_kernel, [narrow, square], [other, factor, gram])
    gram_others = others(gram)
    update_out = ((vocab, width), BF16)
    update, new_first, new_second, three = call(
        update_kernel,
        [update_out, wide, wide, ((3 * rank, width), BF16)],
        [me, columns_own, columns_other, left, first_moment, second_moment],
        [update_out, wide, wide, pltpu.SemaphoreType.DMA((6,))],
        hbm_out=(0, 1, 2),
    )
    basis = call(
        basis_kernel,
        [wide],
        [gram, *gram_others, three],
        [wide, pltpu.SemaphoreType.DMA((2,))],
        hbm_out=(0,),
    )[0]
    return (update, basis, new_first, new_second)


def solution(mesh):
    placed = (P("dp", "vocab", "mp"), P(None, "mp"), P(None, "mp"), P(None, "mp"))
    return jax.shard_map(
        local,
        mesh=mesh,
        in_specs=placed,
        out_specs=(P("vocab", "mp"), P(None, "mp"), P(None, "mp"), P(None, "mp")),
        check_vma=False,
    )
```

```python
import functools
import math

import jax
import jax.numpy as jnp
from jax import lax
from jax.experimental import pallas as pl
from jax.experimental.pallas import tpu as pltpu
from jax.sharding import PartitionSpec as P

F32 = jnp.float32
BF16 = jnp.bfloat16
LANE = 128
EXTRA = 16
TILE = 512
WIDE = 256
VMEM_LIMIT = 28 * 1024 * 1024

VMEM = pl.BlockSpec(memory_space=pltpu.VMEM)
SMEM = pl.BlockSpec(memory_space=pltpu.SMEM)


def thirds(value):
    high = value.astype(BF16).astype(F32)
    rest = value - high
    mid = rest.astype(BF16).astype(F32)
    return high, mid, rest - mid


def stacked(value, axis=0):
    return jnp.concatenate(thirds(value), axis=axis).astype(BF16)


def dot(a, b, ca, cb):
    return lax.dot_general(a, b, (((ca,), (cb,)), ((), ())), preferred_element_type=F32)


def inverse_factor(gram):
    rank = gram.shape[0]
    lanes = lax.broadcasted_iota(jnp.int32, (8, rank), 1)
    subs = lax.broadcasted_iota(jnp.int32, (8, LANE), 0)
    blocks = rank // 8
    both = []
    for b in range(blocks):
        eye = jnp.where(lanes == subs[:, :rank] + 8 * b, 1.0, 0.0).astype(F32)
        both.append(jnp.concatenate([gram[8 * b : 8 * b + 8, :], eye], axis=1))
    scale = []
    for b in range(blocks):
        diag = jnp.ones((8, LANE), F32)
        cols = {
            (j, i): jnp.broadcast_to(both[i][:, 8 * b + j : 8 * b + j + 1], (8, LANE))
            for j in range(8)
            for i in range(b, blocks)
        }
        for j in range(8):
            pivot = cols[j, b][j : j + 1, :]
            inverse = 1.0 / pivot
            diag = jnp.where(subs == j, pivot, diag)
            row = both[b][j : j + 1, :] * inverse
            heads = {m: cols[m, b][j : j + 1, :] * inverse for m in range(j + 1, 8)}
            for i in range(b, blocks):
                f = cols[j, i]
                if i == b:
                    f = jnp.where(subs > j, f, 0.0)
                both[i] = both[i] - f * row
                for m in range(j + 1, 8):
                    cols[m, i] = cols[m, i] - f * heads[m]
        scale.append(lax.rsqrt(diag))
    return jnp.concatenate(
        [both[b][:, rank:] * scale[b][:, :rank] for b in range(blocks)], axis=0
    )


def applied(factor3, block):
    return dot(factor3, jnp.concatenate([block] * 3, axis=0), 1, 0)


def folded(total, rank):
    wide = total[:rank] + total[rank : 2 * rank] + total[2 * rank :]
    return wide[:, :rank] + wide[:, rank : 2 * rank] + wide[:, 2 * rank :]


def span(base, size):
    return pl.ds(pl.multiple_of(base, size), size)


def extra_rows(piece):
    pad = jnp.zeros((EXTRA - 3 * piece.shape[0], piece.shape[1]), F32)
    return jnp.concatenate([*thirds(piece), pad], axis=0).astype(BF16)


def from_extra(e, each):
    return e[:each] + e[each : 2 * each] + e[2 * each : 3 * each]


def gathered_gram(chunks_ref, rank):
    n = chunks_ref.shape[0]
    pieces = [
        from_extra(chunks_ref[c, rank : rank + EXTRA, :].astype(F32), rank // n) for c in range(n)
    ]
    return jnp.concatenate(pieces, axis=0)[:, :rank]


def blocks_of(chunks_ref, rank):
    per = TILE // LANE
    for j in range(chunks_ref.shape[0] // per):
        block = jnp.concatenate([chunks_ref[j * per + q, :rank, :] for q in range(per)], axis=1)
        yield slice(j * TILE, (j + 1) * TILE), block


def gram_of(columns_ref, at):
    three = stacked(columns_ref[:, at])
    return dot(three, three, 1, 1)


def first_theirs_kernel(
    me_ref, basis_hbm, slab_hbm, theirs_ref, left_ref, theirs_slab_ref, mine_slab_ref, basis_ref, sems
):
    me = me_ref[0]
    half = theirs_slab_ref.shape[0]
    basis_copy = pltpu.make_async_copy(basis_hbm, basis_ref, sems.at[0])
    theirs_copies, mine_copies = (
        [
            pltpu.make_async_copy(
                slab_hbm.at[span(core * half + t, WIDE), :],
                ref.at[t : t + WIDE, :],
                sems.at[first + t // WIDE],
            )
            for t in range(0, half, WIDE)
        ]
        for core, ref, first in (
            (1 - me, theirs_slab_ref, 1),
            (me, mine_slab_ref, 1 + half // WIDE),
        )
    )
    for copy in (basis_copy, *theirs_copies):
        copy.start()
    basis_copy.wait()
    for copy in mine_copies:
        copy.start()
    left = basis_ref[...].astype(BF16)
    left_ref[...] = left
    for copy in theirs_copies:
        copy.wait()
    for t in range(0, half, WIDE):
        at = slice(t, t + WIDE)
        theirs_ref[:, at] = dot(left, theirs_slab_ref[at, :], 1, 1).astype(BF16)
    for copy in mine_copies:
        copy.wait()


def first_mine_kernel(left_ref, slab_ref, mine_ref):
    left = left_ref[...]
    for t in range(0, mine_ref.shape[1], WIDE):
        mine_ref[:, t : t + WIDE] = dot(left, slab_ref[t : t + WIDE, :], 1, 1)


def columns_mine_kernel(orthogonal, *refs):
    if orthogonal:
        mine_ref, gram_in_ref, slab_ref, acc_ref, gram_ref, factor_ref, rows_ref = refs
        factor3 = stacked(inverse_factor(gram_in_ref[...]), 1)
        factor_ref[...] = factor3
        mine = applied(factor3, mine_ref[...]).astype(BF16)
        rows_ref[...] = mine
    else:
        mine_ref, slab_ref, acc_ref, gram_ref = refs
        mine = mine_ref[...]
    gram_ref[...] = dot(mine, mine, 1, 1)
    for t in range(0, acc_ref.shape[1], TILE):
        acc_ref[:, t : t + TILE] = dot(mine, slab_ref[:, t : t + TILE], 1, 0)


def add_half(core, rows, acc_ref, slab_ref, out_ref):
    n = out_ref.shape[0]
    per = TILE // LANE
    for j in range(n // per):
        at = span(core * (n * LANE) + j * TILE, TILE)
        product = (acc_ref[:, at] + dot(rows, slab_ref[:, at], 1, 0)).astype(out_ref.dtype)
        for q in range(per):
            out_ref[j * per + q] = product[:, q * LANE : (q + 1) * LANE]


def columns_theirs_kernel(orthogonal, *refs):
    if orthogonal:
        me_ref, other_ref, acc_ref, slab_ref, factor_ref, theirs_ref, rows_ref = refs
        other = applied(factor_ref[...], other_ref[...]).astype(BF16)
        rows_ref[...] = other
    else:
        me_ref, other_ref, acc_ref, slab_ref, theirs_ref = refs
        other = other_ref[...]
    add_half(1 - me_ref[0], other, acc_ref, slab_ref, theirs_ref)


def columns_owned_kernel(
    me_ref, other_ref, acc_ref, slab_ref, gram_mine_ref, owned_ref, extra_ref, gram_ref
):
    other = other_ref[...]
    rank = other.shape[0]
    gram_ref[...] = jnp.zeros_like(gram_ref)
    gram_ref[:, :rank] = gram_mine_ref[...] + dot(other, other, 1, 1)
    each = rank // extra_ref.shape[0]
    for c in range(extra_ref.shape[0]):
        extra_ref[c] = extra_rows(gram_ref[c * each : (c + 1) * each, :])
    add_half(me_ref[0], other, acc_ref, slab_ref, owned_ref)


def join_chunks_kernel(owned_ref, got_ref, extra_ref, out_ref):
    rank = owned_ref.shape[1]
    for c in range(out_ref.shape[0]):
        out_ref[c, :rank, :] = (owned_ref[c] + got_ref[c].astype(F32)).astype(BF16)
        out_ref[c, rank:, :] = extra_ref[c]


def sum_chunks_kernel(parts_ref, out_ref):
    n = parts_ref.shape[0]
    rank = parts_ref.shape[1] - EXTRA
    total = parts_ref[0].astype(F32)
    for c in range(1, n):
        total = total + parts_ref[c].astype(F32)
    extra = extra_rows(from_extra(total[rank:], rank // n))
    piece = jnp.concatenate([total[:rank].astype(BF16), extra], axis=0)
    for c in range(n):
        out_ref[c] = piece


def add_rows(columns, core, acc_ref, slab_ref, out_ref):
    at = span(core * columns.shape[1], columns.shape[1])
    for t in range(0, out_ref.shape[1], WIDE):
        product = dot(columns, slab_ref[t : t + WIDE, at], 1, 1)
        if acc_ref is not None:
            product = acc_ref[:, t : t + WIDE] + product
        out_ref[:, t : t + WIDE] = product.astype(out_ref.dtype)


def rows_own_kernel(
    me_ref, own_ref, theirs_slab_ref, mine_slab_ref,
    factor_ref, theirs_ref, mine_ref, gram_ref, columns_ref, half_ref,
):
    rank = gram_ref.shape[0]
    factor3 = stacked(inverse_factor(gathered_gram(own_ref, rank)), 1)
    factor_ref[...] = factor3
    total = jnp.zeros((3 * rank, 3 * rank), F32)
    for at, block in blocks_of(own_ref, rank):
        columns = applied(factor3, block)
        columns_ref[:, at] = columns
        half_ref[:, at] = columns.astype(BF16)
        total = total + gram_of(columns_ref, at)
    gram_ref[...] = folded(total, rank)
    half = half_ref[...]
    add_rows(half, me_ref[0], None, theirs_slab_ref, theirs_ref)
    add_rows(half, me_ref[0], None, mine_slab_ref, mine_ref)


def rows_theirs_kernel(
    me_ref, other_ref, factor_ref, acc_ref, slab_ref, theirs_ref, columns_ref, half_ref
):
    factor3 = factor_ref[...]
    for at, block in blocks_of(other_ref, factor3.shape[0]):
        columns = applied(factor3, block)
        columns_ref[:, at] = columns
        half_ref[:, at] = columns.astype(BF16)
    add_rows(half_ref[...], 1 - me_ref[0], acc_ref, slab_ref, theirs_ref)


def rows_mine_kernel(
    me_ref, half_ref, columns_ref, gram_own_ref, acc_ref, slab_ref, mine_ref, pack_ref
):
    rank, width = columns_ref.shape
    total = jnp.zeros((3 * rank, 3 * rank), F32)
    for t in range(0, width, TILE):
        total = total + gram_of(columns_ref, slice(t, t + TILE))
    gram = gram_own_ref[...] + folded(total, rank)
    gram = jnp.concatenate([gram[: rank // 2], gram[rank // 2 :]], axis=1)
    pack_ref[...] = jnp.zeros_like(pack_ref)
    pack_ref[:, : 3 * LANE] = stacked(gram, 1)
    add_rows(half_ref[...], 1 - me_ref[0], acc_ref, slab_ref, mine_ref)


def join_rows_kernel(mine_ref, got_ref, pack_ref, out_ref):
    rank = mine_ref.shape[0]
    out_ref[:rank, :] = (mine_ref[...] + got_ref[...].astype(F32)).astype(BF16)
    out_ref[rank:, :] = pack_ref[...]


def sum_packed_kernel(a_ref, b_ref, c_ref, d_ref, rows_ref, gram_ref):
    total = (a_ref[...].astype(F32) + b_ref[...].astype(F32)) + (
        c_ref[...].astype(F32) + d_ref[...].astype(F32)
    )
    rank = rows_ref.shape[0]
    rows_ref[...] = total[:rank].astype(BF16)
    e = total[rank:]
    g = e[:, :LANE] + e[:, LANE : 2 * LANE] + e[:, 2 * LANE : 3 * LANE]
    gram_ref[...] = jnp.concatenate([g[:, :rank], g[:, rank:]], axis=0)


def final_own_kernel(
    scale, me_ref, own_ref, rows_mine_ref, rows_other_ref,
    factor_ref, columns_ref, gram_ref, left_ref,
):
    me = me_ref[0]
    rank, half = rows_mine_ref.shape
    factor3 = stacked(inverse_factor(gathered_gram(own_ref, rank)), 1)
    factor_ref[...] = factor3
    for core, ref in ((me, rows_mine_ref), (1 - me, rows_other_ref)):
        left = applied(factor3, ref[...]).astype(BF16)
        left_ref[:, span(core * half, half)] = (left.astype(F32) * scale).astype(BF16)
    gram_ref[...] = keep_columns(factor3, own_ref, columns_ref)


def keep_columns(factor3, chunks_ref, columns_ref):
    rank = factor3.shape[0]
    total = jnp.zeros((3 * rank, 3 * rank), F32)
    for at, block in blocks_of(chunks_ref, rank):
        columns = applied(factor3, block)
        columns_ref[:, at] = columns
        three = stacked(columns)
        total = total + dot(three, three, 1, 1)
    return folded(total, rank)


def final_other_kernel(other_ref, factor_ref, gram_own_ref, columns_ref, gram_ref):
    gram_ref[...] = gram_own_ref[...] + keep_columns(factor_ref[...], other_ref, columns_ref)


def half_update(core, columns_ref, left, first_ref, second_ref, outs, buffers, sems):
    corr_one = 1.0 - 0.9**10
    corr_two = 1.0 - 0.999**10
    update_ref, new_first_ref, new_second_ref = buffers
    width = columns_ref.shape[1]
    for t in range(0, width, TILE):
        at = span(core * width + t, TILE)
        columns = columns_ref[:, t : t + TILE]
        new_first = 0.9 * first_ref[:, at] + 0.1 * columns
        new_second = 0.999 * second_ref[:, at] + 0.001 * columns * columns
        here = slice(t, t + TILE)
        new_first_ref[:, here] = new_first
        new_second_ref[:, here] = new_second
        direction = new_first / corr_one / (jnp.sqrt(new_second / corr_two) + 1e-08)
        update_ref[:, here] = dot(left, direction.astype(BF16), 1, 0).astype(BF16)
    copies = [
        pltpu.make_async_copy(ref, hbm.at[:, span(core * width, width)], sems.at[i])
        for i, (ref, hbm) in enumerate(zip(buffers, outs))
    ]
    for copy in copies:
        copy.start()
    return copies


def update_own_kernel(me_ref, columns_ref, left_ref, first_ref, second_ref, *refs):
    outs, turned_ref, buffers, sems = refs[:3], refs[3], refs[4:7], refs[7]
    left = left_ref[...].T
    turned_ref[...] = left
    copies = half_update(me_ref[0], columns_ref, left, first_ref, second_ref, outs, buffers, sems)
    for copy in copies:
        copy.wait()


def update_other_kernel(
    me_ref, other_ref, turned_ref, first_ref, second_ref, own_ref, a_ref, b_ref, c_ref, d_ref, *refs
):
    me = me_ref[0]
    outs, basis_hbm, buffers, basis_ref, sems = refs[3:6], refs[6], refs[7:10], refs[10], refs[11]
    copies = half_update(
        1 - me, other_ref, turned_ref[...], first_ref, second_ref, outs, buffers, sems
    )
    factor = inverse_factor((a_ref[...] + b_ref[...]) + (c_ref[...] + d_ref[...]))
    high, mid, _ = thirds(factor)
    wide = jnp.concatenate([high, high, mid], axis=1).astype(BF16)
    width = own_ref.shape[1]
    for i, (core, ref) in enumerate(((me, own_ref), (1 - me, other_ref))):
        for t in range(0, width, TILE):
            high, mid, _ = thirds(ref[:, t : t + TILE])
            tall = jnp.concatenate([high, mid, high], axis=0).astype(BF16)
            basis_ref[:, i * width + t : i * width + t + TILE] = dot(wide, tall, 1, 0)
        copy = pltpu.make_async_copy(
            basis_ref.at[:, i * width : (i + 1) * width],
            basis_hbm.at[:, span(core * width, width)],
            sems.at[3 + i],
        )
        copy.start()
        copies.append(copy)
    for copy in copies:
        copy.wait()


def call(kernel, outs, operands, scratch=(), hbm=(), hbm_out=(), aliases=None):
    def spec(i, x):
        if x.dtype == jnp.int32:
            return SMEM
        return pl.BlockSpec(memory_space=pl.ANY) if i in hbm else VMEM

    moved = sum(x.size * x.dtype.itemsize for x in operands)
    return pl.pallas_call(
        kernel,
        out_shape=[jax.ShapeDtypeStruct(s, t) for s, t in outs],
        in_specs=[spec(i, x) for i, x in enumerate(operands)],
        out_specs=[
            pl.BlockSpec(memory_space=pl.ANY) if i in hbm_out else VMEM for i in range(len(outs))
        ],
        input_output_aliases=aliases or {},
        scratch_shapes=[pltpu.VMEM(*s) if isinstance(s, tuple) else s for s in scratch],
        compiler_params=pltpu.CompilerParams(vmem_limit_bytes=VMEM_LIMIT),
        cost_estimate=pl.CostEstimate(flops=64 * moved, bytes_accessed=moved, transcendentals=0),
    )(*operands)


def swapped(x):
    return lax.ppermute(x, "dp", [(0, 1), (1, 0)])


def others(x):
    n = lax.axis_size("mp")
    return [lax.ppermute(x, "mp", [(i, (i + k) % n) for i in range(n)]) for k in (1, 3, 2)]


def columns_of(me, mine, slabs, owners, gram=None):
    theirs_slab, mine_slab = slabs
    rank, half = mine.shape
    width = mine_slab.shape[1]
    orthogonal = gram is not None
    square = ((rank, rank), F32)
    acc = ((rank, width), F32)
    halves = ((rank, half), BF16)
    chunk = (owners, rank, LANE)
    whole = [((owners, rank + EXTRA, LANE), BF16)]

    other = swapped(mine)
    if orthogonal:
        outs = [acc, square, ((rank, 3 * rank), BF16), halves]
        operands = [mine, gram, mine_slab]
    else:
        outs = [acc, square]
        operands = [mine, mine_slab]
    acc, gram_mine, *rest = call(functools.partial(columns_mine_kernel, orthogonal), outs, operands)
    if orthogonal:
        factor, mine = rest
        theirs, other = call(
            functools.partial(columns_theirs_kernel, True),
            [(chunk, BF16), halves],
            [me, other, acc, theirs_slab, factor],
        )
    else:
        theirs = call(
            functools.partial(columns_theirs_kernel, False),
            [(chunk, BF16)],
            [me, other, acc, theirs_slab],
        )[0]
    got = swapped(theirs)
    owned, extra = call(
        columns_owned_kernel,
        [(chunk, F32), ((owners, EXTRA, LANE), BF16)],
        [me, other, acc, theirs_slab, gram_mine],
        [((rank, LANE), F32)],
    )
    chunks = call(join_chunks_kernel, whole, [owned, got, extra])[0]
    parts = lax.all_to_all(chunks, "vocab", 0, 0)
    copies = call(sum_chunks_kernel, whole, [parts])[0]
    own = lax.all_to_all(copies, "vocab", 0, 0)
    return own, swapped(own), mine, other


def local(grad_parts, old_basis, first_moment, second_moment):
    slab = grad_parts[0]
    vocab, width = slab.shape
    rank = old_basis.shape[0]
    half = vocab // 2
    owners = lax.axis_size("vocab")
    me = lax.axis_index("dp").astype(jnp.int32).reshape(1)
    theirs_out, mine_out = ((rank, half), BF16), ((rank, half), F32)
    wide = ((rank, width), F32)
    narrow = ((rank, width // 2), F32)
    square = ((rank, rank), F32)
    factor_out = ((rank, 3 * rank), BF16)
    half_slab = ((half, width), BF16)

    slab, basis = (pltpu.with_memory_space_constraint(x, pltpu.HBM) for x in (slab, old_basis))
    theirs, left, theirs_slab, mine_slab = call(
        first_theirs_kernel,
        [theirs_out, ((rank, width), BF16), half_slab, half_slab],
        [me, basis, slab],
        [((rank, width), F32), pltpu.SemaphoreType.DMA((1 + vocab // WIDE,))],
        hbm=(1, 2),
    )
    got = swapped(theirs)
    mine = call(first_mine_kernel, [mine_out], [left, mine_slab])[0]
    slabs = (theirs_slab, mine_slab)
    mine = (mine + got.astype(F32)).astype(BF16)
    total = mine.astype(F32)
    for x in others(mine):
        total = total + x.astype(F32)
    own, other, _, _ = columns_of(me, total.astype(BF16), slabs, owners)

    factor, theirs_acc, mine_acc, gram = call(
        rows_own_kernel,
        [factor_out, mine_out, mine_out, square],
        [me, own, theirs_slab, mine_slab],
        [narrow, ((rank, width // 2), BF16)],
    )
    theirs, columns, columns_half = call(
        rows_theirs_kernel,
        [theirs_out, narrow, ((rank, width // 2), BF16)],
        [me, other, factor, theirs_acc, theirs_slab],
    )
    got = swapped(theirs)
    mine, pack = call(
        rows_mine_kernel,
        [mine_out, ((rank // 2, half), BF16)],
        [me, columns_half, columns, gram, mine_acc, mine_slab],
    )
    mine = call(join_rows_kernel, [((rank + rank // 2, half), BF16)], [mine, got, pack])[0]
    mine, gram = call(sum_packed_kernel, [theirs_out, square], [mine, *others(mine)])
    own, other, rows_mine, rows_other = columns_of(me, mine, slabs, owners, gram)

    scale = math.sqrt(vocab * owners)
    assert scale == 2.0 ** round(math.log2(scale))
    factor, columns_own, gram, left = call(
        functools.partial(final_own_kernel, scale),
        [factor_out, narrow, square, ((rank, vocab), BF16)],
        [me, own, rows_mine, rows_other],
    )
    columns_other, gram = call(final_other_kernel, [narrow, square], [other, factor, gram])
    gram_others = others(gram)
    outs = [((vocab, width), BF16), wide, wide]
    buffers = [((vocab, width // 2), BF16), narrow, narrow]
    *begun, turned = call(
        update_own_kernel,
        outs + [((vocab, rank), BF16)],
        [me, columns_own, left, first_moment, second_moment],
        buffers + [pltpu.SemaphoreType.DMA((3,))],
        hbm_out=(0, 1, 2),
    )
    operands = [me, columns_other, turned, first_moment, second_moment, columns_own, gram, *gram_others]
    n = len(operands)
    update, new_first, new_second, basis = call(
        update_other_kernel,
        outs + [wide],
        operands + begun,
        buffers + [wide, pltpu.SemaphoreType.DMA((5,))],
        hbm=(n, n + 1, n + 2),
        hbm_out=(0, 1, 2, 3),
        aliases={n: 0, n + 1: 1, n + 2: 2},
    )
    return (update, basis, new_first, new_second)


def solution(mesh):
    placed = (P("dp", "vocab", "mp"), P(None, "mp"), P(None, "mp"), P(None, "mp"))
    return jax.shard_map(
        local,
        mesh=mesh,
        in_specs=placed,
        out_specs=(P("vocab", "mp"), P(None, "mp"), P(None, "mp"), P(None, "mp")),
        check_vma=False,
    )
```

```python
import functools
import math

import jax
import jax.numpy as jnp
from jax import lax
from jax.experimental import pallas as pl
from jax.experimental.pallas import tpu as pltpu
from jax.sharding import PartitionSpec as P

F32 = jnp.float32
BF16 = jnp.bfloat16
LANE = 128
EXTRA = 16
TILE = 512
WIDE = 256
PIECE = 1024
VMEM_LIMIT = 28 * 1024 * 1024

VMEM = pl.BlockSpec(memory_space=pltpu.VMEM)
SMEM = pl.BlockSpec(memory_space=pltpu.SMEM)


def thirds(value):
    high = value.astype(BF16).astype(F32)
    rest = value - high
    mid = rest.astype(BF16).astype(F32)
    return high, mid, rest - mid


def stacked(value, axis=0):
    return jnp.concatenate(thirds(value), axis=axis).astype(BF16)


def dot(a, b, ca, cb):
    return lax.dot_general(a, b, (((ca,), (cb,)), ((), ())), preferred_element_type=F32)


def inverse_factor(gram):
    rank = gram.shape[0]
    lanes = lax.broadcasted_iota(jnp.int32, (8, rank), 1)
    subs = lax.broadcasted_iota(jnp.int32, (8, LANE), 0)
    blocks = rank // 8
    both = []
    for b in range(blocks):
        eye = jnp.where(lanes == subs[:, :rank] + 8 * b, 1.0, 0.0).astype(F32)
        both.append(jnp.concatenate([gram[8 * b : 8 * b + 8, :], eye], axis=1))
    scale = []
    for b0 in range(0, blocks, 2):
        diags = [jnp.ones((8, LANE), F32)] * 2
        cols = {
            (j, i): jnp.broadcast_to(both[i][:, 8 * b0 + j : 8 * b0 + j + 1], (8, LANE))
            for j in range(16)
            for i in range(b0, blocks)
        }
        for j in range(16):
            b, s = b0 + j // 8, j % 8
            pivot = cols[j, b][s : s + 1, :]
            inverse = 1.0 / pivot
            diags[j // 8] = jnp.where(subs == s, pivot, diags[j // 8])
            row = both[b][s : s + 1, :] * inverse
            heads = {m: cols[m, b][s : s + 1, :] * inverse for m in range(j + 1, 16)}
            for i in range(b, blocks):
                f = cols[j, i]
                if i == b:
                    f = jnp.where(subs > s, f, 0.0)
                both[i] = both[i] - f * row
                for m in range(j + 1, 16):
                    cols[m, i] = cols[m, i] - f * heads[m]
        scale.extend(lax.rsqrt(d) for d in diags)
    return jnp.concatenate(
        [both[b][:, rank:] * scale[b][:, :rank] for b in range(blocks)], axis=0
    )


def applied(factor3, block):
    return dot(factor3, jnp.concatenate([block] * 3, axis=0), 1, 0)


def folded(total, rank):
    wide = total[:rank] + total[rank : 2 * rank] + total[2 * rank :]
    return wide[:, :rank] + wide[:, rank : 2 * rank] + wide[:, 2 * rank :]


def span(base, size):
    return pl.ds(pl.multiple_of(base, size), size)


def extra_rows(piece):
    pad = jnp.zeros((EXTRA - 3 * piece.shape[0], piece.shape[1]), F32)
    return jnp.concatenate([*thirds(piece), pad], axis=0).astype(BF16)


def from_extra(e, each):
    return e[:each] + e[each : 2 * each] + e[2 * each : 3 * each]


def gathered_gram(chunks_ref, rank):
    n = chunks_ref.shape[0]
    pieces = [
        from_extra(chunks_ref[c, rank : rank + EXTRA, :].astype(F32), rank // n) for c in range(n)
    ]
    return jnp.concatenate(pieces, axis=0)[:, :rank]


def blocks_of(chunks_ref, rank):
    per = TILE // LANE
    for j in range(chunks_ref.shape[0] // per):
        block = jnp.concatenate([chunks_ref[j * per + q, :rank, :] for q in range(per)], axis=1)
        yield slice(j * TILE, (j + 1) * TILE), block


def gram_of(columns_ref, at):
    three = stacked(columns_ref[:, at])
    return dot(three, three, 1, 1)


def first_theirs_kernel(
    me_ref, basis_hbm, slab_hbm, theirs_ref, left_ref, theirs_slab_ref, mine_slab_ref, basis_ref, sems
):
    me = me_ref[0]
    half = theirs_slab_ref.shape[0]
    basis_copy = pltpu.make_async_copy(basis_hbm, basis_ref, sems.at[0])
    theirs_copies, mine_copies = (
        [
            pltpu.make_async_copy(
                slab_hbm.at[span(core * half + t, WIDE), :],
                ref.at[t : t + WIDE, :],
                sems.at[first + t // WIDE],
            )
            for t in range(0, half, WIDE)
        ]
        for core, ref, first in (
            (1 - me, theirs_slab_ref, 1),
            (me, mine_slab_ref, 1 + half // WIDE),
        )
    )
    for copy in (basis_copy, *theirs_copies):
        copy.start()
    basis_copy.wait()
    for copy in mine_copies:
        copy.start()
    left = basis_ref[...].astype(BF16)
    left_ref[...] = left
    for copy in theirs_copies:
        copy.wait()
    for t in range(0, half, WIDE):
        at = slice(t, t + WIDE)
        theirs_ref[:, at] = dot(theirs_slab_ref[at, :], left, 1, 1).T.astype(BF16)
    for copy in mine_copies:
        copy.wait()


def first_mine_kernel(left_ref, slab_ref, mine_ref):
    left = left_ref[...]
    for t in range(0, mine_ref.shape[1], WIDE):
        mine_ref[:, t : t + WIDE] = dot(slab_ref[t : t + WIDE, :], left, 1, 1).T


def columns_mine_kernel(orthogonal, *refs):
    if orthogonal:
        mine_ref, gram_in_ref, slab_ref, acc_ref, gram_ref, factor_ref, rows_ref = refs
        factor3 = stacked(inverse_factor(gram_in_ref[...]), 1)
        factor_ref[...] = factor3
        mine = applied(factor3, mine_ref[...]).astype(BF16)
        rows_ref[...] = mine
    else:
        mine_ref, slab_ref, acc_ref, gram_ref = refs
        mine = mine_ref[...]
    gram_ref[...] = dot(mine, mine, 1, 1)
    for t in range(0, acc_ref.shape[1], TILE):
        acc_ref[:, t : t + TILE] = dot(mine, slab_ref[:, t : t + TILE], 1, 0)


def add_half(core, rows, acc_ref, slab_ref, out_ref):
    n = out_ref.shape[0]
    per = TILE // LANE
    for j in range(n // per):
        at = span(core * (n * LANE) + j * TILE, TILE)
        product = (acc_ref[:, at] + dot(rows, slab_ref[:, at], 1, 0)).astype(out_ref.dtype)
        for q in range(per):
            out_ref[j * per + q] = product[:, q * LANE : (q + 1) * LANE]


def columns_theirs_kernel(orthogonal, *refs):
    if orthogonal:
        me_ref, other_ref, acc_ref, slab_ref, factor_ref, theirs_ref, rows_ref = refs
        other = applied(factor_ref[...], other_ref[...]).astype(BF16)
        rows_ref[...] = other
    else:
        me_ref, other_ref, acc_ref, slab_ref, theirs_ref = refs
        other = other_ref[...]
    add_half(1 - me_ref[0], other, acc_ref, slab_ref, theirs_ref)


def columns_owned_kernel(
    me_ref, other_ref, acc_ref, slab_ref, gram_mine_ref, owned_ref, extra_ref, gram_ref
):
    other = other_ref[...]
    rank = other.shape[0]
    gram_ref[...] = jnp.zeros_like(gram_ref)
    gram_ref[:, :rank] = gram_mine_ref[...] + dot(other, other, 1, 1)
    each = rank // extra_ref.shape[0]
    for c in range(extra_ref.shape[0]):
        extra_ref[c] = extra_rows(gram_ref[c * each : (c + 1) * each, :])
    add_half(me_ref[0], other, acc_ref, slab_ref, owned_ref)


def join_chunks_kernel(owned_ref, got_ref, extra_ref, out_ref):
    rank = owned_ref.shape[1]
    for c in range(out_ref.shape[0]):
        out_ref[c, :rank, :] = (owned_ref[c] + got_ref[c].astype(F32)).astype(BF16)
        out_ref[c, rank:, :] = extra_ref[c]


def sum_chunks_kernel(parts_ref, out_ref):
    n = parts_ref.shape[0]
    rank = parts_ref.shape[1] - EXTRA
    total = parts_ref[0].astype(F32)
    for c in range(1, n):
        total = total + parts_ref[c].astype(F32)
    extra = extra_rows(from_extra(total[rank:], rank // n))
    piece = jnp.concatenate([total[:rank].astype(BF16), extra], axis=0)
    for c in range(n):
        out_ref[c] = piece


def add_rows(columns, core, acc_ref, slab_ref, out_ref):
    at = span(core * columns.shape[1], columns.shape[1])
    for t in range(0, out_ref.shape[1], WIDE):
        product = dot(slab_ref[t : t + WIDE, at], columns, 1, 1).T
        if acc_ref is not None:
            product = acc_ref[:, t : t + WIDE] + product
        out_ref[:, t : t + WIDE] = product.astype(out_ref.dtype)


def rows_own_kernel(
    me_ref, own_ref, theirs_slab_ref, mine_slab_ref,
    factor_ref, theirs_ref, mine_ref, gram_ref, columns_ref, half_ref,
):
    rank = gram_ref.shape[0]
    factor3 = stacked(inverse_factor(gathered_gram(own_ref, rank)), 1)
    factor_ref[...] = factor3
    total = jnp.zeros((3 * rank, 3 * rank), F32)
    for at, block in blocks_of(own_ref, rank):
        columns = applied(factor3, block)
        columns_ref[:, at] = columns
        half_ref[:, at] = columns.astype(BF16)
        total = total + gram_of(columns_ref, at)
    gram_ref[...] = folded(total, rank)
    half = half_ref[...]
    add_rows(half, me_ref[0], None, theirs_slab_ref, theirs_ref)
    add_rows(half, me_ref[0], None, mine_slab_ref, mine_ref)


def rows_theirs_kernel(
    me_ref, other_ref, factor_ref, acc_ref, slab_ref, theirs_ref, columns_ref, half_ref
):
    factor3 = factor_ref[...]
    for at, block in blocks_of(other_ref, factor3.shape[0]):
        columns = applied(factor3, block)
        columns_ref[:, at] = columns
        half_ref[:, at] = columns.astype(BF16)
    add_rows(half_ref[...], 1 - me_ref[0], acc_ref, slab_ref, theirs_ref)


def rows_mine_kernel(
    me_ref, half_ref, columns_ref, gram_own_ref, acc_ref, slab_ref, mine_ref, pack_ref
):
    rank, width = columns_ref.shape
    total = jnp.zeros((3 * rank, 3 * rank), F32)
    for t in range(0, width, TILE):
        total = total + gram_of(columns_ref, slice(t, t + TILE))
    gram = gram_own_ref[...] + folded(total, rank)
    gram = jnp.concatenate([gram[: rank // 2], gram[rank // 2 :]], axis=1)
    pack_ref[...] = jnp.zeros_like(pack_ref)
    pack_ref[:, : 3 * LANE] = stacked(gram, 1)
    add_rows(half_ref[...], 1 - me_ref[0], acc_ref, slab_ref, mine_ref)


def join_rows_kernel(mine_ref, got_ref, pack_ref, out_ref):
    rank = mine_ref.shape[0]
    out_ref[:rank, :] = (mine_ref[...] + got_ref[...].astype(F32)).astype(BF16)
    out_ref[rank:, :] = pack_ref[...]


def sum_packed_kernel(a_ref, b_ref, c_ref, d_ref, rows_ref, gram_ref):
    total = (a_ref[...].astype(F32) + b_ref[...].astype(F32)) + (
        c_ref[...].astype(F32) + d_ref[...].astype(F32)
    )
    rank = rows_ref.shape[0]
    rows_ref[...] = total[:rank].astype(BF16)
    e = total[rank:]
    g = e[:, :LANE] + e[:, LANE : 2 * LANE] + e[:, 2 * LANE : 3 * LANE]
    gram_ref[...] = jnp.concatenate([g[:, :rank], g[:, rank:]], axis=0)


def final_own_kernel(
    scale, me_ref, own_ref, rows_mine_ref, rows_other_ref,
    factor_ref, columns_ref, gram_ref, left_ref,
):
    me = me_ref[0]
    rank, half = rows_mine_ref.shape
    factor3 = stacked(inverse_factor(gathered_gram(own_ref, rank)), 1)
    factor_ref[...] = factor3
    for core, ref in ((me, rows_mine_ref), (1 - me, rows_other_ref)):
        left = applied(factor3, ref[...]).astype(BF16)
        left_ref[:, span(core * half, half)] = (left.astype(F32) * scale).astype(BF16)
    gram_ref[...] = keep_columns(factor3, own_ref, columns_ref)


def keep_columns(factor3, chunks_ref, columns_ref):
    rank = factor3.shape[0]
    total = jnp.zeros((3 * rank, 3 * rank), F32)
    for at, block in blocks_of(chunks_ref, rank):
        columns = applied(factor3, block)
        columns_ref[:, at] = columns
        three = stacked(columns)
        total = total + dot(three, three, 1, 1)
    return folded(total, rank)


def final_other_kernel(other_ref, factor_ref, gram_own_ref, columns_ref, gram_ref):
    gram_ref[...] = gram_own_ref[...] + keep_columns(factor_ref[...], other_ref, columns_ref)


def update_pieces(pieces, left, first_ref, second_ref, outs, buffers, sems):
    corr_one = 1.0 - 0.9**10
    corr_two = 1.0 - 0.999**10
    update_ref, new_first_ref, new_second_ref = buffers
    copies = []
    for i, (base, columns_ref, start) in enumerate(pieces):
        for t in range(0, PIECE, TILE):
            at = span(base + start + t, TILE)
            columns = columns_ref[:, start + t : start + t + TILE]
            new_first = 0.9 * first_ref[:, at] + 0.1 * columns
            new_second = 0.999 * second_ref[:, at] + 0.001 * columns * columns
            here = slice(i * PIECE + t, i * PIECE + t + TILE)
            new_first_ref[:, here] = new_first
            new_second_ref[:, here] = new_second
            direction = new_first / corr_one / (jnp.sqrt(new_second / corr_two) + 1e-08)
            update_ref[:, here] = dot(left, direction.astype(BF16), 1, 0).astype(BF16)
        here = slice(i * PIECE, (i + 1) * PIECE)
        for j, (ref, hbm) in enumerate(zip(buffers, outs)):
            copy = pltpu.make_async_copy(
                ref.at[:, here], hbm.at[:, span(base + start, PIECE)], sems.at[3 * i + j]
            )
            copy.start()
            copies.append(copy)
    return copies


def update_most_kernel(me_ref, own_ref, other_ref, left_ref, first_ref, second_ref, *refs):
    outs, turned_ref, buffers, sems = refs[:3], refs[3], refs[4:7], refs[7]
    me = me_ref[0]
    width = own_ref.shape[1]
    left = left_ref[...].T
    turned_ref[...] = left
    pieces = [(me * width, own_ref, t) for t in range(0, width, PIECE)]
    pieces += [((1 - me) * width, other_ref, t) for t in range(0, width - PIECE, PIECE)]
    for copy in update_pieces(pieces, left, first_ref, second_ref, outs, buffers, sems):
        copy.wait()


def update_last_kernel(
    me_ref, own_ref, other_ref, turned_ref, first_ref, second_ref, a_ref, b_ref, c_ref, d_ref, *refs
):
    me = me_ref[0]
    outs, basis_hbm, buffers, basis_ref, sems = refs[3:6], refs[6], refs[7:10], refs[10], refs[11]
    width = own_ref.shape[1]
    pieces = [((1 - me) * width, other_ref, width - PIECE)]
    copies = update_pieces(
        pieces, turned_ref[...], first_ref, second_ref, outs, buffers, sems
    )
    factor = inverse_factor((a_ref[...] + b_ref[...]) + (c_ref[...] + d_ref[...]))
    high, mid, _ = thirds(factor)
    wide = jnp.concatenate([high, high, mid], axis=1).astype(BF16)
    for i, (core, ref) in enumerate(((me, own_ref), (1 - me, other_ref))):
        for t in range(0, width, TILE):
            high, mid, _ = thirds(ref[:, t : t + TILE])
            tall = jnp.concatenate([high, mid, high], axis=0).astype(BF16)
            basis_ref[:, i * width + t : i * width + t + TILE] = dot(wide, tall, 1, 0)
        copy = pltpu.make_async_copy(
            basis_ref.at[:, i * width : (i + 1) * width],
            basis_hbm.at[:, span(core * width, width)],
            sems.at[3 + i],
        )
        copy.start()
        copies.append(copy)
    for copy in copies:
        copy.wait()


def call(kernel, outs, operands, scratch=(), hbm=(), hbm_out=(), aliases=None):
    def spec(i, x):
        if x.dtype == jnp.int32:
            return SMEM
        return pl.BlockSpec(memory_space=pl.ANY) if i in hbm else VMEM

    moved = sum(x.size * x.dtype.itemsize for x in operands)
    return pl.pallas_call(
        kernel,
        out_shape=[jax.ShapeDtypeStruct(s, t) for s, t in outs],
        in_specs=[spec(i, x) for i, x in enumerate(operands)],
        out_specs=[
            pl.BlockSpec(memory_space=pl.ANY) if i in hbm_out else VMEM for i in range(len(outs))
        ],
        input_output_aliases=aliases or {},
        scratch_shapes=[pltpu.VMEM(*s) if isinstance(s, tuple) else s for s in scratch],
        compiler_params=pltpu.CompilerParams(vmem_limit_bytes=VMEM_LIMIT),
        cost_estimate=pl.CostEstimate(flops=64 * moved, bytes_accessed=moved, transcendentals=0),
    )(*operands)


def swapped(x):
    return lax.ppermute(x, "dp", [(0, 1), (1, 0)])


def others(x):
    n = lax.axis_size("mp")
    return [lax.ppermute(x, "mp", [(i, (i + k) % n) for i in range(n)]) for k in (1, 3, 2)]


def columns_of(me, mine, slabs, owners, gram=None):
    theirs_slab, mine_slab = slabs
    rank, half = mine.shape
    width = mine_slab.shape[1]
    orthogonal = gram is not None
    square = ((rank, rank), F32)
    acc = ((rank, width), F32)
    halves = ((rank, half), BF16)
    chunk = (owners, rank, LANE)
    whole = [((owners, rank + EXTRA, LANE), BF16)]

    other = swapped(mine)
    if orthogonal:
        outs = [acc, square, ((rank, 3 * rank), BF16), halves]
        operands = [mine, gram, mine_slab]
    else:
        outs = [acc, square]
        operands = [mine, mine_slab]
    acc, gram_mine, *rest = call(functools.partial(columns_mine_kernel, orthogonal), outs, operands)
    if orthogonal:
        factor, mine = rest
        theirs, other = call(
            functools.partial(columns_theirs_kernel, True),
            [(chunk, BF16), halves],
            [me, other, acc, theirs_slab, factor],
        )
    else:
        theirs = call(
            functools.partial(columns_theirs_kernel, False),
            [(chunk, BF16)],
            [me, other, acc, theirs_slab],
        )[0]
    got = swapped(theirs)
    owned, extra = call(
        columns_owned_kernel,
        [(chunk, F32), ((owners, EXTRA, LANE), BF16)],
        [me, other, acc, theirs_slab, gram_mine],
        [((rank, LANE), F32)],
    )
    chunks = call(join_chunks_kernel, whole, [owned, got, extra])[0]
    parts = lax.all_to_all(chunks, "vocab", 0, 0)
    copies = call(sum_chunks_kernel, whole, [parts])[0]
    own = lax.all_to_all(copies, "vocab", 0, 0)
    return own, swapped(own), mine, other


def local(grad_parts, old_basis, first_moment, second_moment):
    slab = grad_parts[0]
    vocab, width = slab.shape
    rank = old_basis.shape[0]
    half = vocab // 2
    owners = lax.axis_size("vocab")
    me = lax.axis_index("dp").astype(jnp.int32).reshape(1)
    theirs_out, mine_out = ((rank, half), BF16), ((rank, half), F32)
    wide = ((rank, width), F32)
    narrow = ((rank, width // 2), F32)
    square = ((rank, rank), F32)
    factor_out = ((rank, 3 * rank), BF16)
    half_slab = ((half, width), BF16)

    slab, basis = (pltpu.with_memory_space_constraint(x, pltpu.HBM) for x in (slab, old_basis))
    theirs, left, theirs_slab, mine_slab = call(
        first_theirs_kernel,
        [theirs_out, ((rank, width), BF16), half_slab, half_slab],
        [me, basis, slab],
        [((rank, width), F32), pltpu.SemaphoreType.DMA((1 + vocab // WIDE,))],
        hbm=(1, 2),
    )
    got = swapped(theirs)
    mine = call(first_mine_kernel, [mine_out], [left, mine_slab])[0]
    slabs = (theirs_slab, mine_slab)
    mine = (mine + got.astype(F32)).astype(BF16)
    total = mine.astype(F32)
    for x in others(mine):
        total = total + x.astype(F32)
    own, other, _, _ = columns_of(me, total.astype(BF16), slabs, owners)

    factor, theirs_acc, mine_acc, gram = call(
        rows_own_kernel,
        [factor_out, mine_out, mine_out, square],
        [me, own, theirs_slab, mine_slab],
        [narrow, ((rank, width // 2), BF16)],
    )
    theirs, columns, columns_half = call(
        rows_theirs_kernel,
        [theirs_out, narrow, ((rank, width // 2), BF16)],
        [me, other, factor, theirs_acc, theirs_slab],
    )
    got = swapped(theirs)
    mine, pack = call(
        rows_mine_kernel,
        [mine_out, ((rank // 2, half), BF16)],
        [me, columns_half, columns, gram, mine_acc, mine_slab],
    )
    mine = call(join_rows_kernel, [((rank + rank // 2, half), BF16)], [mine, got, pack])[0]
    mine, gram = call(sum_packed_kernel, [theirs_out, square], [mine, *others(mine)])
    own, other, rows_mine, rows_other = columns_of(me, mine, slabs, owners, gram)

    scale = math.sqrt(vocab * owners)
    assert scale == 2.0 ** round(math.log2(scale))
    factor, columns_own, gram, left = call(
        functools.partial(final_own_kernel, scale),
        [factor_out, narrow, square, ((rank, vocab), BF16)],
        [me, own, rows_mine, rows_other],
    )
    columns_other, gram = call(final_other_kernel, [narrow, square], [other, factor, gram])
    gram_others = others(gram)
    outs = [((vocab, width), BF16), wide, wide]

    def buffers(columns):
        return [((vocab, columns), BF16), ((rank, columns), F32), ((rank, columns), F32)]

    *begun, turned = call(
        update_most_kernel,
        outs + [((vocab, rank), BF16)],
        [me, columns_own, columns_other, left, first_moment, second_moment],
        buffers(width - PIECE) + [pltpu.SemaphoreType.DMA((3 * (width // PIECE - 1),))],
        hbm_out=(0, 1, 2),
    )
    operands = [me, columns_own, columns_other, turned, first_moment, second_moment]
    operands += [gram, *gram_others]
    n = len(operands)
    update, new_first, new_second, basis = call(
        update_last_kernel,
        outs + [wide],
        operands + begun,
        buffers(PIECE) + [wide, pltpu.SemaphoreType.DMA((5,))],
        hbm=(n, n + 1, n + 2),
        hbm_out=(0, 1, 2, 3),
        aliases={n: 0, n + 1: 1, n + 2: 2},
    )
    return (update, basis, new_first, new_second)


def solution(mesh):
    placed = (P("dp", "vocab", "mp"), P(None, "mp"), P(None, "mp"), P(None, "mp"))
    return jax.shard_map(
        local,
        mesh=mesh,
        in_specs=placed,
        out_specs=(P("vocab", "mp"), P(None, "mp"), P(None, "mp"), P(None, "mp")),
        check_vma=False,
    )
```

```python
import functools
import math

import jax
import jax.numpy as jnp
from jax import lax
from jax.experimental import pallas as pl
from jax.experimental.pallas import tpu as pltpu
from jax.sharding import PartitionSpec as P

F32 = jnp.float32
BF16 = jnp.bfloat16
LANE = 128
EXTRA = 16
TILE = 512
WIDE = 256
PIECE = 1024
PANEL = 16
VMEM_LIMIT = 28 * 1024 * 1024

VMEM = pl.BlockSpec(memory_space=pltpu.VMEM)
SMEM = pl.BlockSpec(memory_space=pltpu.SMEM)


def thirds(value):
    high = value.astype(BF16).astype(F32)
    rest = value - high
    mid = rest.astype(BF16).astype(F32)
    return high, mid, rest - mid


def stacked(value, axis=0):
    return jnp.concatenate(thirds(value), axis=axis).astype(BF16)


def dot(a, b, ca, cb):
    return lax.dot_general(a, b, (((ca,), (cb,)), ((), ())), preferred_element_type=F32)


def inverse_factor(gram):
    rank = gram.shape[0]
    lanes = lax.broadcasted_iota(jnp.int32, (8, rank), 1)
    subs = lax.broadcasted_iota(jnp.int32, (8, LANE), 0)
    blocks = rank // 8
    both = []
    for b in range(blocks):
        eye = jnp.where(lanes == subs[:, :rank] + 8 * b, 1.0, 0.0).astype(F32)
        both.append(jnp.concatenate([gram[8 * b : 8 * b + 8, :], eye], axis=1))
    scale = []
    for b0 in range(0, blocks, PANEL // 8):
        diags = [jnp.ones((8, LANE), F32)] * (PANEL // 8)
        cols = {
            (j, i): jnp.broadcast_to(both[i][:, 8 * b0 + j : 8 * b0 + j + 1], (8, LANE))
            for j in range(PANEL)
            for i in range(b0, blocks)
        }
        for j in range(PANEL):
            b, s = b0 + j // 8, j % 8
            pivot = cols[j, b][s : s + 1, :]
            inverse = 1.0 / pivot
            diags[j // 8] = jnp.where(subs == s, pivot, diags[j // 8])
            row = both[b][s : s + 1, :] * inverse
            heads = {m: cols[m, b][s : s + 1, :] * inverse for m in range(j + 1, PANEL)}
            for i in range(b, blocks):
                f = cols[j, i]
                if i == b:
                    f = jnp.where(subs > s, f, 0.0)
                both[i] = both[i] - f * row
                for m in range(j + 1, PANEL):
                    cols[m, i] = cols[m, i] - f * heads[m]
        scale.extend(lax.rsqrt(d) for d in diags)
    return jnp.concatenate(
        [both[b][:, rank:] * scale[b][:, :rank] for b in range(blocks)], axis=0
    )


def applied(factor3, block):
    return dot(factor3, jnp.concatenate([block] * 3, axis=0), 1, 0)


def folded(total, rank):
    wide = total[:rank] + total[rank : 2 * rank] + total[2 * rank :]
    return wide[:, :rank] + wide[:, rank : 2 * rank] + wide[:, 2 * rank :]


def span(base, size):
    return pl.ds(pl.multiple_of(base, size), size)


def extra_rows(piece):
    pad = jnp.zeros((EXTRA - 3 * piece.shape[0], piece.shape[1]), F32)
    return jnp.concatenate([*thirds(piece), pad], axis=0).astype(BF16)


def from_extra(e, each):
    return e[:each] + e[each : 2 * each] + e[2 * each : 3 * each]


def gathered_gram(chunks_ref, rank):
    n = chunks_ref.shape[0]
    pieces = [
        from_extra(chunks_ref[c, rank : rank + EXTRA, :].astype(F32), rank // n) for c in range(n)
    ]
    return jnp.concatenate(pieces, axis=0)[:, :rank]


def blocks_of(chunks_ref, rank):
    per = TILE // LANE
    for j in range(chunks_ref.shape[0] // per):
        block = jnp.concatenate([chunks_ref[j * per + q, :rank, :] for q in range(per)], axis=1)
        yield slice(j * TILE, (j + 1) * TILE), block


def gram_of(columns_ref, at):
    three = stacked(columns_ref[:, at])
    return dot(three, three, 1, 1)


def first_theirs_kernel(
    me_ref, basis_hbm, slab_hbm, theirs_ref, left_ref, theirs_slab_ref, mine_slab_ref, basis_ref, sems
):
    me = me_ref[0]
    half = theirs_slab_ref.shape[0]
    basis_copy = pltpu.make_async_copy(basis_hbm, basis_ref, sems.at[0])
    theirs_copies, mine_copies = (
        [
            pltpu.make_async_copy(
                slab_hbm.at[span(core * half + t, WIDE), :],
                ref.at[t : t + WIDE, :],
                sems.at[first + t // WIDE],
            )
            for t in range(0, half, WIDE)
        ]
        for core, ref, first in (
            (1 - me, theirs_slab_ref, 1),
            (me, mine_slab_ref, 1 + half // WIDE),
        )
    )
    for copy in (basis_copy, *theirs_copies):
        copy.start()
    basis_copy.wait()
    for copy in mine_copies:
        copy.start()
    left = basis_ref[...].astype(BF16)
    left_ref[...] = left
    for copy in theirs_copies:
        copy.wait()
    for t in range(0, half, WIDE):
        at = slice(t, t + WIDE)
        theirs_ref[:, at] = dot(theirs_slab_ref[at, :], left, 1, 1).T.astype(BF16)
    for copy in mine_copies:
        copy.wait()


def first_mine_kernel(left_ref, slab_ref, mine_ref):
    left = left_ref[...]
    for t in range(0, mine_ref.shape[1], WIDE):
        mine_ref[:, t : t + WIDE] = dot(slab_ref[t : t + WIDE, :], left, 1, 1).T


def columns_mine_kernel(orthogonal, *refs):
    if orthogonal:
        me_ref, mine_ref, gram_in_ref, slab_ref, acc_ref, gram_ref, factor_ref, rows_ref = refs
        factor3 = stacked(inverse_factor(gram_in_ref[...]), 1)
        factor_ref[...] = factor3
        mine = applied(factor3, mine_ref[...]).astype(BF16)
        rows_ref[...] = mine
    else:
        me_ref, mine_ref, slab_ref, acc_ref, gram_ref = refs
        mine = mine_ref[...]
    gram_ref[...] = dot(mine, mine, 1, 1)
    width = acc_ref.shape[1]
    for t in range(0, width, TILE):
        at = span((1 - me_ref[0]) * width + t, TILE)
        acc_ref[:, t : t + TILE] = dot(mine, slab_ref[:, at], 1, 0)


def put_chunks(out_ref, j, product):
    per = TILE // LANE
    product = product.astype(out_ref.dtype)
    for q in range(per):
        out_ref[j * per + q] = product[:, q * LANE : (q + 1) * LANE]


def columns_theirs_kernel(orthogonal, *refs):
    if orthogonal:
        me_ref, other_ref, acc_ref, slab_ref, factor_ref, theirs_ref, rows_ref = refs
        other = applied(factor_ref[...], other_ref[...]).astype(BF16)
        rows_ref[...] = other
    else:
        me_ref, other_ref, acc_ref, slab_ref, theirs_ref = refs
        other = other_ref[...]
    width = acc_ref.shape[1]
    for j in range(width // TILE):
        at = span((1 - me_ref[0]) * width + j * TILE, TILE)
        product = acc_ref[:, j * TILE : (j + 1) * TILE] + dot(other, slab_ref[:, at], 1, 0)
        put_chunks(theirs_ref, j, product)


def columns_owned_kernel(
    me_ref, mine_ref, other_ref, theirs_slab_ref, mine_slab_ref, gram_mine_ref,
    owned_ref, extra_ref, gram_ref,
):
    mine, other = mine_ref[...], other_ref[...]
    rank = other.shape[0]
    gram_ref[...] = jnp.zeros_like(gram_ref)
    gram_ref[:, :rank] = gram_mine_ref[...] + dot(other, other, 1, 1)
    each = rank // extra_ref.shape[0]
    for c in range(extra_ref.shape[0]):
        extra_ref[c] = extra_rows(gram_ref[c * each : (c + 1) * each, :])
    width = theirs_slab_ref.shape[1] // 2
    for j in range(width // TILE):
        at = span(me_ref[0] * width + j * TILE, TILE)
        product = dot(mine, mine_slab_ref[:, at], 1, 0) + dot(other, theirs_slab_ref[:, at], 1, 0)
        put_chunks(owned_ref, j, product)


def join_chunks_kernel(owned_ref, got_ref, extra_ref, out_ref):
    rank = owned_ref.shape[1]
    for c in range(out_ref.shape[0]):
        out_ref[c, :rank, :] = (owned_ref[c] + got_ref[c].astype(F32)).astype(BF16)
        out_ref[c, rank:, :] = extra_ref[c]


def sum_chunks_kernel(parts_ref, out_ref):
    n = parts_ref.shape[0]
    rank = parts_ref.shape[1] - EXTRA
    total = parts_ref[0].astype(F32)
    for c in range(1, n):
        total = total + parts_ref[c].astype(F32)
    extra = extra_rows(from_extra(total[rank:], rank // n))
    piece = jnp.concatenate([total[:rank].astype(BF16), extra], axis=0)
    for c in range(n):
        out_ref[c] = piece


def add_rows(columns, core, acc_ref, slab_ref, out_ref):
    at = span(core * columns.shape[1], columns.shape[1])
    for t in range(0, out_ref.shape[1], WIDE):
        product = dot(slab_ref[t : t + WIDE, at], columns, 1, 1).T
        if acc_ref is not None:
            product = acc_ref[:, t : t + WIDE] + product
        out_ref[:, t : t + WIDE] = product.astype(out_ref.dtype)


def rows_own_kernel(
    me_ref, own_ref, theirs_slab_ref, mine_slab_ref,
    factor_ref, theirs_ref, mine_ref, gram_ref, columns_ref, half_ref,
):
    rank = gram_ref.shape[0]
    factor3 = stacked(inverse_factor(gathered_gram(own_ref, rank)), 1)
    factor_ref[...] = factor3
    total = jnp.zeros((3 * rank, 3 * rank), F32)
    for at, block in blocks_of(own_ref, rank):
        columns = applied(factor3, block)
        columns_ref[:, at] = columns
        half_ref[:, at] = columns.astype(BF16)
        total = total + gram_of(columns_ref, at)
    gram_ref[...] = folded(total, rank)
    half = half_ref[...]
    add_rows(half, me_ref[0], None, theirs_slab_ref, theirs_ref)
    add_rows(half, me_ref[0], None, mine_slab_ref, mine_ref)


def rows_theirs_kernel(
    me_ref, other_ref, factor_ref, acc_ref, slab_ref, theirs_ref, columns_ref, half_ref
):
    factor3 = factor_ref[...]
    for at, block in blocks_of(other_ref, factor3.shape[0]):
        columns = applied(factor3, block)
        columns_ref[:, at] = columns
        half_ref[:, at] = columns.astype(BF16)
    add_rows(half_ref[...], 1 - me_ref[0], acc_ref, slab_ref, theirs_ref)


def rows_mine_kernel(
    me_ref, half_ref, columns_ref, gram_own_ref, acc_ref, slab_ref, mine_ref, pack_ref
):
    rank, width = columns_ref.shape
    total = jnp.zeros((3 * rank, 3 * rank), F32)
    for t in range(0, width, TILE):
        total = total + gram_of(columns_ref, slice(t, t + TILE))
    gram = gram_own_ref[...] + folded(total, rank)
    gram = jnp.concatenate([gram[: rank // 2], gram[rank // 2 :]], axis=1)
    pack_ref[...] = jnp.zeros_like(pack_ref)
    pack_ref[:, : 3 * LANE] = stacked(gram, 1)
    add_rows(half_ref[...], 1 - me_ref[0], acc_ref, slab_ref, mine_ref)


def join_rows_kernel(mine_ref, got_ref, pack_ref, out_ref):
    rank = mine_ref.shape[0]
    out_ref[:rank, :] = (mine_ref[...] + got_ref[...].astype(F32)).astype(BF16)
    out_ref[rank:, :] = pack_ref[...]


def sum_packed_kernel(a_ref, b_ref, c_ref, d_ref, rows_ref, gram_ref):
    total = (a_ref[...].astype(F32) + b_ref[...].astype(F32)) + (
        c_ref[...].astype(F32) + d_ref[...].astype(F32)
    )
    rank = rows_ref.shape[0]
    rows_ref[...] = total[:rank].astype(BF16)
    e = total[rank:]
    g = e[:, :LANE] + e[:, LANE : 2 * LANE] + e[:, 2 * LANE : 3 * LANE]
    gram_ref[...] = jnp.concatenate([g[:, :rank], g[:, rank:]], axis=0)


def final_own_kernel(
    scale, me_ref, own_ref, rows_mine_ref, rows_other_ref,
    factor_ref, columns_ref, gram_ref, left_ref,
):
    me = me_ref[0]
    rank, half = rows_mine_ref.shape
    factor3 = stacked(inverse_factor(gathered_gram(own_ref, rank)), 1)
    factor_ref[...] = factor3
    for core, ref in ((me, rows_mine_ref), (1 - me, rows_other_ref)):
        left = applied(factor3, ref[...]).astype(BF16)
        left_ref[:, span(core * half, half)] = (left.astype(F32) * scale).astype(BF16)
    gram_ref[...] = keep_columns(factor3, own_ref, columns_ref)


def keep_columns(factor3, chunks_ref, columns_ref):
    rank = factor3.shape[0]
    total = jnp.zeros((3 * rank, 3 * rank), F32)
    for at, block in blocks_of(chunks_ref, rank):
        columns = applied(factor3, block)
        columns_ref[:, at] = columns
        three = stacked(columns)
        total = total + dot(three, three, 1, 1)
    return folded(total, rank)


def final_other_kernel(other_ref, factor_ref, gram_own_ref, columns_ref, gram_ref):
    gram_ref[...] = gram_own_ref[...] + keep_columns(factor_ref[...], other_ref, columns_ref)


def update_pieces(pieces, left, first_ref, second_ref, outs, buffers, sems):
    corr_one = 1.0 - 0.9**10
    corr_two = 1.0 - 0.999**10
    update_ref, new_first_ref, new_second_ref = buffers
    copies = []
    for i, (base, columns_ref, start) in enumerate(pieces):
        for t in range(0, PIECE, TILE):
            at = span(base + start + t, TILE)
            columns = columns_ref[:, start + t : start + t + TILE]
            new_first = 0.9 * first_ref[:, at] + 0.1 * columns
            new_second = 0.999 * second_ref[:, at] + 0.001 * columns * columns
            here = slice(i * PIECE + t, i * PIECE + t + TILE)
            new_first_ref[:, here] = new_first
            new_second_ref[:, here] = new_second
            direction = new_first / corr_one / (jnp.sqrt(new_second / corr_two) + 1e-08)
            update_ref[:, here] = dot(left, direction.astype(BF16), 1, 0).astype(BF16)
        here = slice(i * PIECE, (i + 1) * PIECE)
        for j, (ref, hbm) in enumerate(zip(buffers, outs)):
            copy = pltpu.make_async_copy(
                ref.at[:, here], hbm.at[:, span(base + start, PIECE)], sems.at[3 * i + j]
            )
            copy.start()
            copies.append(copy)
    return copies


def update_most_kernel(me_ref, own_ref, other_ref, left_ref, first_ref, second_ref, *refs):
    outs, turned_ref, buffers, sems = refs[:3], refs[3], refs[4:7], refs[7]
    me = me_ref[0]
    width = own_ref.shape[1]
    left = left_ref[...].T
    turned_ref[...] = left
    pieces = [(me * width, own_ref, t) for t in range(0, width, PIECE)]
    pieces += [((1 - me) * width, other_ref, t) for t in range(0, width - PIECE, PIECE)]
    for copy in update_pieces(pieces, left, first_ref, second_ref, outs, buffers, sems):
        copy.wait()


def update_last_kernel(
    me_ref, own_ref, other_ref, turned_ref, first_ref, second_ref, a_ref, b_ref, c_ref, d_ref, *refs
):
    me = me_ref[0]
    outs, basis_hbm, buffers, basis_ref, sems = refs[3:6], refs[6], refs[7:10], refs[10], refs[11]
    width = own_ref.shape[1]
    pieces = [((1 - me) * width, other_ref, width - PIECE)]
    copies = update_pieces(
        pieces, turned_ref[...], first_ref, second_ref, outs, buffers, sems
    )
    factor = inverse_factor((a_ref[...] + b_ref[...]) + (c_ref[...] + d_ref[...]))
    high, mid, _ = thirds(factor)
    wide = jnp.concatenate([high, high, mid], axis=1).astype(BF16)
    for i, (core, ref) in enumerate(((me, own_ref), (1 - me, other_ref))):
        for t in range(0, width, TILE):
            high, mid, _ = thirds(ref[:, t : t + TILE])
            tall = jnp.concatenate([high, mid, high], axis=0).astype(BF16)
            basis_ref[:, i * width + t : i * width + t + TILE] = dot(wide, tall, 1, 0)
        copy = pltpu.make_async_copy(
            basis_ref.at[:, i * width : (i + 1) * width],
            basis_hbm.at[:, span(core * width, width)],
            sems.at[3 + i],
        )
        copy.start()
        copies.append(copy)
    for copy in copies:
        copy.wait()


def call(kernel, outs, operands, scratch=(), hbm=(), hbm_out=(), aliases=None):
    def spec(i, x):
        if x.dtype == jnp.int32:
            return SMEM
        return pl.BlockSpec(memory_space=pl.ANY) if i in hbm else VMEM

    moved = sum(x.size * x.dtype.itemsize for x in operands)
    return pl.pallas_call(
        kernel,
        out_shape=[jax.ShapeDtypeStruct(s, t) for s, t in outs],
        in_specs=[spec(i, x) for i, x in enumerate(operands)],
        out_specs=[
            pl.BlockSpec(memory_space=pl.ANY) if i in hbm_out else VMEM for i in range(len(outs))
        ],
        input_output_aliases=aliases or {},
        scratch_shapes=[pltpu.VMEM(*s) if isinstance(s, tuple) else s for s in scratch],
        compiler_params=pltpu.CompilerParams(vmem_limit_bytes=VMEM_LIMIT),
        cost_estimate=pl.CostEstimate(flops=64 * moved, bytes_accessed=moved, transcendentals=0),
    )(*operands)


def swapped(x):
    return lax.ppermute(x, "dp", [(0, 1), (1, 0)])


def others(x):
    n = lax.axis_size("mp")
    return [lax.ppermute(x, "mp", [(i, (i + k) % n) for i in range(n)]) for k in (1, 3, 2)]


def columns_of(me, mine, slabs, owners, gram=None):
    theirs_slab, mine_slab = slabs
    rank, half = mine.shape
    width = mine_slab.shape[1]
    orthogonal = gram is not None
    square = ((rank, rank), F32)
    acc = ((rank, width // 2), F32)
    halves = ((rank, half), BF16)
    chunk = (owners, rank, LANE)
    whole = [((owners, rank + EXTRA, LANE), BF16)]

    other = swapped(mine)
    if orthogonal:
        outs = [acc, square, ((rank, 3 * rank), BF16), halves]
        operands = [me, mine, gram, mine_slab]
    else:
        outs = [acc, square]
        operands = [me, mine, mine_slab]
    acc, gram_mine, *rest = call(functools.partial(columns_mine_kernel, orthogonal), outs, operands)
    if orthogonal:
        factor, mine = rest
        theirs, other = call(
            functools.partial(columns_theirs_kernel, True),
            [(chunk, BF16), halves],
            [me, other, acc, theirs_slab, factor],
        )
    else:
        theirs = call(
            functools.partial(columns_theirs_kernel, False),
            [(chunk, BF16)],
            [me, other, acc, theirs_slab],
        )[0]
    got = swapped(theirs)
    owned, extra = call(
        columns_owned_kernel,
        [(chunk, F32), ((owners, EXTRA, LANE), BF16)],
        [me, mine, other, theirs_slab, mine_slab, gram_mine],
        [((rank, LANE), F32)],
    )
    chunks = call(join_chunks_kernel, whole, [owned, got, extra])[0]
    parts = lax.all_to_all(chunks, "vocab", 0, 0)
    copies = call(sum_chunks_kernel, whole, [parts])[0]
    own = lax.all_to_all(copies, "vocab", 0, 0)
    return own, swapped(own), mine, other


def local(grad_parts, old_basis, first_moment, second_moment):
    slab = grad_parts[0]
    vocab, width = slab.shape
    rank = old_basis.shape[0]
    half = vocab // 2
    owners = lax.axis_size("vocab")
    me = lax.axis_index("dp").astype(jnp.int32).reshape(1)
    theirs_out, mine_out = ((rank, half), BF16), ((rank, half), F32)
    wide = ((rank, width), F32)
    narrow = ((rank, width // 2), F32)
    square = ((rank, rank), F32)
    factor_out = ((rank, 3 * rank), BF16)
    half_slab = ((half, width), BF16)

    slab, basis = (pltpu.with_memory_space_constraint(x, pltpu.HBM) for x in (slab, old_basis))
    theirs, left, theirs_slab, mine_slab = call(
        first_theirs_kernel,
        [theirs_out, ((rank, width), BF16), half_slab, half_slab],
        [me, basis, slab],
        [((rank, width), F32), pltpu.SemaphoreType.DMA((1 + vocab // WIDE,))],
        hbm=(1, 2),
    )
    got = swapped(theirs)
    mine = call(first_mine_kernel, [mine_out], [left, mine_slab])[0]
    slabs = (theirs_slab, mine_slab)
    mine = (mine + got.astype(F32)).astype(BF16)
    total = mine.astype(F32)
    for x in others(mine):
        total = total + x.astype(F32)
    own, other, _, _ = columns_of(me, total.astype(BF16), slabs, owners)

    factor, theirs_acc, mine_acc, gram = call(
        rows_own_kernel,
        [factor_out, mine_out, mine_out, square],
        [me, own, theirs_slab, mine_slab],
        [narrow, ((rank, width // 2), BF16)],
    )
    theirs, columns, columns_half = call(
        rows_theirs_kernel,
        [theirs_out, narrow, ((rank, width // 2), BF16)],
        [me, other, factor, theirs_acc, theirs_slab],
    )
    got = swapped(theirs)
    mine, pack = call(
        rows_mine_kernel,
        [mine_out, ((rank // 2, half), BF16)],
        [me, columns_half, columns, gram, mine_acc, mine_slab],
    )
    mine = call(join_rows_kernel, [((rank + rank // 2, half), BF16)], [mine, got, pack])[0]
    mine, gram = call(sum_packed_kernel, [theirs_out, square], [mine, *others(mine)])
    own, other, rows_mine, rows_other = columns_of(me, mine, slabs, owners, gram)

    scale = math.sqrt(vocab * owners)
    assert scale == 2.0 ** round(math.log2(scale))
    factor, columns_own, gram, left = call(
        functools.partial(final_own_kernel, scale),
        [factor_out, narrow, square, ((rank, vocab), BF16)],
        [me, own, rows_mine, rows_other],
    )
    columns_other, gram = call(final_other_kernel, [narrow, square], [other, factor, gram])
    gram_others = others(gram)
    outs = [((vocab, width), BF16), wide, wide]

    def buffers(columns):
        return [((vocab, columns), BF16), ((rank, columns), F32), ((rank, columns), F32)]

    *begun, turned = call(
        update_most_kernel,
        outs + [((vocab, rank), BF16)],
        [me, columns_own, columns_other, left, first_moment, second_moment],
        buffers(width - PIECE) + [pltpu.SemaphoreType.DMA((3 * (width // PIECE - 1),))],
        hbm_out=(0, 1, 2),
    )
    operands = [me, columns_own, columns_other, turned, first_moment, second_moment]
    operands += [gram, *gram_others]
    n = len(operands)
    update, new_first, new_second, basis = call(
        update_last_kernel,
        outs + [wide],
        operands + begun,
        buffers(PIECE) + [wide, pltpu.SemaphoreType.DMA((5,))],
        hbm=(n, n + 1, n + 2),
        hbm_out=(0, 1, 2, 3),
        aliases={n: 0, n + 1: 1, n + 2: 2},
    )
    return (update, basis, new_first, new_second)


def solution(mesh):
    placed = (P("dp", "vocab", "mp"), P(None, "mp"), P(None, "mp"), P(None, "mp"))
    return jax.shard_map(
        local,
        mesh=mesh,
        in_specs=placed,
        out_specs=(P("vocab", "mp"), P(None, "mp"), P(None, "mp"), P(None, "mp")),
        check_vma=False,
    )
```

```python
import functools
import math

import jax
import jax.numpy as jnp
from jax import lax
from jax.experimental import pallas as pl
from jax.experimental.pallas import tpu as pltpu
from jax.sharding import PartitionSpec as P

F32 = jnp.float32
BF16 = jnp.bfloat16
LANE = 128
EXTRA = 16
TILE = 512
WIDE = 256
PIECE = 1024
PANEL = 16
VMEM_LIMIT = 28 * 1024 * 1024

VMEM = pl.BlockSpec(memory_space=pltpu.VMEM)
SMEM = pl.BlockSpec(memory_space=pltpu.SMEM)


def thirds(value):
    high = value.astype(BF16).astype(F32)
    rest = value - high
    mid = rest.astype(BF16).astype(F32)
    return high, mid, rest - mid


def stacked(value, axis=0):
    return jnp.concatenate(thirds(value), axis=axis).astype(BF16)


def dot(a, b, ca, cb):
    return lax.dot_general(a, b, (((ca,), (cb,)), ((), ())), preferred_element_type=F32)


def inverse_factor(gram):
    rank = gram.shape[0]
    lanes = lax.broadcasted_iota(jnp.int32, (8, rank), 1)
    subs = lax.broadcasted_iota(jnp.int32, (8, LANE), 0)
    blocks = rank // 8
    both = []
    for b in range(blocks):
        eye = jnp.where(lanes == subs[:, :rank] + 8 * b, 1.0, 0.0).astype(F32)
        both.append(jnp.concatenate([gram[8 * b : 8 * b + 8, :], eye], axis=1))
    scale = []
    for b0 in range(0, blocks, PANEL // 8):
        diags = [jnp.ones((8, LANE), F32)] * (PANEL // 8)
        cols = {
            (j, i): jnp.broadcast_to(both[i][:, 8 * b0 + j : 8 * b0 + j + 1], (8, LANE))
            for j in range(PANEL)
            for i in range(b0, blocks)
        }
        for j in range(PANEL):
            b, s = b0 + j // 8, j % 8
            pivot = cols[j, b][s : s + 1, :]
            inverse = 1.0 / pivot
            diags[j // 8] = jnp.where(subs == s, pivot, diags[j // 8])
            row = both[b][s : s + 1, :] * inverse
            heads = {m: cols[m, b][s : s + 1, :] * inverse for m in range(j + 1, PANEL)}
            for i in range(b, blocks):
                f = cols[j, i]
                if i == b:
                    f = jnp.where(subs > s, f, 0.0)
                both[i] = both[i] - f * row
                for m in range(j + 1, PANEL):
                    cols[m, i] = cols[m, i] - f * heads[m]
        scale.extend(lax.rsqrt(d) for d in diags)
    return jnp.concatenate(
        [both[b][:, rank:] * scale[b][:, :rank] for b in range(blocks)], axis=0
    )


def applied(factor3, block):
    return dot(factor3, jnp.concatenate([block] * 3, axis=0), 1, 0)


def folded(total, rank):
    wide = total[:rank] + total[rank : 2 * rank] + total[2 * rank :]
    return wide[:, :rank] + wide[:, rank : 2 * rank] + wide[:, 2 * rank :]


def span(base, size):
    return pl.ds(pl.multiple_of(base, size), size)


def extra_rows(piece):
    pad = jnp.zeros((EXTRA - 3 * piece.shape[0], piece.shape[1]), F32)
    return jnp.concatenate([*thirds(piece), pad], axis=0).astype(BF16)


def from_extra(e, each):
    return e[:each] + e[each : 2 * each] + e[2 * each : 3 * each]


def gathered_gram(chunks_ref, rank):
    n = chunks_ref.shape[0]
    pieces = [
        from_extra(chunks_ref[c, rank : rank + EXTRA, :].astype(F32), rank // n) for c in range(n)
    ]
    return jnp.concatenate(pieces, axis=0)[:, :rank]


def blocks_of(chunks_ref, rank):
    per = TILE // LANE
    for j in range(chunks_ref.shape[0] // per):
        block = jnp.concatenate([chunks_ref[j * per + q, :rank, :] for q in range(per)], axis=1)
        yield slice(j * TILE, (j + 1) * TILE), block


def gram_of(columns_ref, at):
    three = stacked(columns_ref[:, at])
    return dot(three, three, 1, 1)


def first_theirs_kernel(
    me_ref, basis_hbm, slab_hbm, theirs_ref, left_ref, theirs_slab_ref, mine_slab_ref, basis_ref, sems
):
    me = me_ref[0]
    half = theirs_slab_ref.shape[0]
    basis_copy = pltpu.make_async_copy(basis_hbm, basis_ref, sems.at[0])
    theirs_copies, mine_copies = (
        [
            pltpu.make_async_copy(
                slab_hbm.at[span(core * half + t, WIDE), :],
                ref.at[t : t + WIDE, :],
                sems.at[first + t // WIDE],
            )
            for t in range(0, half, WIDE)
        ]
        for core, ref, first in (
            (1 - me, theirs_slab_ref, 1),
            (me, mine_slab_ref, 1 + half // WIDE),
        )
    )
    for copy in (basis_copy, *theirs_copies):
        copy.start()
    basis_copy.wait()
    for copy in mine_copies:
        copy.start()
    left = basis_ref[...].astype(BF16)
    left_ref[...] = left
    for copy in theirs_copies:
        copy.wait()
    for t in range(0, half, WIDE):
        at = slice(t, t + WIDE)
        theirs_ref[:, at] = dot(theirs_slab_ref[at, :], left, 1, 1).T.astype(BF16)
    for copy in mine_copies:
        copy.wait()


def first_mine_kernel(left_ref, slab_ref, mine_ref):
    left = left_ref[...]
    for t in range(0, mine_ref.shape[1], WIDE):
        mine_ref[:, t : t + WIDE] = dot(slab_ref[t : t + WIDE, :], left, 1, 1).T


def columns_mine_kernel(orthogonal, *refs):
    if orthogonal:
        me_ref, mine_ref, gram_in_ref, slab_ref, acc_ref, gram_ref, factor_ref, rows_ref = refs
        factor3 = stacked(inverse_factor(gram_in_ref[...]), 1)
        factor_ref[...] = factor3
        mine = applied(factor3, mine_ref[...]).astype(BF16)
        rows_ref[...] = mine
    else:
        me_ref, mine_ref, slab_ref, acc_ref, gram_ref = refs
        mine = mine_ref[...]
    gram_ref[...] = dot(mine, mine, 1, 1)
    width = acc_ref.shape[1]
    for t in range(0, width, TILE):
        at = span((1 - me_ref[0]) * width + t, TILE)
        acc_ref[:, t : t + TILE] = dot(mine, slab_ref[:, at], 1, 0)


def put_chunks(out_ref, j, product):
    per = TILE // LANE
    product = product.astype(out_ref.dtype)
    for q in range(per):
        out_ref[j * per + q] = product[:, q * LANE : (q + 1) * LANE]


def columns_theirs_kernel(orthogonal, *refs):
    if orthogonal:
        me_ref, other_ref, acc_ref, slab_ref, factor_ref, theirs_ref, rows_ref = refs
        other = applied(factor_ref[...], other_ref[...]).astype(BF16)
        rows_ref[...] = other
    else:
        me_ref, other_ref, acc_ref, slab_ref, theirs_ref = refs
        other = other_ref[...]
    width = acc_ref.shape[1]
    for j in range(width // TILE):
        at = span((1 - me_ref[0]) * width + j * TILE, TILE)
        product = acc_ref[:, j * TILE : (j + 1) * TILE] + dot(other, slab_ref[:, at], 1, 0)
        put_chunks(theirs_ref, j, product)


def columns_owned_kernel(
    me_ref, mine_ref, other_ref, theirs_slab_ref, mine_slab_ref, gram_mine_ref,
    owned_ref, extra_ref, gram_ref,
):
    mine, other = mine_ref[...], other_ref[...]
    rank = other.shape[0]
    gram_ref[...] = jnp.zeros_like(gram_ref)
    gram_ref[:, :rank] = gram_mine_ref[...] + dot(other, other, 1, 1)
    each = rank // extra_ref.shape[0]
    for c in range(extra_ref.shape[0]):
        extra_ref[c] = extra_rows(gram_ref[c * each : (c + 1) * each, :])
    width = theirs_slab_ref.shape[1] // 2
    for j in range(width // TILE):
        at = span(me_ref[0] * width + j * TILE, TILE)
        product = dot(mine, mine_slab_ref[:, at], 1, 0) + dot(other, theirs_slab_ref[:, at], 1, 0)
        put_chunks(owned_ref, j, product)


def join_chunks_kernel(owned_ref, got_ref, extra_ref, out_ref):
    rank = owned_ref.shape[1]
    for c in range(out_ref.shape[0]):
        out_ref[c, :rank, :] = (owned_ref[c] + got_ref[c].astype(F32)).astype(BF16)
        out_ref[c, rank:, :] = extra_ref[c]


def sum_chunks_kernel(parts_ref, out_ref):
    n = parts_ref.shape[0]
    rank = parts_ref.shape[1] - EXTRA
    total = parts_ref[0].astype(F32)
    for c in range(1, n):
        total = total + parts_ref[c].astype(F32)
    extra = extra_rows(from_extra(total[rank:], rank // n))
    piece = jnp.concatenate([total[:rank].astype(BF16), extra], axis=0)
    for c in range(n):
        out_ref[c] = piece


def add_rows(columns, core, acc_ref, slab_ref, out_ref):
    at = span(core * columns.shape[1], columns.shape[1])
    for t in range(0, out_ref.shape[1], WIDE):
        product = dot(slab_ref[t : t + WIDE, at], columns, 1, 1).T
        if acc_ref is not None:
            product = acc_ref[:, t : t + WIDE] + product
        out_ref[:, t : t + WIDE] = product.astype(out_ref.dtype)


def rows_own_kernel(
    me_ref, own_ref, theirs_slab_ref, mine_slab_ref,
    factor_ref, theirs_ref, mine_ref, gram_ref, columns_ref, half_ref,
):
    rank = gram_ref.shape[0]
    factor3 = stacked(inverse_factor(gathered_gram(own_ref, rank)), 1)
    factor_ref[...] = factor3
    total = jnp.zeros((3 * rank, 3 * rank), F32)
    for at, block in blocks_of(own_ref, rank):
        columns = applied(factor3, block)
        columns_ref[:, at] = columns
        half_ref[:, at] = columns.astype(BF16)
        total = total + gram_of(columns_ref, at)
    gram_ref[...] = folded(total, rank)
    half = half_ref[...]
    add_rows(half, me_ref[0], None, theirs_slab_ref, theirs_ref)
    add_rows(half, me_ref[0], None, mine_slab_ref, mine_ref)


def rows_theirs_kernel(
    me_ref, other_ref, factor_ref, acc_ref, slab_ref, theirs_ref, columns_ref, half_ref
):
    factor3 = factor_ref[...]
    for at, block in blocks_of(other_ref, factor3.shape[0]):
        columns = applied(factor3, block)
        columns_ref[:, at] = columns
        half_ref[:, at] = columns.astype(BF16)
    add_rows(half_ref[...], 1 - me_ref[0], acc_ref, slab_ref, theirs_ref)


def rows_mine_kernel(
    me_ref, half_ref, columns_ref, gram_own_ref, acc_ref, slab_ref, mine_ref, pack_ref
):
    rank, width = columns_ref.shape
    total = jnp.zeros((3 * rank, 3 * rank), F32)
    for t in range(0, width, TILE):
        total = total + gram_of(columns_ref, slice(t, t + TILE))
    gram = gram_own_ref[...] + folded(total, rank)
    pack_ref[...] = packed_gram(gram).astype(BF16)
    add_rows(half_ref[...], 1 - me_ref[0], acc_ref, slab_ref, mine_ref)


def square_places(size):
    return (lax.broadcasted_iota(jnp.int32, (size, size), i) for i in range(2))


def packed_gram(gram):
    size = gram.shape[0] // 2
    row, column = square_places(size)
    low, corner = gram[size:, :size], gram[size:, size:]
    mixed = jnp.where(row >= column, gram[:size, :size], corner)
    diagonal = jnp.sum(jnp.where(row == column, corner, 0.0), axis=1, keepdims=True)
    lanes = lax.broadcasted_iota(jnp.int32, (size, 2 * size), 1)
    tail = jnp.zeros((size, 2 * size), F32)
    for i, part in enumerate(thirds(diagonal)):
        tail = jnp.where(lanes == i, part, tail)
    full = jnp.concatenate([*thirds(jnp.concatenate([low, mixed], axis=1)), tail], axis=1)
    return jnp.concatenate([full[: size // 2], full[size // 2 :]], axis=1)


def unpacked_gram(e, rank):
    size = rank // 2
    row, column = square_places(size)
    full = jnp.concatenate([e[:, : 4 * rank], e[:, 4 * rank :]], axis=0)
    both = full[:, :rank] + full[:, rank : 2 * rank] + full[:, 2 * rank : 3 * rank]
    tail = full[:, 3 * rank :]
    diagonal = tail[:, 0:1] + tail[:, 1:2] + tail[:, 2:3]
    turned = both.T
    low, mixed = both[:, :size], both[:, size:]
    first = jnp.where(row >= column, mixed, turned[size:])
    corner = jnp.where(row < column, mixed, jnp.where(row > column, turned[size:], diagonal))
    return jnp.concatenate(
        [jnp.concatenate([first, turned[:size]], axis=1), jnp.concatenate([low, corner], axis=1)],
        axis=0,
    )


def join_rows_kernel(mine_ref, got_ref, pack_ref, out_ref):
    rank = mine_ref.shape[0]
    out_ref[:rank, :] = (mine_ref[...] + got_ref[...].astype(F32)).astype(BF16)
    out_ref[rank:, :] = pack_ref[...]


def sum_packed_kernel(a_ref, b_ref, c_ref, d_ref, rows_ref, gram_ref):
    total = (a_ref[...].astype(F32) + b_ref[...].astype(F32)) + (
        c_ref[...].astype(F32) + d_ref[...].astype(F32)
    )
    rank = rows_ref.shape[0]
    rows_ref[...] = total[:rank].astype(BF16)
    gram_ref[...] = unpacked_gram(total[rank:], rank)


def final_own_kernel(
    scale, me_ref, own_ref, rows_mine_ref, rows_other_ref,
    factor_ref, columns_ref, gram_ref, left_ref,
):
    me = me_ref[0]
    rank, half = rows_mine_ref.shape
    factor3 = stacked(inverse_factor(gathered_gram(own_ref, rank)), 1)
    factor_ref[...] = factor3
    for core, ref in ((me, rows_mine_ref), (1 - me, rows_other_ref)):
        left = applied(factor3, ref[...]).astype(BF16)
        left_ref[:, span(core * half, half)] = (left.astype(F32) * scale).astype(BF16)
    gram_ref[...] = keep_columns(factor3, own_ref, columns_ref)


def keep_columns(factor3, chunks_ref, columns_ref):
    rank = factor3.shape[0]
    total = jnp.zeros((3 * rank, 3 * rank), F32)
    for at, block in blocks_of(chunks_ref, rank):
        columns = applied(factor3, block)
        columns_ref[:, at] = columns
        three = stacked(columns)
        total = total + dot(three, three, 1, 1)
    return folded(total, rank)


def final_other_kernel(other_ref, factor_ref, gram_own_ref, columns_ref, gram_ref):
    gram_ref[...] = gram_own_ref[...] + keep_columns(factor_ref[...], other_ref, columns_ref)


def update_pieces(pieces, left, first_ref, second_ref, outs, buffers, sems):
    corr_one = 1.0 - 0.9**10
    corr_two = 1.0 - 0.999**10
    update_ref, new_first_ref, new_second_ref = buffers
    copies = []
    put = 0
    for i, (base, columns_ref, start, size) in enumerate(pieces):
        for t in range(0, size, TILE):
            at = span(base + start + t, TILE)
            columns = columns_ref[:, start + t : start + t + TILE]
            new_first = 0.9 * first_ref[:, at] + 0.1 * columns
            new_second = 0.999 * second_ref[:, at] + 0.001 * columns * columns
            here = slice(put + t, put + t + TILE)
            new_first_ref[:, here] = new_first
            new_second_ref[:, here] = new_second
            direction = new_first / corr_one / (jnp.sqrt(new_second / corr_two) + 1e-08)
            update_ref[:, here] = dot(left, direction.astype(BF16), 1, 0).astype(BF16)
        here = slice(put, put + size)
        put += size
        for j, (ref, hbm) in enumerate(zip(buffers, outs)):
            copy = pltpu.make_async_copy(
                ref.at[:, here], hbm.at[:, piece_at(base + start, size)], sems.at[3 * i + j]
            )
            copy.start()
            copies.append(copy)
    return copies


def piece_at(base, size):
    return pl.ds(pl.multiple_of(base, TILE), size)


def cuts(width):
    start = 0
    while start < width:
        size = PIECE if width - start > PIECE else TILE
        yield start, size
        start += size


def update_kernel(me_ref, own_ref, other_ref, left_ref, first_ref, second_ref, *refs):
    outs, buffers, sems = refs[:3], refs[3:6], refs[6]
    me = me_ref[0]
    width = own_ref.shape[1]
    left = left_ref[...].T
    pieces = [(me * width, own_ref, t, PIECE) for t in range(0, width, PIECE)]
    pieces += [((1 - me) * width, other_ref, t, size) for t, size in cuts(width)]
    for copy in update_pieces(pieces, left, first_ref, second_ref, outs, buffers, sems):
        copy.wait()


def basis_kernel(me_ref, own_ref, other_ref, a_ref, b_ref, c_ref, d_ref, basis_hbm, basis_ref, sems):
    me = me_ref[0]
    width = own_ref.shape[1]
    factor = inverse_factor((a_ref[...] + b_ref[...]) + (c_ref[...] + d_ref[...]))
    high, mid, _ = thirds(factor)
    wide = jnp.concatenate([high, high, mid], axis=1).astype(BF16)
    copies = []
    for i, (core, ref) in enumerate(((me, own_ref), (1 - me, other_ref))):
        for t in range(0, width, TILE):
            high, mid, _ = thirds(ref[:, t : t + TILE])
            tall = jnp.concatenate([high, mid, high], axis=0).astype(BF16)
            basis_ref[:, i * width + t : i * width + t + TILE] = dot(wide, tall, 1, 0)
        copy = pltpu.make_async_copy(
            basis_ref.at[:, i * width : (i + 1) * width],
            basis_hbm.at[:, span(core * width, width)],
            sems.at[i],
        )
        copy.start()
        copies.append(copy)
    for copy in copies:
        copy.wait()


def call(kernel, outs, operands, scratch=(), hbm=(), hbm_out=(), aliases=None):
    def spec(i, x):
        if x.dtype == jnp.int32:
            return SMEM
        return pl.BlockSpec(memory_space=pl.ANY) if i in hbm else VMEM

    moved = sum(x.size * x.dtype.itemsize for x in operands)
    return pl.pallas_call(
        kernel,
        out_shape=[jax.ShapeDtypeStruct(s, t) for s, t in outs],
        in_specs=[spec(i, x) for i, x in enumerate(operands)],
        out_specs=[
            pl.BlockSpec(memory_space=pl.ANY) if i in hbm_out else VMEM for i in range(len(outs))
        ],
        input_output_aliases=aliases or {},
        scratch_shapes=[pltpu.VMEM(*s) if isinstance(s, tuple) else s for s in scratch],
        compiler_params=pltpu.CompilerParams(vmem_limit_bytes=VMEM_LIMIT),
        cost_estimate=pl.CostEstimate(flops=64 * moved, bytes_accessed=moved, transcendentals=0),
    )(*operands)


def swapped(x):
    return lax.ppermute(x, "dp", [(0, 1), (1, 0)])


def others(x):
    n = lax.axis_size("mp")
    return [lax.ppermute(x, "mp", [(i, (i + k) % n) for i in range(n)]) for k in (1, 3, 2)]


def columns_of(me, mine, slabs, owners, gram=None):
    theirs_slab, mine_slab = slabs
    rank, half = mine.shape
    width = mine_slab.shape[1]
    orthogonal = gram is not None
    square = ((rank, rank), F32)
    acc = ((rank, width // 2), F32)
    halves = ((rank, half), BF16)
    chunk = (owners, rank, LANE)
    whole = [((owners, rank + EXTRA, LANE), BF16)]

    other = swapped(mine)
    if orthogonal:
        outs = [acc, square, ((rank, 3 * rank), BF16), halves]
        operands = [me, mine, gram, mine_slab]
    else:
        outs = [acc, square]
        operands = [me, mine, mine_slab]
    acc, gram_mine, *rest = call(functools.partial(columns_mine_kernel, orthogonal), outs, operands)
    if orthogonal:
        factor, mine = rest
        theirs, other = call(
            functools.partial(columns_theirs_kernel, True),
            [(chunk, BF16), halves],
            [me, other, acc, theirs_slab, factor],
        )
    else:
        theirs = call(
            functools.partial(columns_theirs_kernel, False),
            [(chunk, BF16)],
            [me, other, acc, theirs_slab],
        )[0]
    got = swapped(theirs)
    owned, extra = call(
        columns_owned_kernel,
        [(chunk, F32), ((owners, EXTRA, LANE), BF16)],
        [me, mine, other, theirs_slab, mine_slab, gram_mine],
        [((rank, LANE), F32)],
    )
    chunks = call(join_chunks_kernel, whole, [owned, got, extra])[0]
    parts = lax.all_to_all(chunks, "vocab", 0, 0)
    copies = call(sum_chunks_kernel, whole, [parts])[0]
    own = lax.all_to_all(copies, "vocab", 0, 0)
    return own, swapped(own), mine, other


def local(grad_parts, old_basis, first_moment, second_moment):
    slab = grad_parts[0]
    vocab, width = slab.shape
    rank = old_basis.shape[0]
    half = vocab // 2
    owners = lax.axis_size("vocab")
    me = lax.axis_index("dp").astype(jnp.int32).reshape(1)
    theirs_out, mine_out = ((rank, half), BF16), ((rank, half), F32)
    wide = ((rank, width), F32)
    narrow = ((rank, width // 2), F32)
    square = ((rank, rank), F32)
    factor_out = ((rank, 3 * rank), BF16)
    half_slab = ((half, width), BF16)

    slab, basis = (pltpu.with_memory_space_constraint(x, pltpu.HBM) for x in (slab, old_basis))
    theirs, left, theirs_slab, mine_slab = call(
        first_theirs_kernel,
        [theirs_out, ((rank, width), BF16), half_slab, half_slab],
        [me, basis, slab],
        [((rank, width), F32), pltpu.SemaphoreType.DMA((1 + vocab // WIDE,))],
        hbm=(1, 2),
    )
    got = swapped(theirs)
    mine = call(first_mine_kernel, [mine_out], [left, mine_slab])[0]
    slabs = (theirs_slab, mine_slab)
    mine = (mine + got.astype(F32)).astype(BF16)
    total = mine.astype(F32)
    for x in others(mine):
        total = total + x.astype(F32)
    own, other, _, _ = columns_of(me, total.astype(BF16), slabs, owners)

    factor, theirs_acc, mine_acc, gram = call(
        rows_own_kernel,
        [factor_out, mine_out, mine_out, square],
        [me, own, theirs_slab, mine_slab],
        [narrow, ((rank, width // 2), BF16)],
    )
    theirs, columns, columns_half = call(
        rows_theirs_kernel,
        [theirs_out, narrow, ((rank, width // 2), BF16)],
        [me, other, factor, theirs_acc, theirs_slab],
    )
    got = swapped(theirs)
    mine, pack = call(
        rows_mine_kernel,
        [mine_out, ((EXTRA, half), BF16)],
        [me, columns_half, columns, gram, mine_acc, mine_slab],
    )
    mine = call(join_rows_kernel, [((rank + EXTRA, half), BF16)], [mine, got, pack])[0]
    mine, gram = call(sum_packed_kernel, [theirs_out, square], [mine, *others(mine)])
    own, other, rows_mine, rows_other = columns_of(me, mine, slabs, owners, gram)

    scale = math.sqrt(vocab * owners)
    assert scale == 2.0 ** round(math.log2(scale))
    factor, columns_own, gram, left = call(
        functools.partial(final_own_kernel, scale),
        [factor_out, narrow, square, ((rank, vocab), BF16)],
        [me, own, rows_mine, rows_other],
    )
    columns_other, gram = call(final_other_kernel, [narrow, square], [other, factor, gram])
    gram_others = others(gram)
    outs = [((vocab, width), BF16), wide, wide]

    def buffers(columns):
        return [((vocab, columns), BF16), ((rank, columns), F32), ((rank, columns), F32)]

    update, new_first, new_second = call(
        update_kernel,
        outs,
        [me, columns_own, columns_other, left, first_moment, second_moment],
        buffers(width) + [pltpu.SemaphoreType.DMA((3 * (width // TILE),))],
        hbm_out=(0, 1, 2),
    )
    basis = call(
        basis_kernel,
        [wide],
        [me, columns_own, columns_other, gram, *gram_others],
        [wide, pltpu.SemaphoreType.DMA((2,))],
        hbm_out=(0,),
    )[0]
    return (update, basis, new_first, new_second)


def solution(mesh):
    placed = (P("dp", "vocab", "mp"), P(None, "mp"), P(None, "mp"), P(None, "mp"))
    return jax.shard_map(
        local,
        mesh=mesh,
        in_specs=placed,
        out_specs=(P("vocab", "mp"), P(None, "mp"), P(None, "mp"), P(None, "mp")),
        check_vma=False,
    )
```

```python
import functools
import math

import jax
import jax.numpy as jnp
from jax import lax
from jax.experimental import pallas as pl
from jax.experimental.pallas import tpu as pltpu
from jax.sharding import PartitionSpec as P

F32 = jnp.float32
BF16 = jnp.bfloat16
LANE = 128
EXTRA = 16
TILE = 512
WIDE = 256
PIECE = 1024
PANEL = 16
VMEM_LIMIT = 28 * 1024 * 1024

VMEM = pl.BlockSpec(memory_space=pltpu.VMEM)
SMEM = pl.BlockSpec(memory_space=pltpu.SMEM)


def thirds(value):
    high = value.astype(BF16).astype(F32)
    rest = value - high
    mid = rest.astype(BF16).astype(F32)
    return high, mid, rest - mid


def stacked(value, axis=0):
    return jnp.concatenate(thirds(value), axis=axis).astype(BF16)


def dot(a, b, ca, cb):
    return lax.dot_general(a, b, (((ca,), (cb,)), ((), ())), preferred_element_type=F32)


def inverse_factor(gram):
    rank = gram.shape[0]
    lanes = lax.broadcasted_iota(jnp.int32, (8, rank), 1)
    subs = lax.broadcasted_iota(jnp.int32, (8, LANE), 0)
    blocks = rank // 8
    both = []
    for b in range(blocks):
        eye = jnp.where(lanes == subs[:, :rank] + 8 * b, 1.0, 0.0).astype(F32)
        both.append(jnp.concatenate([gram[8 * b : 8 * b + 8, :], eye], axis=1))
    scale = []
    for b0 in range(0, blocks, PANEL // 8):
        diags = [jnp.ones((8, LANE), F32)] * (PANEL // 8)
        cols = {
            (j, i): jnp.broadcast_to(both[i][:, 8 * b0 + j : 8 * b0 + j + 1], (8, LANE))
            for j in range(PANEL)
            for i in range(b0, blocks)
        }
        for j in range(PANEL):
            b, s = b0 + j // 8, j % 8
            pivot = cols[j, b][s : s + 1, :]
            inverse = 1.0 / pivot
            diags[j // 8] = jnp.where(subs == s, pivot, diags[j // 8])
            row = both[b][s : s + 1, :] * inverse
            heads = {m: cols[m, b][s : s + 1, :] * inverse for m in range(j + 1, PANEL)}
            for i in range(b, blocks):
                f = cols[j, i]
                if i == b:
                    f = jnp.where(subs > s, f, 0.0)
                both[i] = both[i] - f * row
                for m in range(j + 1, PANEL):
                    cols[m, i] = cols[m, i] - f * heads[m]
        scale.extend(lax.rsqrt(d) for d in diags)
    return jnp.concatenate(
        [both[b][:, rank:] * scale[b][:, :rank] for b in range(blocks)], axis=0
    )


def applied(factor3, block):
    return dot(factor3, jnp.concatenate([block] * 3, axis=0), 1, 0)


def folded(total, rank):
    wide = total[:rank] + total[rank : 2 * rank] + total[2 * rank :]
    return wide[:, :rank] + wide[:, rank : 2 * rank] + wide[:, 2 * rank :]


def span(base, size):
    return pl.ds(pl.multiple_of(base, size), size)


def extra_rows(piece):
    pad = jnp.zeros((EXTRA - 3 * piece.shape[0], piece.shape[1]), F32)
    return jnp.concatenate([*thirds(piece), pad], axis=0).astype(BF16)


def from_extra(e, each):
    return e[:each] + e[each : 2 * each] + e[2 * each : 3 * each]


def gathered_gram(chunks_ref, rank):
    n = chunks_ref.shape[0]
    pieces = [
        from_extra(chunks_ref[c, rank : rank + EXTRA, :].astype(F32), rank // n) for c in range(n)
    ]
    return jnp.concatenate(pieces, axis=0)[:, :rank]


def blocks_of(chunks_ref, rank):
    per = TILE // LANE
    for j in range(chunks_ref.shape[0] // per):
        block = jnp.concatenate([chunks_ref[j * per + q, :rank, :] for q in range(per)], axis=1)
        yield slice(j * TILE, (j + 1) * TILE), block


def gram_of(columns_ref, at):
    three = stacked(columns_ref[:, at])
    return dot(three, three, 1, 1)


def first_theirs_kernel(
    me_ref, basis_hbm, slab_hbm, theirs_ref, left_ref, theirs_slab_ref, mine_slab_ref, basis_ref, sems
):
    me = me_ref[0]
    half = theirs_slab_ref.shape[0]
    basis_copy = pltpu.make_async_copy(basis_hbm, basis_ref, sems.at[0])
    theirs_copies, mine_copies = (
        [
            pltpu.make_async_copy(
                slab_hbm.at[span(core * half + t, WIDE), :],
                ref.at[t : t + WIDE, :],
                sems.at[first + t // WIDE],
            )
            for t in range(0, half, WIDE)
        ]
        for core, ref, first in (
            (1 - me, theirs_slab_ref, 1),
            (me, mine_slab_ref, 1 + half // WIDE),
        )
    )
    for copy in (basis_copy, *theirs_copies):
        copy.start()
    basis_copy.wait()
    for copy in mine_copies:
        copy.start()
    left = basis_ref[...].astype(BF16)
    left_ref[...] = left
    for copy in theirs_copies:
        copy.wait()
    for t in range(0, half, WIDE):
        at = slice(t, t + WIDE)
        theirs_ref[:, at] = dot(theirs_slab_ref[at, :], left, 1, 1).T.astype(BF16)
    for copy in mine_copies:
        copy.wait()


def first_mine_kernel(left_ref, slab_ref, mine_ref):
    left = left_ref[...]
    for t in range(0, mine_ref.shape[1], WIDE):
        mine_ref[:, t : t + WIDE] = dot(slab_ref[t : t + WIDE, :], left, 1, 1).T


def columns_mine_kernel(orthogonal, *refs):
    if orthogonal:
        me_ref, mine_ref, gram_in_ref, slab_ref, acc_ref, gram_ref, factor_ref, rows_ref = refs
        factor3 = stacked(inverse_factor(gram_in_ref[...]), 1)
        factor_ref[...] = factor3
        mine = applied(factor3, mine_ref[...]).astype(BF16)
        rows_ref[...] = mine
    else:
        me_ref, mine_ref, slab_ref, acc_ref, gram_ref = refs
        mine = mine_ref[...]
    gram_ref[...] = dot(mine, mine, 1, 1)
    width = acc_ref.shape[1]
    for t in range(0, width, TILE):
        at = span((1 - me_ref[0]) * width + t, TILE)
        acc_ref[:, t : t + TILE] = dot(mine, slab_ref[:, at], 1, 0)


def put_chunks(out_ref, j, product):
    per = TILE // LANE
    product = product.astype(out_ref.dtype)
    for q in range(per):
        out_ref[j * per + q] = product[:, q * LANE : (q + 1) * LANE]


def columns_theirs_kernel(orthogonal, *refs):
    if orthogonal:
        me_ref, other_ref, acc_ref, slab_ref, factor_ref, theirs_ref, rows_ref = refs
        other = applied(factor_ref[...], other_ref[...]).astype(BF16)
        rows_ref[...] = other
    else:
        me_ref, other_ref, acc_ref, slab_ref, theirs_ref = refs
        other = other_ref[...]
    width = acc_ref.shape[1]
    for j in range(width // TILE):
        at = span((1 - me_ref[0]) * width + j * TILE, TILE)
        product = acc_ref[:, j * TILE : (j + 1) * TILE] + dot(other, slab_ref[:, at], 1, 0)
        put_chunks(theirs_ref, j, product)


def columns_owned_kernel(
    me_ref, mine_ref, other_ref, theirs_slab_ref, mine_slab_ref, gram_mine_ref,
    owned_ref, extra_ref, gram_ref,
):
    mine, other = mine_ref[...], other_ref[...]
    rank = other.shape[0]
    gram_ref[...] = jnp.zeros_like(gram_ref)
    gram_ref[:, :rank] = gram_mine_ref[...] + dot(other, other, 1, 1)
    each = rank // extra_ref.shape[0]
    for c in range(extra_ref.shape[0]):
        extra_ref[c] = extra_rows(gram_ref[c * each : (c + 1) * each, :])
    width = theirs_slab_ref.shape[1] // 2
    for j in range(width // TILE):
        at = span(me_ref[0] * width + j * TILE, TILE)
        product = dot(mine, mine_slab_ref[:, at], 1, 0) + dot(other, theirs_slab_ref[:, at], 1, 0)
        put_chunks(owned_ref, j, product)


def join_chunks_kernel(owned_ref, got_ref, extra_ref, out_ref):
    rank = owned_ref.shape[1]
    for c in range(out_ref.shape[0]):
        out_ref[c, :rank, :] = (owned_ref[c] + got_ref[c].astype(F32)).astype(BF16)
        out_ref[c, rank:, :] = extra_ref[c]


def sum_chunks_kernel(parts_ref, out_ref):
    n = parts_ref.shape[0]
    rank = parts_ref.shape[1] - EXTRA
    total = parts_ref[0].astype(F32)
    for c in range(1, n):
        total = total + parts_ref[c].astype(F32)
    extra = extra_rows(from_extra(total[rank:], rank // n))
    piece = jnp.concatenate([total[:rank].astype(BF16), extra], axis=0)
    for c in range(n):
        out_ref[c] = piece


def add_rows(columns, core, acc_ref, slab_ref, out_ref):
    at = span(core * columns.shape[1], columns.shape[1])
    for t in range(0, out_ref.shape[1], WIDE):
        product = dot(slab_ref[t : t + WIDE, at], columns, 1, 1).T
        if acc_ref is not None:
            product = acc_ref[:, t : t + WIDE] + product
        out_ref[:, t : t + WIDE] = product.astype(out_ref.dtype)


def rows_own_kernel(
    me_ref, own_ref, theirs_slab_ref, mine_slab_ref,
    factor_ref, theirs_ref, mine_ref, gram_ref, columns_ref, half_ref,
):
    rank = gram_ref.shape[0]
    factor3 = stacked(inverse_factor(gathered_gram(own_ref, rank)), 1)
    factor_ref[...] = factor3
    total = jnp.zeros((3 * rank, 3 * rank), F32)
    for at, block in blocks_of(own_ref, rank):
        columns = applied(factor3, block)
        columns_ref[:, at] = columns
        half_ref[:, at] = columns.astype(BF16)
        total = total + gram_of(columns_ref, at)
    gram_ref[...] = folded(total, rank)
    half = half_ref[...]
    add_rows(half, me_ref[0], None, theirs_slab_ref, theirs_ref)
    add_rows(half, me_ref[0], None, mine_slab_ref, mine_ref)


def rows_theirs_kernel(
    me_ref, other_ref, factor_ref, acc_ref, slab_ref, theirs_ref, columns_ref, half_ref
):
    factor3 = factor_ref[...]
    for at, block in blocks_of(other_ref, factor3.shape[0]):
        columns = applied(factor3, block)
        columns_ref[:, at] = columns
        half_ref[:, at] = columns.astype(BF16)
    add_rows(half_ref[...], 1 - me_ref[0], acc_ref, slab_ref, theirs_ref)


def rows_mine_kernel(
    me_ref, half_ref, columns_ref, gram_own_ref, acc_ref, slab_ref, mine_ref, pack_ref
):
    rank, width = columns_ref.shape
    total = jnp.zeros((3 * rank, 3 * rank), F32)
    for t in range(0, width, TILE):
        total = total + gram_of(columns_ref, slice(t, t + TILE))
    gram = gram_own_ref[...] + folded(total, rank)
    pack_ref[...] = packed_gram(gram).astype(BF16)
    add_rows(half_ref[...], 1 - me_ref[0], acc_ref, slab_ref, mine_ref)


def square_places(size):
    return (lax.broadcasted_iota(jnp.int32, (size, size), i) for i in range(2))


def packed_gram(gram):
    size = gram.shape[0] // 2
    row, column = square_places(size)
    low, corner = gram[size:, :size], gram[size:, size:]
    mixed = jnp.where(row >= column, gram[:size, :size], corner)
    diagonal = jnp.sum(jnp.where(row == column, corner, 0.0), axis=1, keepdims=True)
    lanes = lax.broadcasted_iota(jnp.int32, (size, 2 * size), 1)
    tail = jnp.zeros((size, 2 * size), F32)
    for i, part in enumerate(thirds(diagonal)):
        tail = jnp.where(lanes == i, part, tail)
    full = jnp.concatenate([*thirds(jnp.concatenate([low, mixed], axis=1)), tail], axis=1)
    return jnp.concatenate([full[: size // 2], full[size // 2 :]], axis=1)


def unpacked_gram(e, rank):
    size = rank // 2
    row, column = square_places(size)
    full = jnp.concatenate([e[:, : 4 * rank], e[:, 4 * rank :]], axis=0)
    both = full[:, :rank] + full[:, rank : 2 * rank] + full[:, 2 * rank : 3 * rank]
    tail = full[:, 3 * rank :]
    diagonal = tail[:, 0:1] + tail[:, 1:2] + tail[:, 2:3]
    turned = both.T
    low, mixed = both[:, :size], both[:, size:]
    first = jnp.where(row >= column, mixed, turned[size:])
    corner = jnp.where(row < column, mixed, jnp.where(row > column, turned[size:], diagonal))
    return jnp.concatenate(
        [jnp.concatenate([first, turned[:size]], axis=1), jnp.concatenate([low, corner], axis=1)],
        axis=0,
    )


def join_rows_kernel(mine_ref, got_ref, pack_ref, out_ref):
    rank = mine_ref.shape[0]
    out_ref[:rank, :] = (mine_ref[...] + got_ref[...].astype(F32)).astype(BF16)
    out_ref[rank:, :] = pack_ref[...]


def sum_packed_kernel(a_ref, b_ref, c_ref, d_ref, rows_ref, gram_ref):
    total = (a_ref[...].astype(F32) + b_ref[...].astype(F32)) + (
        c_ref[...].astype(F32) + d_ref[...].astype(F32)
    )
    rank = rows_ref.shape[0]
    rows_ref[...] = total[:rank].astype(BF16)
    gram_ref[...] = unpacked_gram(total[rank:], rank)


def final_own_kernel(
    scale, me_ref, own_ref, rows_mine_ref, rows_other_ref,
    factor_ref, columns_ref, gram_ref, left_ref,
):
    me = me_ref[0]
    rank, half = rows_mine_ref.shape
    factor3 = stacked(inverse_factor(gathered_gram(own_ref, rank)), 1)
    factor_ref[...] = factor3
    for core, ref in ((me, rows_mine_ref), (1 - me, rows_other_ref)):
        left = applied(factor3, ref[...]).astype(BF16)
        left_ref[:, span(core * half, half)] = (left.astype(F32) * scale).astype(BF16)
    gram_ref[...] = keep_columns(factor3, own_ref, columns_ref)


def keep_columns(factor3, chunks_ref, columns_ref):
    rank = factor3.shape[0]
    total = jnp.zeros((3 * rank, 3 * rank), F32)
    for at, block in blocks_of(chunks_ref, rank):
        columns = applied(factor3, block)
        columns_ref[:, at] = columns
        three = stacked(columns)
        total = total + dot(three, three, 1, 1)
    return folded(total, rank)


def final_other_kernel(other_ref, factor_ref, gram_own_ref, columns_ref, gram_ref):
    gram_ref[...] = gram_own_ref[...] + keep_columns(factor_ref[...], other_ref, columns_ref)


def update_pieces(pieces, left, first_ref, second_ref, outs, buffers, sems):
    corr_one = 1.0 - 0.9**10
    corr_two = 1.0 - 0.999**10
    update_ref, new_first_ref, new_second_ref = buffers
    copies = []
    put = 0
    for i, (base, columns_ref, start, size) in enumerate(pieces):
        for t in range(0, size, TILE):
            at = span(base + start + t, TILE)
            columns = columns_ref[:, start + t : start + t + TILE]
            new_first = 0.9 * first_ref[:, at] + 0.1 * columns
            new_second = 0.999 * second_ref[:, at] + 0.001 * columns * columns
            here = slice(put + t, put + t + TILE)
            new_first_ref[:, here] = new_first
            new_second_ref[:, here] = new_second
            direction = new_first / corr_one / (jnp.sqrt(new_second / corr_two) + 1e-08)
            update_ref[:, here] = dot(left, direction.astype(BF16), 1, 0).astype(BF16)
        here = slice(put, put + size)
        put += size
        for j, (ref, hbm) in enumerate(zip(buffers, outs)):
            copy = pltpu.make_async_copy(
                ref.at[:, here], hbm.at[:, piece_at(base + start, size)], sems.at[3 * i + j]
            )
            copy.start()
            copies.append(copy)
    return copies


def piece_at(base, size):
    return pl.ds(pl.multiple_of(base, TILE), size)


def cuts(width):
    start = 0
    while start < width:
        size = PIECE if width - start > PIECE else TILE
        yield start, size
        start += size


def update_kernel(me_ref, own_ref, other_ref, left_ref, first_ref, second_ref, *refs):
    outs, buffers, sems = refs[:3], refs[3:6], refs[6]
    me = me_ref[0]
    width = own_ref.shape[1]
    left = left_ref[...].T
    pieces = [(me * width, own_ref, t, PIECE) for t in range(0, width, PIECE)]
    pieces += [((1 - me) * width, other_ref, t, size) for t, size in cuts(width)]
    for copy in update_pieces(pieces, left, first_ref, second_ref, outs, buffers, sems):
        copy.wait()


def basis_kernel(me_ref, own_ref, other_ref, a_ref, b_ref, c_ref, d_ref, basis_hbm, basis_ref, sems):
    me = me_ref[0]
    width = own_ref.shape[1]
    factor = inverse_factor((a_ref[...] + b_ref[...]) + (c_ref[...] + d_ref[...]))
    high, mid, _ = thirds(factor)
    wide = jnp.concatenate([high, high, mid], axis=1).astype(BF16)
    copies = []
    for i, (core, ref) in enumerate(((me, own_ref), (1 - me, other_ref))):
        for t in range(0, width, TILE):
            high, mid, _ = thirds(ref[:, t : t + TILE])
            tall = jnp.concatenate([high, mid, high], axis=0).astype(BF16)
            here = slice(i * width + t, i * width + t + TILE)
            basis_ref[:, here] = dot(wide, tall, 1, 0)
            copy = pltpu.make_async_copy(
                basis_ref.at[:, here],
                basis_hbm.at[:, span(core * width + t, TILE)],
                sems.at[len(copies)],
            )
            copy.start()
            copies.append(copy)
    for copy in copies:
        copy.wait()


def call(kernel, outs, operands, scratch=(), hbm=(), hbm_out=(), aliases=None):
    def spec(i, x):
        if x.dtype == jnp.int32:
            return SMEM
        return pl.BlockSpec(memory_space=pl.ANY) if i in hbm else VMEM

    moved = sum(x.size * x.dtype.itemsize for x in operands)
    return pl.pallas_call(
        kernel,
        out_shape=[jax.ShapeDtypeStruct(s, t) for s, t in outs],
        in_specs=[spec(i, x) for i, x in enumerate(operands)],
        out_specs=[
            pl.BlockSpec(memory_space=pl.ANY) if i in hbm_out else VMEM for i in range(len(outs))
        ],
        input_output_aliases=aliases or {},
        scratch_shapes=[pltpu.VMEM(*s) if isinstance(s, tuple) else s for s in scratch],
        compiler_params=pltpu.CompilerParams(vmem_limit_bytes=VMEM_LIMIT),
        cost_estimate=pl.CostEstimate(flops=64 * moved, bytes_accessed=moved, transcendentals=0),
    )(*operands)


def swapped(x):
    return lax.ppermute(x, "dp", [(0, 1), (1, 0)])


def others(x):
    n = lax.axis_size("mp")
    return [lax.ppermute(x, "mp", [(i, (i + k) % n) for i in range(n)]) for k in (1, 3, 2)]


def columns_of(me, mine, slabs, owners, gram=None):
    theirs_slab, mine_slab = slabs
    rank, half = mine.shape
    width = mine_slab.shape[1]
    orthogonal = gram is not None
    square = ((rank, rank), F32)
    acc = ((rank, width // 2), F32)
    halves = ((rank, half), BF16)
    chunk = (owners, rank, LANE)
    whole = [((owners, rank + EXTRA, LANE), BF16)]

    other = swapped(mine)
    if orthogonal:
        outs = [acc, square, ((rank, 3 * rank), BF16), halves]
        operands = [me, mine, gram, mine_slab]
    else:
        outs = [acc, square]
        operands = [me, mine, mine_slab]
    acc, gram_mine, *rest = call(functools.partial(columns_mine_kernel, orthogonal), outs, operands)
    if orthogonal:
        factor, mine = rest
        theirs, other = call(
            functools.partial(columns_theirs_kernel, True),
            [(chunk, BF16), halves],
            [me, other, acc, theirs_slab, factor],
        )
    else:
        theirs = call(
            functools.partial(columns_theirs_kernel, False),
            [(chunk, BF16)],
            [me, other, acc, theirs_slab],
        )[0]
    got = swapped(theirs)
    owned, extra = call(
        columns_owned_kernel,
        [(chunk, F32), ((owners, EXTRA, LANE), BF16)],
        [me, mine, other, theirs_slab, mine_slab, gram_mine],
        [((rank, LANE), F32)],
    )
    chunks = call(join_chunks_kernel, whole, [owned, got, extra])[0]
    parts = lax.all_to_all(chunks, "vocab", 0, 0)
    copies = call(sum_chunks_kernel, whole, [parts])[0]
    own = lax.all_to_all(copies, "vocab", 0, 0)
    return own, swapped(own), mine, other


def local(grad_parts, old_basis, first_moment, second_moment):
    slab = grad_parts[0]
    vocab, width = slab.shape
    rank = old_basis.shape[0]
    half = vocab // 2
    owners = lax.axis_size("vocab")
    me = lax.axis_index("dp").astype(jnp.int32).reshape(1)
    theirs_out, mine_out = ((rank, half), BF16), ((rank, half), F32)
    wide = ((rank, width), F32)
    narrow = ((rank, width // 2), F32)
    square = ((rank, rank), F32)
    factor_out = ((rank, 3 * rank), BF16)
    half_slab = ((half, width), BF16)

    slab, basis = (pltpu.with_memory_space_constraint(x, pltpu.HBM) for x in (slab, old_basis))
    theirs, left, theirs_slab, mine_slab = call(
        first_theirs_kernel,
        [theirs_out, ((rank, width), BF16), half_slab, half_slab],
        [me, basis, slab],
        [((rank, width), F32), pltpu.SemaphoreType.DMA((1 + vocab // WIDE,))],
        hbm=(1, 2),
    )
    got = swapped(theirs)
    mine = call(first_mine_kernel, [mine_out], [left, mine_slab])[0]
    slabs = (theirs_slab, mine_slab)
    mine = (mine + got.astype(F32)).astype(BF16)
    total = mine.astype(F32)
    for x in others(mine):
        total = total + x.astype(F32)
    own, other, _, _ = columns_of(me, total.astype(BF16), slabs, owners)

    factor, theirs_acc, mine_acc, gram = call(
        rows_own_kernel,
        [factor_out, mine_out, mine_out, square],
        [me, own, theirs_slab, mine_slab],
        [narrow, ((rank, width // 2), BF16)],
    )
    theirs, columns, columns_half = call(
        rows_theirs_kernel,
        [theirs_out, narrow, ((rank, width // 2), BF16)],
        [me, other, factor, theirs_acc, theirs_slab],
    )
    got = swapped(theirs)
    mine, pack = call(
        rows_mine_kernel,
        [mine_out, ((EXTRA, half), BF16)],
        [me, columns_half, columns, gram, mine_acc, mine_slab],
    )
    mine = call(join_rows_kernel, [((rank + EXTRA, half), BF16)], [mine, got, pack])[0]
    mine, gram = call(sum_packed_kernel, [theirs_out, square], [mine, *others(mine)])
    own, other, rows_mine, rows_other = columns_of(me, mine, slabs, owners, gram)

    scale = math.sqrt(vocab * owners)
    assert scale == 2.0 ** round(math.log2(scale))
    factor, columns_own, gram, left = call(
        functools.partial(final_own_kernel, scale),
        [factor_out, narrow, square, ((rank, vocab), BF16)],
        [me, own, rows_mine, rows_other],
    )
    columns_other, gram = call(final_other_kernel, [narrow, square], [other, factor, gram])
    gram_others = others(gram)
    outs = [((vocab, width), BF16), wide, wide]

    def buffers(columns):
        return [((vocab, columns), BF16), ((rank, columns), F32), ((rank, columns), F32)]

    update, new_first, new_second = call(
        update_kernel,
        outs,
        [me, columns_own, columns_other, left, first_moment, second_moment],
        buffers(width) + [pltpu.SemaphoreType.DMA((3 * (width // TILE),))],
        hbm_out=(0, 1, 2),
    )
    basis = call(
        basis_kernel,
        [wide],
        [me, columns_own, columns_other, gram, *gram_others],
        [wide, pltpu.SemaphoreType.DMA((width // TILE,))],
        hbm_out=(0,),
    )[0]
    return (update, basis, new_first, new_second)


def solution(mesh):
    placed = (P("dp", "vocab", "mp"), P(None, "mp"), P(None, "mp"), P(None, "mp"))
    return jax.shard_map(
        local,
        mesh=mesh,
        in_specs=placed,
        out_specs=(P("vocab", "mp"), P(None, "mp"), P(None, "mp"), P(None, "mp")),
        check_vma=False,
    )
```
